256 devices in a mesh: dp: 16 (over y, x), clus: 8 (over z), tensor: 2 (over core).
Axes of the slice: x: 4, y: 4, z: 8, core: 2. Of those that a mesh axis runs over, the one named last changes fastest.
Arguments:
- hidden: bfloat16 [1536, 257, 1024], P(('dp', 'clus'), None, 'tensor'), may hold values from -6 to 6
- token_lengths: int32 [1536], P(('dp', 'clus')), may hold values from 129 to 257, as said below
- image_counts: int32 [128], P(('dp', 'clus')), may hold values from 11 to 12, as said below
- cluster_ids: int32 [1536], P(('dp', 'clus', 'tensor')), may hold values from 0 to 63, as said below
- order_ranks: int32 [1536], P(('dp', 'clus', 'tensor')), may hold values from 0 to 1535, each once
- ln_gains: float32 [3, 1024], replicated, may hold values from 0.5 to 1.5
- ln_biases: float32 [3, 1024], replicated, may hold values from -3 to 3
- w_qkv: bfloat16 [1024, 3, 1024], P(None, None, 'tensor'), may hold values from -8 to 8
- layer_biases: float32 [4, 1024], replicated, may hold values from -3 to 3
- w_out: bfloat16 [1024, 1024], P('tensor'), may hold values from -0.1875 to 0.1875
- w_fc1: bfloat16 [1024, 4096], P(None, ('clus', 'tensor')), may hold values from -0.1875 to 0.1875
- fc1_bias: float32 [4096], P(('clus', 'tensor')), may hold values from -3 to 3
- w_fc2: bfloat16 [4096, 1024], P(('clus', 'tensor')), may hold values from -0.09375 to 0.09375
- w_proj: bfloat16 [1024, 768], P(('clus', 'tensor')), may hold values from -0.1875 to 0.1875
Outputs:
- features: bfloat16 [1536, 768], P(('dp', 'clus', 'tensor'))
- nearest_similarity: float32 [1536], P(('dp', 'clus', 'tensor'))
The draws below stay inside these ranges and needn't reach their ends.
Inputs may be any that keep to these rules, and one draw needn't show every extreme that they name: `token_lengths`: each length is 1 + (256) m // 16 for a whole m from 8 to 16; some image has length 257. `image_counts`: the live images of a batch of 12 are its first ones; some batch is full and some lacks one. `cluster_ids`: the owner of cluster c is c // 4. In each aligned block of 96 images, at most 7 belong to clusters of one owner, and some owner gets exactly 7.
All inputs are finite; a program needn't handle non-finite values.
Results may differ from the reference program's by a relative error of at most 0.018.
Values may be sent and summed in bfloat16 or wider, within the bound.
No kernel may reach another device: no remote copies, remote signals or barrier semaphores. Data moves between devices by JAX's collectives and lax.ppermute only.
A program may use at most 128 MiB of HBM per device.

```python
import jax
import jax.numpy as jnp
from jax import lax

D = 1024
FF = 4096
E = 768
HEAD = 64
TOK = 257
IMG_DEV = 12
CLUS_DP = 4
GROUPS = 128
IMAGES = 1536
ROWS_DP = 96
MOST = 7
CLUSTERS = 64


def cluster_table(key):
    key_hot, key_pick, key_within, key_shuffle = jax.random.split(key, 4)
    blocks = IMAGES // ROWS_DP
    owners = CLUSTERS // CLUS_DP
    hot_owner = jax.random.randint(key_hot, (), 0, owners)
    tickets = (owners - 1) * MOST
    chosen = jax.vmap(lambda subkey: jax.random.permutation(subkey, tickets)[:ROWS_DP - MOST])(jax.random.split(key_pick, blocks))
    others = chosen // MOST
    others = others + (others >= hot_owner).astype(jnp.int32)
    hot_rows = jnp.zeros((blocks, MOST), jnp.int32) + hot_owner
    owner_rows = jnp.concatenate([hot_rows, others.astype(jnp.int32)], axis=1)
    within = jax.random.randint(key_within, (blocks, ROWS_DP), 0, CLUS_DP)
    cluster_of = owner_rows * CLUS_DP + within
    shuffle = jax.vmap(lambda subkey: jax.random.permutation(subkey, ROWS_DP))(jax.random.split(key_shuffle, blocks))
    cluster_of = jnp.take_along_axis(cluster_of, shuffle, axis=1)
    return cluster_of.reshape(IMAGES).astype(jnp.int32)


def draw_cluster_ids(key, part):
    return cluster_table(key)


def draw_hidden(key, part):
    cluster_of = cluster_table(key)
    key = jax.random.fold_in(key, 7)
    key_noise, key_proto, key_mix = jax.random.split(key, 3)
    noise = jax.random.normal(key_noise, (IMAGES, TOK, D), jnp.float32)
    protos = jax.random.normal(key_proto, (CLUSTERS, D), jnp.float32)
    mix_weight = jax.random.uniform(key_mix, (IMAGES, 1), jnp.float32, 0.4, 1.2)
    head_row = 0.6 * noise[:, 0] + mix_weight * protos[cluster_of]
    drawn = jnp.concatenate([head_row[:, None], noise[:, 1:]], axis=1)
    return jnp.clip(drawn, -6.0, 6.0).astype(jnp.bfloat16)


def draw_w_qkv(key, part):
    key = jax.random.fold_in(key, 5)
    key_base = jax.random.fold_in(key, 0)
    base = jax.random.normal(key_base, (D, 3, D), jnp.float32) * D ** (-0.5)
    return jnp.clip(base, -8.0, 8.0).astype(jnp.bfloat16)


def draw_token_lengths(key, part):
    key = jax.random.fold_in(key, 9)
    key_steps, key_long = jax.random.split(key, 2)
    steps_drawn = jax.random.randint(key_steps, (IMAGES,), 8, 17)
    lengths = 1 + (TOK - 1) * steps_drawn // 16
    longest = jax.random.randint(key_long, (), 0, IMAGES)
    return jnp.where(jnp.arange(IMAGES) == longest, TOK, lengths).astype(jnp.int32)


def draw_image_counts(key, part):
    key = jax.random.fold_in(key, 3)
    key_count, key_full, key_short = jax.random.split(key, 3)
    missing = (jax.random.randint(key_count, (GROUPS,), 0, 16) == 0).astype(jnp.int32)
    counts = IMG_DEV - missing
    full_group = jax.random.randint(key_full, (), 0, GROUPS)
    short_group = (full_group + 1 + jax.random.randint(key_short, (), 0, GROUPS - 1)) % GROUPS
    position = jnp.arange(GROUPS)
    counts = jnp.where(position == full_group, IMG_DEV, counts)
    counts = jnp.where(position == short_group, IMG_DEV - 1, counts)
    return counts.astype(jnp.int32)


def level_of(key, extent, cuts, least, high):
    factor_of, own = 1.0, jax.random.fold_in(key, 6)
    for dim, shards_of in cuts:
        draws = jnp.exp(jax.random.uniform(jax.random.fold_in(own, dim), (shards_of,), jnp.float32, least / len(cuts), high / len(cuts)))
        factor_of = factor_of * jnp.repeat(draws, extent[dim] // shards_of).reshape([-1 if axis == dim else 1 for axis in range(len(extent))])
    return factor_of


def centred(stream_key, dims, deviation, most, shards=(), dtype=jnp.bfloat16):
    values = jax.random.normal(stream_key, dims, jnp.float32) * deviation
    if len(shards) > 0:
        values = level_of(stream_key, dims, shards, -0.22, 0.18) * values
    return jnp.clip(values, min=-most, max=most).astype(dtype)


def setup_inputs(seed: int = 0) -> dict:
    splits = jax.random.split(jax.random.key(seed), 15)
    hidden = draw_hidden(jax.random.fold_in(splits[14], 71), 0)
    token_lengths = draw_token_lengths(jax.random.fold_in(splits[14], 71), 0)
    image_counts = draw_image_counts(jax.random.fold_in(splits[14], 71), 0)
    cluster_ids = draw_cluster_ids(jax.random.fold_in(splits[14], 71), 0)
    order_ranks = jax.random.permutation(splits[4], IMAGES).astype(jnp.int32)
    ln_gains = jnp.clip(1.0 + 0.1 * jax.random.normal(splits[5], (3, D), jnp.float32), 0.5, 1.5)
    ln_biases = centred(splits[6], (3, D), 0.3, 3.0, (), jnp.float32)
    w_qkv = draw_w_qkv(jax.random.fold_in(splits[14], 71), 0)
    layer_biases = centred(splits[8], (4, D), 0.5, 3.0, (), jnp.float32)
    w_out = centred(splits[9], (D, D), D ** -0.5, 0.1875, ((0, 2),))
    w_fc1 = centred(splits[10], (D, FF), D ** -0.5, 0.1875, ((1, 16),))
    fc1_bias = centred(splits[11], (FF,), 0.5, 3.0, ((0, 16),), jnp.float32)
    w_fc2 = centred(splits[12], (FF, D), FF ** -0.5, 0.09375, ((0, 16),))
    w_proj = centred(splits[13], (D, E), D ** -0.5, 0.1875, ((0, 16),))
    return dict(hidden=hidden, token_lengths=token_lengths, image_counts=image_counts, cluster_ids=cluster_ids, order_ranks=order_ranks, ln_gains=ln_gains, ln_biases=ln_biases, w_qkv=w_qkv, layer_biases=layer_biases, w_out=w_out, w_fc1=w_fc1, fc1_bias=fc1_bias, w_fc2=w_fc2, w_proj=w_proj)


norm_eps = 1e-05

def layer_norm(values, gain_row, shift_row):
    average = lax.optimization_barrier(jnp.mean(values, axis=-1, keepdims=True))
    centered = values - average
    spread = lax.optimization_barrier(jnp.mean(centered * centered, axis=-1, keepdims=True))
    return centered * lax.rsqrt(spread + norm_eps) * gain_row + shift_row

def quick_gelu(values):
    return values * jax.nn.sigmoid(1.702 * values)

def reference(hidden, token_lengths, image_counts, cluster_ids, order_ranks, ln_gains, ln_biases, w_qkv, layer_biases, w_out, w_fc1, fc1_bias, w_fc2, w_proj):
    heads = D // HEAD
    scale = HEAD ** (-0.5)
    key_value_weight = w_qkv[:, 1:, :].astype(jnp.float32)

    def encode_group(group_inputs):
        states, lengths = group_inputs
        count = states.shape[0]
        normed = layer_norm(states.astype(jnp.float32), ln_gains[0], ln_biases[0]).astype(jnp.bfloat16)
        query = ((jnp.dot(normed[:, 0], w_qkv[:, 0, :], preferred_element_type=jnp.float32) + layer_biases[0]) * scale).astype(jnp.bfloat16)
        key_value = jnp.einsum('itd,dke->itke', normed.astype(jnp.float32), key_value_weight)
        keys = key_value[:, :, 0].astype(jnp.bfloat16).reshape(count, TOK, heads, HEAD)
        values = (key_value[:, :, 1] + layer_biases[1]).astype(jnp.bfloat16).reshape(count, TOK, heads, HEAD)
        scores = jnp.einsum('ihe,ithe->iht', query.reshape(count, heads, HEAD).astype(jnp.float32), keys.astype(jnp.float32))
        allowed = jnp.arange(TOK)[None, None, :] < lengths[:, None, None]
        scores = jnp.where(allowed, scores, -1e+30)
        highest = lax.optimization_barrier(jnp.max(scores, axis=-1, keepdims=True))
        exponent = jnp.exp(scores - highest)
        weights = (exponent / lax.optimization_barrier(jnp.sum(exponent, axis=-1, keepdims=True))).astype(jnp.bfloat16)
        context = jnp.einsum('iht,ithe->ihe', weights.astype(jnp.float32), values.astype(jnp.float32)).astype(jnp.bfloat16).reshape(count, D)
        attended = jnp.dot(context, w_out, preferred_element_type=jnp.float32)
        first = states[:, 0].astype(jnp.float32) + attended + layer_biases[2]
        mixed = layer_norm(first, ln_gains[1], ln_biases[1]).astype(jnp.bfloat16)
        inner = quick_gelu(jnp.dot(mixed, w_fc1, preferred_element_type=jnp.float32) + fc1_bias).astype(jnp.bfloat16)
        second = first + jnp.dot(inner, w_fc2, preferred_element_type=jnp.float32) + layer_biases[3]
        pooled = layer_norm(second, ln_gains[2], ln_biases[2]).astype(jnp.bfloat16)
        return jnp.dot(pooled, w_proj, preferred_element_type=jnp.float32).astype(jnp.bfloat16)
    grouped = hidden.reshape(GROUPS, IMG_DEV, TOK, D)
    lengths_grouped = token_lengths.reshape(GROUPS, IMG_DEV)
    features = lax.map(encode_group, (grouped, lengths_grouped)).reshape(IMAGES, E)
    as_float = features.astype(jnp.float32)
    unit = (as_float * lax.rsqrt(lax.optimization_barrier(jnp.sum(as_float * as_float, axis=-1, keepdims=True)) + 1e-06)).astype(jnp.bfloat16)
    index = jnp.arange(IMAGES)
    alive = index % IMG_DEV < jnp.repeat(image_counts, IMG_DEV)
    similar = jnp.dot(unit, unit.T, preferred_element_type=jnp.float32)
    allowed = alive[:, None] & alive[None, :] & (cluster_ids[:, None] == cluster_ids[None, :]) & (order_ranks[None, :] < order_ranks[:, None])
    best_value = lax.optimization_barrier(jnp.max(jnp.where(allowed, similar, -2.0), axis=1))
    nearest_similarity = jnp.maximum(best_value, -1.0)
    return (features, nearest_similarity)
```

```python
import jax
import jax.numpy as jnp
from jax import lax
from jax.experimental import pallas as pl
from jax.experimental.pallas import tpu as pltpu
from jax.sharding import PartitionSpec as P

HEAD = 64
CLUS_DP = 4
SLOT = 8
PAD = 16
INTS = 128
EPS = 1e-05
F32 = jnp.float32
BF16 = jnp.bfloat16
MEMBERS = ("clus", "tensor")


def iota(shape, axis):
    return lax.broadcasted_iota(jnp.int32, shape, axis)


def layer_norm(values, gain_row, shift_row):
    average = jnp.mean(values, axis=-1, keepdims=True)
    centered = values - average
    spread = jnp.mean(centered * centered, axis=-1, keepdims=True)
    return centered * lax.rsqrt(spread + EPS) * gain_row + shift_row


def as_column(row):
    size = row.shape[1]
    eye = iota((size, size), 0) == iota((size, size), 1)
    return jnp.sum(jnp.where(eye, row, 0.0), axis=1, keepdims=True)


def nt_dot(left, right):
    return lax.dot_general(left, right, (((1,), (1,)), ((), ())), preferred_element_type=F32)


def tn_dot(left, right):
    return lax.dot_general(left, right, (((0,), (0,)), ((), ())), preferred_element_type=F32)


def query_kernel(cls_ref, gains_ref, shifts_ref, w_ref, biases_ref, probe_ref, sums_ref, const_ref):
    images, half = cls_ref.shape[1:]
    tensor = lax.axis_index("tensor")
    rows = jnp.concatenate([cls_ref[0], cls_ref[1]], axis=1).astype(F32)
    normed = layer_norm(rows, gains_ref[0:1, :], shifts_ref[0:1, :]).astype(BF16)
    start = pl.multiple_of(tensor * half, half)
    query = jnp.dot(normed, w_ref[0], preferred_element_type=F32)
    query = (query + biases_ref[0:1, pl.ds(start, half)]) * HEAD ** (-0.5)
    query = query.astype(BF16).astype(F32)
    mask = iota((PAD, half), 0) == iota((PAD, half), 1) // HEAD
    spread = jnp.where(mask[None], query[:, None, :], 0.0).reshape(images * PAD, half).astype(BF16)
    probe = nt_dot(spread, w_ref[1])
    const = jnp.sum(probe * shifts_ref[0:1, :], axis=1, keepdims=True)
    probe = (probe * gains_ref[0:1, :]).astype(BF16)
    probe_ref[...] = probe
    sums = jnp.sum(probe.astype(F32), axis=1, keepdims=True)
    pick = (iota((images * PAD, PAD), 0) % PAD) == iota((images * PAD, PAD), 1)
    sums_ref[...] = jnp.sum(jnp.where(pick, sums, 0.0).reshape(images, PAD, PAD), axis=1)
    const_ref[...] = jnp.sum(jnp.where(pick, const, 0.0).reshape(images, PAD, PAD), axis=1)


def attend_kernel(
    own_ref,
    other_ref,
    lengths_ref,
    counts_ref,
    clusters_ref,
    ranks_ref,
    probe_ref,
    sums_ref,
    const_ref,
    cls_ref,
    gains_ref,
    shifts_ref,
    biases_ref,
    w_ref,
    w_out_ref,
    out_ref,
    mixed_ref,
):
    step = pl.program_id(0)
    block, tokens, half = own_ref.shape
    width = 2 * half
    tensor = lax.axis_index("tensor")
    sides = (
        (own_ref, pl.multiple_of(tensor * half, half)),
        (other_ref, pl.multiple_of((1 - tensor) * half, half)),
    )
    for j in range(block):
        image = step * block + j
        start = pl.multiple_of(image * PAD, PAD)
        total = sum(jnp.sum(ref[j].astype(F32), axis=1, keepdims=True) for ref, _ in sides)
        mean = total * (1.0 / width)
        spread = 0.0
        scores = 0.0
        for ref, lane in sides:
            centered = ref[j].astype(F32) - mean
            spread += jnp.sum(centered * centered, axis=1, keepdims=True)
            scores += nt_dot(ref[j], probe_ref[pl.ds(start, PAD), pl.ds(lane, half)])
        scale = lax.rsqrt(spread * (1.0 / width) + EPS)
        scores = (scores - mean * sums_ref[pl.ds(image, 1), :]) * scale
        scores += const_ref[pl.ds(image, 1), :]
        inside = iota((tokens, PAD), 0) < lengths_ref[image]
        scores = jnp.where(inside, scores, -1e30)
        exponent = jnp.exp(scores - jnp.max(scores, axis=0, keepdims=True))
        weights = exponent / jnp.sum(exponent, axis=0, keepdims=True)
        part = (weights * scale).astype(BF16)
        offset = as_column(jnp.sum(part.astype(F32) * mean, axis=0, keepdims=True))
        for ref, lane in sides:
            summed = tn_dot(part, ref[j]) - offset
            summed = summed * gains_ref[0:1, pl.ds(lane, half)] + shifts_ref[0:1, pl.ds(lane, half)]
            mixed_ref[pl.ds(start, PAD), pl.ds(lane, half)] = summed.astype(BF16)

    @pl.when(step == pl.num_programs(0) - 1)
    def _():
        images = mixed_ref.shape[0] // PAD
        clus = lax.axis_index("clus")
        own_start = pl.multiple_of(tensor * half, half)
        context = jnp.dot(mixed_ref[...], w_ref[0], preferred_element_type=F32)
        mask = (iota((images * PAD, half), 0) % PAD) == iota((images * PAD, half), 1) // HEAD
        context = jnp.sum(jnp.where(mask, context, 0.0).reshape(images, PAD, half), axis=1)
        context = context + biases_ref[1:2, pl.ds(own_start, half)]
        fill = jnp.zeros((PAD - images, half), F32)
        context = jnp.concatenate([context, fill], axis=0).astype(BF16)
        out = jnp.dot(context, w_out_ref[...], preferred_element_type=F32)
        residual = jnp.concatenate([cls_ref[0], cls_ref[1]], axis=1).astype(F32)
        residual = jnp.where(tensor == 0, residual, 0.0)
        residual = jnp.concatenate([residual, jnp.zeros((PAD - images, width), F32)], axis=0)
        row, lane = iota((PAD, width), 0), iota((PAD, width), 1)
        own_images = images // 2
        for j in range(own_images):
            place = tensor * own_images + j
            hit = (lane // (2 * PAD) == clus) & (lane % PAD == place)
            cluster, rank = clusters_ref[j], ranks_ref[j]
            alive = (place < counts_ref[0]).astype(jnp.int32)
            for k, value in enumerate((cluster, rank // 64, rank % 64, alive)):
                residual = jnp.where(hit & (row == images + k), value.astype(F32), residual)
        out_ref[...] = (out + residual).astype(BF16)


def mlp_kernel(
    rows_ref, gains_ref, shifts_ref, biases_ref, w1_ref, b1_ref, w2_ref, out_ref, first_ref, meta_ref
):
    total, width = rows_ref.shape
    images = PAD - 4
    members = total // PAD
    member = lax.axis_index("clus") * 2 + lax.axis_index("tensor")
    rows = rows_ref[...]
    ints = jnp.sum(rows[:, :total].astype(F32).reshape(members, PAD, total), axis=0)
    cluster, rank_high, rank_low, alive = (ints[images + k : images + k + 1] for k in range(4))
    owner = jnp.floor(cluster * (1.0 / CLUS_DP))
    lane = iota((1, total), 1)
    valid = lane % PAD < images
    place = lane - (lane & PAD)
    before = iota((total, total), 0)
    earlier = (
        (as_column(owner) == owner) & (before % (2 * PAD) < images) & (before < place)
    )
    slot = jnp.sum(jnp.where(earlier, 1.0, 0.0), axis=0, keepdims=True)
    target = jnp.where(valid, owner * SLOT + slot, -1.0)
    slots = members * SLOT
    chosen = jnp.where(iota((slots, total), 0).astype(F32) == target, 1.0, 0.0).astype(BF16)
    first = jnp.dot(chosen, rows, preferred_element_type=F32) + biases_ref[2:3, :]
    mixed = layer_norm(first, gains_ref[1:2, :], shifts_ref[1:2, :]).astype(BF16)
    inner = jnp.dot(mixed, w1_ref[...], preferred_element_type=F32) + b1_ref[...]
    inner = (inner * jax.nn.sigmoid(1.702 * inner)).astype(BF16)
    out_ref[...] = jnp.dot(inner, w2_ref[...], preferred_element_type=F32).astype(BF16)
    mine = (iota((PAD, total), 0) + member * SLOT).astype(F32) == target
    mine = mine & (iota((PAD, total), 0) < SLOT)
    picked = jnp.dot(
        jnp.where(mine, 1.0, 0.0).astype(BF16), rows, preferred_element_type=F32
    )
    first_ref[...] = picked[:SLOT] + biases_ref[2:3, :]
    single = (mine & (lane % (2 * PAD) < PAD))[:SLOT]
    home = ((lane // (2 * PAD)) * images + lane % PAD + 1).astype(F32)
    meta = jnp.zeros((SLOT, INTS), F32)
    for k, value in enumerate((cluster, rank_high, rank_low, alive, home)):
        column = jnp.sum(jnp.where(single, value, 0.0), axis=1, keepdims=True)
        meta = jnp.where(iota((SLOT, INTS), 1) == k, column, meta)
    meta_ref[...] = meta


def embed_kernel(
    parts_ref, first_ref, meta_ref, gains_ref, shifts_ref, biases_ref, w_ref, send_ref, feat_ref
):
    second = jnp.sum(parts_ref[...].astype(F32), axis=0) + first_ref[...] + biases_ref[3:4, :]
    pooled = layer_norm(second, gains_ref[2:3, :], shifts_ref[2:3, :]).astype(BF16)
    features = jnp.dot(pooled, w_ref[...], preferred_element_type=F32).astype(BF16)
    feat_ref[...] = features
    as_float = features.astype(F32)
    unit = as_float * lax.rsqrt(jnp.sum(as_float * as_float, axis=-1, keepdims=True) + 1e-06)
    row = jnp.concatenate([unit, meta_ref[...]], axis=1).astype(BF16)
    send_ref[...] = jnp.broadcast_to(row[None], send_ref.shape)


def nearest_kernel(keys_ref, own_ref, feat_ref, meta_ref, out_ref):
    width = feat_ref.shape[1]
    keys = keys_ref[...]
    similar = nt_dot(own_ref[0][:, :width], keys[:, :width])
    select = (iota((SLOT, INTS), 0) == iota((SLOT, INTS), 1)).astype(F32).astype(BF16)
    key_ints = nt_dot(select, keys[:, width:])
    lane = iota((SLOT, INTS), 1)
    cluster, rank_high, rank_low, alive, home = (
        jnp.sum(jnp.where(lane == k, meta_ref[...], 0.0), axis=1, keepdims=True) for k in range(5)
    )
    key_rank = key_ints[1:2] * 64.0 + key_ints[2:3]
    allowed = (
        (key_ints[3:4] > 0.5)
        & (key_ints[0:1] == cluster)
        & (key_rank < rank_high * 64.0 + rank_low)
    )
    best = jnp.max(jnp.where(allowed, similar, -2.0), axis=1, keepdims=True)
    best = jnp.where(alive > 0.5, jnp.maximum(best, -1.0), -1.0)
    high = best.astype(BF16).astype(F32)
    middle = (best - high).astype(BF16).astype(F32)
    low = best - high - middle
    tail = jnp.where(lane == 0, high, jnp.where(lane == 1, middle, jnp.where(lane == 2, low, 0.0)))
    data = jnp.concatenate([feat_ref[...].astype(F32), tail], axis=1)
    data = jnp.concatenate([data, jnp.zeros_like(data)], axis=0).astype(BF16)
    slots = out_ref.shape[0]
    code = iota((SLOT, slots), 1)
    own_images = (PAD - 4) // 2
    wanted = jnp.where(code % SLOT < own_images, code // SLOT * own_images + code % SLOT + 1, -1)
    hit = jnp.where(wanted.astype(F32) == home, 1.0, 0.0)
    hit = jnp.concatenate([hit, jnp.zeros_like(hit)], axis=0).astype(BF16)
    out_ref[...] = tn_dot(hit, data).astype(BF16)


def struct(shape, dtype):
    return jax.ShapeDtypeStruct(shape, dtype)


def whole(memory=pltpu.VMEM):
    return pl.BlockSpec(memory_space=memory)


def local(
    hidden,
    token_lengths,
    image_counts,
    cluster_ids,
    order_ranks,
    ln_gains,
    ln_biases,
    w_qkv,
    layer_biases,
    w_out,
    w_fc1,
    fc1_bias,
    w_fc2,
    w_proj,
):
    images, tokens, half = hidden.shape
    width = 2 * half
    embed = w_proj.shape[1]
    members = lax.axis_size("clus") * 2
    owners = lax.axis_size("dp")
    own_images = images // 2
    params = pltpu.CompilerParams(vmem_limit_bytes=48 * 1024 * 1024)
    other = lax.ppermute(hidden, "tensor", [(0, 1), (1, 0)])
    cls = lax.all_gather(hidden[:, 0, :], "tensor", axis=0, tiled=False)
    proj = lax.all_gather(w_proj, MEMBERS, axis=0, tiled=True)
    w_three = jnp.transpose(w_qkv, (1, 0, 2))
    probe, sums, const = pl.pallas_call(
        query_kernel,
        grid=(1,),
        out_shape=(
            struct((images * PAD, width), BF16),
            struct((images, PAD), F32),
            struct((images, PAD), F32),
        ),
        in_specs=[whole(), whole(), whole(), pl.BlockSpec((2, width, half), lambda i: (0, 0, 0)), whole()],
        out_specs=[whole()] * 3,
        compiler_params=params,
    )(cls, ln_gains, ln_biases, w_three, layer_biases)
    block = 3
    partial = pl.pallas_call(
        attend_kernel,
        grid=(images // block,),
        out_shape=struct((PAD, width), BF16),
        in_specs=[
            pl.BlockSpec((block, tokens, half), lambda i: (i, 0, 0)),
            pl.BlockSpec((block, tokens, half), lambda i: (i, 0, 0)),
            whole(pltpu.SMEM),
            whole(pltpu.SMEM),
            whole(pltpu.SMEM),
            whole(pltpu.SMEM),
            whole(),
            whole(),
            whole(),
            whole(),
            whole(),
            whole(),
            whole(),
            pl.BlockSpec((1, width, half), lambda i: (2, 0, 0)),
            whole(),
        ],
        out_specs=whole(),
        scratch_shapes=[pltpu.VMEM((images * PAD, width), BF16)],
        compiler_params=params,
    )(
        hidden,
        other,
        token_lengths,
        image_counts,
        cluster_ids,
        order_ranks,
        probe,
        sums,
        const,
        cls,
        ln_gains,
        ln_biases,
        layer_biases,
        w_three,
        w_out,
    )
    rows = lax.all_gather(partial, MEMBERS, axis=0, tiled=True)
    sent, first, meta = pl.pallas_call(
        mlp_kernel,
        out_shape=(
            struct((members * SLOT, width), BF16),
            struct((SLOT, width), F32),
            struct((SLOT, INTS), F32),
        ),
        compiler_params=params,
    )(rows, ln_gains, ln_biases, layer_biases, w_fc1, fc1_bias.reshape(1, -1), w_fc2)
    parts = lax.all_to_all(
        sent.reshape(members, SLOT, width), MEMBERS, split_axis=0, concat_axis=0, tiled=True
    )
    send, features = pl.pallas_call(
        embed_kernel,
        out_shape=(struct((owners, SLOT, embed + INTS), BF16), struct((SLOT, embed), BF16)),
        compiler_params=params,
    )(parts, first, meta, ln_gains, ln_biases, layer_biases, proj)
    keys = lax.all_to_all(send, "dp", split_axis=0, concat_axis=0, tiled=True)
    back = pl.pallas_call(
        nearest_kernel,
        out_shape=struct((members * SLOT, embed + INTS), BF16),
        compiler_params=params,
    )(keys.reshape(owners * SLOT, embed + INTS), send, features, meta)
    home = lax.all_to_all(
        back.reshape(members, SLOT, embed + INTS), MEMBERS, split_axis=0, concat_axis=0, tiled=True
    )
    home = jnp.sum(home[:, :own_images].astype(F32), axis=0)
    nearest = home[:, embed] + home[:, embed + 1] + home[:, embed + 2]
    return (home[:, :embed].astype(BF16), nearest)


def solution(mesh):
    return jax.shard_map(
        local,
        mesh=mesh,
        in_specs=(
            P(("dp", "clus"), None, "tensor"),
            P(("dp", "clus")),
            P(("dp", "clus")),
            P(("dp", "clus", "tensor")),
            P(("dp", "clus", "tensor")),
            P(),
            P(),
            P(None, None, "tensor"),
            P(),
            P("tensor", None),
            P(None, ("clus", "tensor")),
            P(("clus", "tensor")),
            P(("clus", "tensor"), None),
            P(("clus", "tensor"), None),
        ),
        out_specs=(P(("dp", "clus", "tensor"), None), P(("dp", "clus", "tensor"))),
        check_vma=False,
    )
```

```python
import jax
import jax.numpy as jnp
from jax import lax
from jax.experimental import pallas as pl
from jax.experimental.pallas import tpu as pltpu
from jax.sharding import PartitionSpec as P

HEAD = 64
CLUS_DP = 4
SLOT = 8
PAD = 16
INTS = 128
STAT = 128
TABLE = 384
CLS = 272
EPS = 1e-05
F32 = jnp.float32
BF16 = jnp.bfloat16
MEMBERS = ("clus", "tensor")


def iota(shape, axis):
    return lax.broadcasted_iota(jnp.int32, shape, axis)


def layer_norm(values, gain_row, shift_row):
    average = jnp.mean(values, axis=-1, keepdims=True)
    centered = values - average
    spread = jnp.mean(centered * centered, axis=-1, keepdims=True)
    return centered * lax.rsqrt(spread + EPS) * gain_row + shift_row


def as_column(row):
    size = row.shape[1]
    eye = iota((size, size), 0) == iota((size, size), 1)
    return jnp.sum(jnp.where(eye, row, 0.0), axis=1, keepdims=True)


def nt_dot(left, right):
    return lax.dot_general(left, right, (((1,), (1,)), ((), ())), preferred_element_type=F32)


def tn_dot(left, right):
    return lax.dot_general(left, right, (((0,), (0,)), ((), ())), preferred_element_type=F32)


def stats_kernel(own_ref, out_ref):
    images, tokens, half = own_ref.shape
    lane = iota((tokens, STAT), 1)
    table = jnp.zeros((tokens, STAT), F32)
    for i in range(images):
        states = own_ref[i].astype(F32)
        total = jnp.sum(states, axis=1, keepdims=True)
        centered = states - total * (1.0 / half)
        spread = jnp.sum(centered * centered, axis=1, keepdims=True)
        table = jnp.where(lane == i, total, table)
        table = jnp.where(lane == PAD + i, spread, table)
    out_ref[:tokens, :] = table
    first = own_ref[:, 0, :].astype(F32)
    for k in range(half // STAT):
        out_ref[CLS + k * PAD : CLS + k * PAD + images, :] = first[:, k * STAT : (k + 1) * STAT]


def query_kernel(
    stats_ref,
    gains_ref,
    shifts_ref,
    w_ref,
    biases_ref,
    probe_ref,
    sums_ref,
    const_ref,
    mean_ref,
    scale_ref,
    first_ref,
):
    images, width = first_ref.shape[0] - 4, first_ref.shape[1]
    half = width // 2
    tensor = lax.axis_index("tensor")
    first = jnp.concatenate(
        [
            stats_ref[side, CLS + k * PAD : CLS + k * PAD + images, :]
            for side in range(2)
            for k in range(half // STAT)
        ],
        axis=1,
    )
    first_ref[:images, :] = first
    first_ref[images:, :] = jnp.zeros((PAD - images, width), F32)
    normed = layer_norm(first, gains_ref[0:1, :], shifts_ref[0:1, :]).astype(BF16)
    start = pl.multiple_of(tensor * half, half)
    query = jnp.dot(normed, w_ref[0], preferred_element_type=F32)
    query = (query + biases_ref[0:1, pl.ds(start, half)]) * HEAD ** (-0.5)
    query = query.astype(BF16).astype(F32)
    mask = iota((PAD, half), 0) == iota((PAD, half), 1) // HEAD
    spread = jnp.where(mask[None], query[:, None, :], 0.0).reshape(images * PAD, half).astype(BF16)
    probe = nt_dot(spread, w_ref[1])
    const = jnp.sum(probe * shifts_ref[0:1, :], axis=1, keepdims=True)
    probe = (probe * gains_ref[0:1, :]).astype(BF16)
    probe_ref[tensor] = probe[:, :half]
    probe_ref[1 - tensor] = probe[:, half:]
    sums = jnp.sum(probe.astype(F32), axis=1, keepdims=True)
    sums_ref[...] = jnp.broadcast_to(sums, sums_ref.shape)
    const_ref[...] = jnp.broadcast_to(const, const_ref.shape)
    left, right = jnp.transpose(stats_ref[0]), jnp.transpose(stats_ref[1])
    mean_ref[...] = (left[:PAD] + right[:PAD]) * (1.0 / width)
    apart = (left[:PAD] - right[:PAD]) * (1.0 / half)
    spread = left[PAD : 2 * PAD] + right[PAD : 2 * PAD] + apart * apart * (half / 2)
    scale_ref[...] = lax.rsqrt(spread * (1.0 / width) + EPS)


def attend_kernel(
    own_ref,
    other_ref,
    lengths_ref,
    counts_ref,
    clusters_ref,
    ranks_ref,
    probe_ref,
    sums_ref,
    const_ref,
    mean_ref,
    scale_ref,
    first_ref,
    gains_ref,
    shifts_ref,
    biases_ref,
    w_ref,
    w_out_ref,
    w_proj_ref,
    out_ref,
    mixed_ref,
):
    images, tokens, half = own_ref.shape
    width = 2 * half
    tensor = lax.axis_index("tensor")
    clus = lax.axis_index("clus")
    own_start = pl.multiple_of(tensor * half, half)
    other_start = pl.multiple_of((1 - tensor) * half, half)
    sides = ((own_ref, own_start), (other_ref, other_start))
    lane = iota((PAD, tokens), 1)
    for i in range(images):
        heads = slice(i * PAD, (i + 1) * PAD)
        scores = nt_dot(probe_ref[0, heads], own_ref[i]) + nt_dot(probe_ref[1, heads], other_ref[i])
        mean, scale = mean_ref[i : i + 1, :tokens], scale_ref[i : i + 1, :tokens]
        scores = (scores - sums_ref[heads, 0:1] * mean) * scale + const_ref[heads, 0:1]
        scores = jnp.where(lane < lengths_ref[i], scores, -1e30)
        exponent = jnp.exp(scores - jnp.max(scores, axis=1, keepdims=True))
        weights = exponent * (1.0 / jnp.sum(exponent, axis=1, keepdims=True))
        part = (weights * scale).astype(BF16)
        offset = jnp.sum(part.astype(F32) * mean, axis=1, keepdims=True)
        for ref, start in sides:
            summed = jnp.dot(part, ref[i], preferred_element_type=F32) - offset
            summed = summed * gains_ref[0:1, pl.ds(start, half)]
            summed = summed + shifts_ref[0:1, pl.ds(start, half)]
            mixed_ref[heads, pl.ds(start, half)] = summed.astype(BF16)
    context = jnp.dot(mixed_ref[...], w_ref[2], preferred_element_type=F32)
    mask = iota((PAD, half), 0) == iota((PAD, half), 1) // HEAD
    context = jnp.sum(jnp.where(mask[None], context.reshape(images, PAD, half), 0.0), axis=1)
    context = context + biases_ref[1:2, pl.ds(own_start, half)]
    fill = jnp.zeros((PAD - images, half), F32)
    context = jnp.concatenate([context, fill], axis=0).astype(BF16)
    out = jnp.dot(context, w_out_ref[...], preferred_element_type=F32)
    extra = jnp.where(tensor == 0, first_ref[...], 0.0)
    row, lane = iota((PAD, width), 0), iota((PAD, width), 1)
    own_images = images // 2
    for j in range(own_images):
        place = tensor * own_images + j
        hit = (lane // (2 * PAD) == clus) & (lane % PAD == place)
        cluster, rank = clusters_ref[j], ranks_ref[j]
        alive = (place < counts_ref[0]).astype(jnp.int32)
        for k, value in enumerate((cluster, rank // 64, rank % 64, alive)):
            extra = jnp.where(hit & (row == images + k), value.astype(F32), extra)
    out_ref[:PAD, :] = (out + extra).astype(BF16)
    quarter, embed = w_proj_ref.shape[0] // 4, w_proj_ref.shape[1]
    out_ref[PAD:, :embed] = w_proj_ref[: 3 * quarter, :]
    rest = width - embed
    for k in range(3):
        rows = slice(PAD + k * quarter, PAD + (k + 1) * quarter)
        out_ref[rows, embed:] = w_proj_ref[3 * quarter :, k * rest : (k + 1) * rest]


def unpack_kernel(rows_ref, out_ref):
    members, size = rows_ref.shape[:2]
    embed = out_ref.shape[1]
    rest = rows_ref.shape[2] - embed
    quarter = (size - PAD) // 3
    for m in range(members):
        start = m * 4 * quarter
        out_ref[start : start + 3 * quarter, :] = rows_ref[m, PAD:, :embed]
        for k in range(3):
            rows = slice(PAD + k * quarter, PAD + (k + 1) * quarter)
            out_ref[start + 3 * quarter : start + 4 * quarter, k * rest : (k + 1) * rest] = (
                rows_ref[m, rows, embed:]
            )


def mlp_kernel(
    rows_ref, gains_ref, shifts_ref, biases_ref, w1_ref, b1_ref, w2_ref, out_ref, first_ref, meta_ref
):
    members, _, width = rows_ref.shape
    total = members * PAD
    images = PAD - 4
    member = lax.axis_index("clus") * 2 + lax.axis_index("tensor")
    rows = rows_ref[:, :PAD, :].reshape(total, width)
    ints = jnp.sum(rows[:, :total].astype(F32).reshape(members, PAD, total), axis=0)
    cluster, rank_high, rank_low, alive = (ints[images + k : images + k + 1] for k in range(4))
    owner = jnp.floor(cluster * (1.0 / CLUS_DP))
    lane = iota((1, total), 1)
    valid = lane % PAD < images
    place = lane - (lane & PAD)
    before = iota((total, total), 0)
    earlier = (
        (as_column(owner) == owner) & (before % (2 * PAD) < images) & (before < place)
    )
    slot = jnp.sum(jnp.where(earlier, 1.0, 0.0), axis=0, keepdims=True)
    target = jnp.where(valid, owner * SLOT + slot, -1.0)
    slots = members * SLOT
    chosen = jnp.where(iota((slots, total), 0).astype(F32) == target, 1.0, 0.0).astype(BF16)
    first = jnp.dot(chosen, rows, preferred_element_type=F32) + biases_ref[2:3, :]
    mixed = layer_norm(first, gains_ref[1:2, :], shifts_ref[1:2, :]).astype(BF16)
    inner = jnp.dot(mixed, w1_ref[...], preferred_element_type=F32) + b1_ref[...]
    inner = (inner * jax.nn.sigmoid(1.702 * inner)).astype(BF16)
    out_ref[...] = jnp.dot(inner, w2_ref[...], preferred_element_type=F32).astype(BF16)
    mine = (iota((PAD, total), 0) + member * SLOT).astype(F32) == target
    mine = mine & (iota((PAD, total), 0) < SLOT)
    picked = jnp.dot(
        jnp.where(mine, 1.0, 0.0).astype(BF16), rows, preferred_element_type=F32
    )
    first_ref[...] = picked[:SLOT] + biases_ref[2:3, :]
    single = (mine & (lane % (2 * PAD) < PAD))[:SLOT]
    home = ((lane // (2 * PAD)) * images + lane % PAD + 1).astype(F32)
    meta = jnp.zeros((SLOT, INTS), F32)
    for k, value in enumerate((cluster, rank_high, rank_low, alive, home)):
        column = jnp.sum(jnp.where(single, value, 0.0), axis=1, keepdims=True)
        meta = jnp.where(iota((SLOT, INTS), 1) == k, column, meta)
    meta_ref[...] = meta


def embed_kernel(
    parts_ref, first_ref, meta_ref, gains_ref, shifts_ref, biases_ref, w_ref, send_ref, feat_ref
):
    second = jnp.sum(parts_ref[...].astype(F32), axis=0) + first_ref[...] + biases_ref[3:4, :]
    pooled = layer_norm(second, gains_ref[2:3, :], shifts_ref[2:3, :]).astype(BF16)
    features = jnp.dot(pooled, w_ref[...], preferred_element_type=F32).astype(BF16)
    feat_ref[...] = features
    as_float = features.astype(F32)
    unit = as_float * lax.rsqrt(jnp.sum(as_float * as_float, axis=-1, keepdims=True) + 1e-06)
    row = jnp.concatenate([unit, meta_ref[...]], axis=1).astype(BF16)
    send_ref[...] = jnp.broadcast_to(row[None], send_ref.shape)


def nearest_kernel(keys_ref, own_ref, feat_ref, meta_ref, out_ref):
    width = feat_ref.shape[1]
    keys = keys_ref[...]
    similar = nt_dot(own_ref[0][:, :width], keys[:, :width])
    select = (iota((SLOT, INTS), 0) == iota((SLOT, INTS), 1)).astype(F32).astype(BF16)
    key_ints = nt_dot(select, keys[:, width:])
    lane = iota((SLOT, INTS), 1)
    cluster, rank_high, rank_low, alive, home = (
        jnp.sum(jnp.where(lane == k, meta_ref[...], 0.0), axis=1, keepdims=True) for k in range(5)
    )
    key_rank = key_ints[1:2] * 64.0 + key_ints[2:3]
    allowed = (
        (key_ints[3:4] > 0.5)
        & (key_ints[0:1] == cluster)
        & (key_rank < rank_high * 64.0 + rank_low)
    )
    best = jnp.max(jnp.where(allowed, similar, -2.0), axis=1, keepdims=True)
    best = jnp.where(alive > 0.5, jnp.maximum(best, -1.0), -1.0)
    high = best.astype(BF16).astype(F32)
    middle = (best - high).astype(BF16).astype(F32)
    low = best - high - middle
    tail = jnp.where(lane == 0, high, jnp.where(lane == 1, middle, jnp.where(lane == 2, low, 0.0)))
    data = jnp.concatenate([feat_ref[...].astype(F32), tail], axis=1)
    data = jnp.concatenate([data, jnp.zeros_like(data)], axis=0).astype(BF16)
    slots = out_ref.shape[0]
    code = iota((SLOT, slots), 1)
    own_images = (PAD - 4) // 2
    wanted = jnp.where(code % SLOT < own_images, code // SLOT * own_images + code % SLOT + 1, -1)
    hit = jnp.where(wanted.astype(F32) == home, 1.0, 0.0)
    hit = jnp.concatenate([hit, jnp.zeros_like(hit)], axis=0).astype(BF16)
    out_ref[...] = tn_dot(hit, data).astype(BF16)


def struct(shape, dtype):
    return jax.ShapeDtypeStruct(shape, dtype)


def whole(memory=pltpu.VMEM):
    return pl.BlockSpec(memory_space=memory)


def local(
    hidden,
    token_lengths,
    image_counts,
    cluster_ids,
    order_ranks,
    ln_gains,
    ln_biases,
    w_qkv,
    layer_biases,
    w_out,
    w_fc1,
    fc1_bias,
    w_fc2,
    w_proj,
):
    images, tokens, half = hidden.shape
    width = 2 * half
    embed = w_proj.shape[1]
    members = lax.axis_size("clus") * 2
    owners = lax.axis_size("dp")
    own_images = images // 2
    params = pltpu.CompilerParams(vmem_limit_bytes=24 * 1024 * 1024)
    other = lax.ppermute(hidden, "tensor", [(0, 1), (1, 0)])
    w_three = jnp.transpose(w_qkv, (1, 0, 2))
    stats = pl.pallas_call(
        stats_kernel, out_shape=struct((TABLE, STAT), F32), compiler_params=params
    )(hidden)
    stats = lax.all_gather(stats, "tensor", axis=0, tiled=False)
    heads = images * PAD
    probe, sums, const, mean, scale, residual = pl.pallas_call(
        query_kernel,
        out_shape=(
            struct((2, heads, half), BF16),
            struct((heads, STAT), F32),
            struct((heads, STAT), F32),
            struct((PAD, TABLE), F32),
            struct((PAD, TABLE), F32),
            struct((PAD, width), F32),
        ),
        compiler_params=params,
    )(stats, ln_gains, ln_biases, w_three, layer_biases)
    shard = w_proj.shape[0] * embed // width
    partial = pl.pallas_call(
        attend_kernel,
        out_shape=struct((PAD + shard, width), BF16),
        in_specs=[whole()] * 2 + [whole(pltpu.SMEM)] * 4 + [whole()] * 12,
        out_specs=whole(),
        scratch_shapes=[pltpu.VMEM((heads, width), BF16)],
        compiler_params=params,
    )(
        hidden,
        other,
        token_lengths,
        image_counts,
        cluster_ids,
        order_ranks,
        probe,
        sums,
        const,
        mean,
        scale,
        residual,
        ln_gains,
        ln_biases,
        layer_biases,
        w_three,
        w_out,
        w_proj,
    )
    rows = lax.all_gather(partial, MEMBERS, axis=0, tiled=False)
    rows = rows.reshape(members, PAD + shard, width)
    proj = pl.pallas_call(
        unpack_kernel, out_shape=struct((width, embed), BF16), compiler_params=params
    )(rows)
    sent, first, meta = pl.pallas_call(
        mlp_kernel,
        out_shape=(
            struct((members * SLOT, width), BF16),
            struct((SLOT, width), F32),
            struct((SLOT, INTS), F32),
        ),
        compiler_params=params,
    )(rows, ln_gains, ln_biases, layer_biases, w_fc1, fc1_bias.reshape(1, -1), w_fc2)
    parts = lax.all_to_all(
        sent.reshape(members, SLOT, width), MEMBERS, split_axis=0, concat_axis=0, tiled=True
    )
    send, features = pl.pallas_call(
        embed_kernel,
        out_shape=(struct((owners, SLOT, embed + INTS), BF16), struct((SLOT, embed), BF16)),
        compiler_params=params,
    )(parts, first, meta, ln_gains, ln_biases, layer_biases, proj)
    keys = lax.all_to_all(send, "dp", split_axis=0, concat_axis=0, tiled=True)
    back = pl.pallas_call(
        nearest_kernel,
        out_shape=struct((members * SLOT, embed + INTS), BF16),
        compiler_params=params,
    )(keys.reshape(owners * SLOT, embed + INTS), send, features, meta)
    home = lax.all_to_all(
        back.reshape(members, SLOT, embed + INTS), MEMBERS, split_axis=0, concat_axis=0, tiled=True
    )
    home = jnp.sum(home[:, :own_images].astype(F32), axis=0)
    nearest = home[:, embed] + home[:, embed + 1] + home[:, embed + 2]
    return (home[:, :embed].astype(BF16), nearest)


def solution(mesh):
    return jax.shard_map(
        local,
        mesh=mesh,
        in_specs=(
            P(("dp", "clus"), None, "tensor"),
            P(("dp", "clus")),
            P(("dp", "clus")),
            P(("dp", "clus", "tensor")),
            P(("dp", "clus", "tensor")),
            P(),
            P(),
            P(None, None, "tensor"),
            P(),
            P("tensor", None),
            P(None, ("clus", "tensor")),
            P(("clus", "tensor")),
            P(("clus", "tensor"), None),
            P(("clus", "tensor"), None),
        ),
        out_specs=(P(("dp", "clus", "tensor"), None), P(("dp", "clus", "tensor"))),
        check_vma=False,
    )
```

```python
import jax
import jax.numpy as jnp
from jax import lax
from jax.experimental import pallas as pl
from jax.experimental.pallas import tpu as pltpu
from jax.sharding import PartitionSpec as P

HEAD = 64
CLUS_DP = 4
SLOT = 8
PAD = 16
INTS = 128
STAT = 128
TABLE = 384
EPS = 1e-05
F32 = jnp.float32
BF16 = jnp.bfloat16
MEMBERS = ("clus", "tensor")


def iota(shape, axis):
    return lax.broadcasted_iota(jnp.int32, shape, axis)


def layer_norm(values, gain_row, shift_row):
    average = jnp.mean(values, axis=-1, keepdims=True)
    centered = values - average
    spread = jnp.mean(centered * centered, axis=-1, keepdims=True)
    return centered * lax.rsqrt(spread + EPS) * gain_row + shift_row


def as_column(row):
    size = row.shape[1]
    eye = iota((size, size), 0) == iota((size, size), 1)
    return jnp.sum(jnp.where(eye, row, 0.0), axis=1, keepdims=True)


def nt_dot(left, right):
    return lax.dot_general(left, right, (((1,), (1,)), ((), ())), preferred_element_type=F32)


def tn_dot(left, right):
    return lax.dot_general(left, right, (((0,), (0,)), ((), ())), preferred_element_type=F32)


def copies_kernel(shard_ref, out_ref, sem):
    copies = [
        pltpu.make_async_copy(shard_ref, out_ref.at[c], sem.at[c]) for c in range(out_ref.shape[0])
    ]
    for copy in copies:
        copy.start()
    for copy in copies:
        copy.wait()


def stats_kernel(own_ref, table_ref):
    images, tokens, half = own_ref.shape
    rows, lane = table_ref.shape[1], iota((tokens, STAT), 1)
    table = jnp.zeros((tokens, STAT), F32)
    for i in range(images):
        states = own_ref[i].astype(F32)
        total = jnp.sum(states, axis=1, keepdims=True)
        centered = states - total * (1.0 / half)
        spread = jnp.sum(centered * centered, axis=1, keepdims=True)
        table = jnp.where(lane == i, total, table)
        table = jnp.where(lane == PAD + i, spread, table)
    table = jnp.concatenate([table, jnp.zeros((rows - tokens, STAT), F32)], axis=0)
    table_ref[...] = jnp.transpose(table)[: 2 * PAD]


def score_kernel(
    own_ref,
    other_ref,
    lengths_ref,
    gains_ref,
    shifts_ref,
    w_ref,
    biases_ref,
    raw_ref,
    sums_ref,
    const_ref,
    first_ref,
):
    images, tokens, half = own_ref.shape
    width = 2 * half
    tensor = lax.axis_index("tensor")
    own_first, other_first = own_ref[:, 0, :].astype(F32), other_ref[:, 0, :].astype(F32)
    first = jnp.concatenate(
        [
            jnp.where(tensor == 0, own_first, other_first),
            jnp.where(tensor == 0, other_first, own_first),
        ],
        axis=1,
    )
    first_ref[:images, :] = first
    first_ref[images:, :] = jnp.zeros((PAD - images, width), F32)
    normed = layer_norm(first, gains_ref[0:1, :], shifts_ref[0:1, :]).astype(BF16)
    start = pl.multiple_of(tensor * half, half)
    query = jnp.dot(normed, w_ref[0], preferred_element_type=F32)
    query = (query + biases_ref[0:1, pl.ds(start, half)]) * HEAD ** (-0.5)
    query = query.astype(BF16).astype(F32)
    mask = iota((PAD, half), 0) == iota((PAD, half), 1) // HEAD
    spread = jnp.where(mask[None], query[:, None, :], 0.0).reshape(images * PAD, half).astype(BF16)
    probe = nt_dot(spread, w_ref[1])
    const = jnp.sum(probe * shifts_ref[0:1, :], axis=1, keepdims=True)
    probe = (probe * gains_ref[0:1, :]).astype(BF16)
    sums = jnp.sum(probe.astype(F32), axis=1, keepdims=True)
    sums_ref[...] = jnp.broadcast_to(sums, sums_ref.shape)
    const_ref[...] = jnp.broadcast_to(const, const_ref.shape)
    own_probe = jnp.where(tensor == 0, probe[:, :half], probe[:, half:])
    other_probe = jnp.where(tensor == 0, probe[:, half:], probe[:, :half])
    lane = iota((PAD, tokens), 1)
    for i in range(images):
        heads = slice(i * PAD, (i + 1) * PAD)
        scores = nt_dot(own_probe[heads], own_ref[i]) + nt_dot(other_probe[heads], other_ref[i])
        raw_ref[heads, :tokens] = jnp.where(lane < lengths_ref[i], scores, -1e30)


def attend_kernel(
    own_ref,
    other_ref,
    counts_ref,
    clusters_ref,
    ranks_ref,
    own_table_ref,
    other_table_ref,
    raw_ref,
    sums_ref,
    const_ref,
    first_ref,
    gains_ref,
    shifts_ref,
    biases_ref,
    w_ref,
    w_out_ref,
    out_ref,
    mixed_ref,
):
    images, tokens, half = own_ref.shape
    width = 2 * half
    tensor = lax.axis_index("tensor")
    clus = lax.axis_index("clus")
    own_start = pl.multiple_of(tensor * half, half)
    other_start = pl.multiple_of((1 - tensor) * half, half)
    left, right = own_table_ref[...], other_table_ref[...]
    mean = (left[:images] + right[:images]) * (1.0 / width)
    apart = (left[:images] - right[:images]) * (1.0 / half)
    spread = left[PAD : PAD + images] + right[PAD : PAD + images] + apart * apart * (half / 2)
    scale = lax.rsqrt(spread * (1.0 / width) + EPS)
    mean, scale = (
        jnp.broadcast_to(row[:, None, :], (images, PAD, row.shape[1])).reshape(
            images * PAD, row.shape[1]
        )[:, :tokens]
        for row in (mean, scale)
    )
    scores = (raw_ref[:, :tokens] - sums_ref[:, 0:1] * mean) * scale + const_ref[:, 0:1]
    exponent = jnp.exp(scores - jnp.max(scores, axis=1, keepdims=True))
    weights = exponent * (1.0 / jnp.sum(exponent, axis=1, keepdims=True))
    part = (weights * scale).astype(BF16)
    offset = jnp.sum(part.astype(F32) * mean, axis=1, keepdims=True)
    for ref, start in ((own_ref, own_start), (other_ref, other_start)):
        gain, shift = gains_ref[0:1, pl.ds(start, half)], shifts_ref[0:1, pl.ds(start, half)]
        for i in range(images):
            heads = slice(i * PAD, (i + 1) * PAD)
            summed = jnp.dot(part[heads], ref[i], preferred_element_type=F32) - offset[heads]
            mixed_ref[heads, pl.ds(start, half)] = (summed * gain + shift).astype(BF16)
    context = jnp.dot(mixed_ref[...], w_ref[2], preferred_element_type=F32)
    mask = iota((PAD, half), 0) == iota((PAD, half), 1) // HEAD
    context = jnp.sum(jnp.where(mask[None], context.reshape(images, PAD, half), 0.0), axis=1)
    context = context + biases_ref[1:2, pl.ds(own_start, half)]
    fill = jnp.zeros((PAD - images, half), F32)
    context = jnp.concatenate([context, fill], axis=0).astype(BF16)
    out = jnp.dot(context, w_out_ref[...], preferred_element_type=F32)
    extra = jnp.where(tensor == 0, first_ref[...], 0.0)
    row, lane = iota((PAD, width), 0), iota((PAD, width), 1)
    own_images = images // 2
    for j in range(own_images):
        place = tensor * own_images + j
        hit = (lane // (2 * PAD) == clus) & (lane % PAD == place)
        cluster, rank = clusters_ref[j], ranks_ref[j]
        alive = (place < counts_ref[0]).astype(jnp.int32)
        for k, value in enumerate((cluster, rank // 64, rank % 64, alive)):
            extra = jnp.where(hit & (row == images + k), value.astype(F32), extra)
    out_ref[...] = (out + extra).astype(BF16)


def unpack_kernel(own_ref, other_ref, out_ref):
    clus, rows = own_ref.shape[:2]
    tensor = lax.axis_index("tensor")
    for c in range(clus):
        for ref, side in ((own_ref, tensor), (other_ref, 1 - tensor)):
            start = pl.multiple_of((2 * c + side) * rows, rows)
            out_ref[pl.ds(start, rows), :] = ref[c]


def mlp_kernel(
    rows_ref,
    gains_ref,
    shifts_ref,
    biases_ref,
    w1_ref,
    b1_ref,
    w2_ref,
    held_ref,
    out_ref,
    first_ref,
    meta_ref,
    passed_ref,
):
    total, width = rows_ref.shape
    images = PAD - 4
    members = total // PAD
    member = lax.axis_index("clus") * 2 + lax.axis_index("tensor")
    rows = rows_ref[...]
    ints = jnp.sum(rows[:, :total].astype(F32).reshape(members, PAD, total), axis=0)
    cluster, rank_high, rank_low, alive = (ints[images + k : images + k + 1] for k in range(4))
    owner = jnp.floor(cluster * (1.0 / CLUS_DP))
    lane = iota((1, total), 1)
    valid = lane % PAD < images
    place = lane - (lane & PAD)
    before = iota((total, total), 0)
    earlier = (
        (as_column(owner) == owner) & (before % (2 * PAD) < images) & (before < place)
    )
    slot = jnp.sum(jnp.where(earlier, 1.0, 0.0), axis=0, keepdims=True)
    target = jnp.where(valid, owner * SLOT + slot, -1.0)
    slots = members * SLOT
    chosen = jnp.where(iota((slots, total), 0).astype(F32) == target, 1.0, 0.0).astype(BF16)
    first = jnp.dot(chosen, rows, preferred_element_type=F32) + biases_ref[2:3, :]
    mixed = layer_norm(first, gains_ref[1:2, :], shifts_ref[1:2, :]).astype(BF16)
    inner = jnp.dot(mixed, w1_ref[...], preferred_element_type=F32) + b1_ref[...]
    inner = (inner * jax.nn.sigmoid(1.702 * inner)).astype(BF16)
    out_ref[...] = jnp.dot(inner, w2_ref[...], preferred_element_type=F32).astype(BF16)
    mine = (iota((PAD, total), 0) + member * SLOT).astype(F32) == target
    mine = mine & (iota((PAD, total), 0) < SLOT)
    picked = jnp.dot(
        jnp.where(mine, 1.0, 0.0).astype(BF16), rows, preferred_element_type=F32
    )
    first_ref[...] = picked[:SLOT] + biases_ref[2:3, :]
    single = (mine & (lane % (2 * PAD) < PAD))[:SLOT]
    home = ((lane // (2 * PAD)) * images + lane % PAD + 1).astype(F32)
    meta = jnp.zeros((SLOT, INTS), F32)
    for k, value in enumerate((cluster, rank_high, rank_low, alive, home)):
        column = jnp.sum(jnp.where(single, value, 0.0), axis=1, keepdims=True)
        meta = jnp.where(iota((SLOT, INTS), 1) == k, column, meta)
    meta_ref[...] = meta


def embed_kernel(
    parts_ref, first_ref, meta_ref, gains_ref, shifts_ref, biases_ref, w_ref, send_ref, feat_ref
):
    second = jnp.sum(parts_ref[...].astype(F32), axis=0) + first_ref[...] + biases_ref[3:4, :]
    pooled = layer_norm(second, gains_ref[2:3, :], shifts_ref[2:3, :]).astype(BF16)
    features = jnp.dot(pooled, w_ref[...], preferred_element_type=F32).astype(BF16)
    feat_ref[...] = features
    as_float = features.astype(F32)
    unit = as_float * lax.rsqrt(jnp.sum(as_float * as_float, axis=-1, keepdims=True) + 1e-06)
    row = jnp.concatenate([unit, meta_ref[...]], axis=1).astype(BF16)
    send_ref[...] = jnp.broadcast_to(row[None], send_ref.shape)


def nearest_kernel(keys_ref, own_ref, feat_ref, meta_ref, out_ref):
    width = feat_ref.shape[1]
    keys = keys_ref[...]
    similar = nt_dot(own_ref[0][:, :width], keys[:, :width])
    select = (iota((SLOT, INTS), 0) == iota((SLOT, INTS), 1)).astype(F32).astype(BF16)
    key_ints = nt_dot(select, keys[:, width:])
    lane = iota((SLOT, INTS), 1)
    cluster, rank_high, rank_low, alive, home = (
        jnp.sum(jnp.where(lane == k, meta_ref[...], 0.0), axis=1, keepdims=True) for k in range(5)
    )
    key_rank = key_ints[1:2] * 64.0 + key_ints[2:3]
    allowed = (
        (key_ints[3:4] > 0.5)
        & (key_ints[0:1] == cluster)
        & (key_rank < rank_high * 64.0 + rank_low)
    )
    best = jnp.max(jnp.where(allowed, similar, -2.0), axis=1, keepdims=True)
    best = jnp.where(alive > 0.5, jnp.maximum(best, -1.0), -1.0)
    high = best.astype(BF16).astype(F32)
    middle = (best - high).astype(BF16).astype(F32)
    low = best - high - middle
    tail = jnp.where(lane == 0, high, jnp.where(lane == 1, middle, jnp.where(lane == 2, low, 0.0)))
    data = jnp.concatenate([feat_ref[...].astype(F32), tail], axis=1)
    data = jnp.concatenate([data, jnp.zeros_like(data)], axis=0).astype(BF16)
    slots = out_ref.shape[0]
    code = iota((SLOT, slots), 1)
    own_images = (PAD - 4) // 2
    wanted = jnp.where(code % SLOT < own_images, code // SLOT * own_images + code % SLOT + 1, -1)
    hit = jnp.where(wanted.astype(F32) == home, 1.0, 0.0)
    hit = jnp.concatenate([hit, jnp.zeros_like(hit)], axis=0).astype(BF16)
    out_ref[...] = tn_dot(hit, data).astype(BF16)


def struct(shape, dtype):
    return jax.ShapeDtypeStruct(shape, dtype)


def cost(micros):
    return pl.CostEstimate(
        flops=int(micros * 1.15e9), bytes_accessed=int(micros * 3.69e6), transcendentals=0
    )


def whole(memory=pltpu.VMEM):
    return pl.BlockSpec(memory_space=memory)


def local(
    hidden,
    token_lengths,
    image_counts,
    cluster_ids,
    order_ranks,
    ln_gains,
    ln_biases,
    w_qkv,
    layer_biases,
    w_out,
    w_fc1,
    fc1_bias,
    w_fc2,
    w_proj,
):
    images, tokens, half = hidden.shape
    width = 2 * half
    embed = w_proj.shape[1]
    members = lax.axis_size("clus") * 2
    owners = lax.axis_size("dp")
    own_images = images // 2
    params = pltpu.CompilerParams(vmem_limit_bytes=24 * 1024 * 1024)
    swap = [(0, 1), (1, 0)]
    heads = images * PAD
    hbm = pl.BlockSpec(memory_space=pltpu.HBM)
    other = lax.ppermute(hidden, "tensor", swap)
    copied = pl.pallas_call(
        copies_kernel,
        out_shape=struct((members // 2, *w_proj.shape), BF16),
        in_specs=[hbm],
        out_specs=hbm,
        scratch_shapes=[pltpu.SemaphoreType.DMA((members // 2,))],
        compiler_params=params,
        cost_estimate=cost(4.0),
    )(w_proj)
    proj = lax.all_to_all(copied, "clus", split_axis=0, concat_axis=0, tiled=True)
    w_three = jnp.transpose(w_qkv, (1, 0, 2))
    table = pl.pallas_call(
        stats_kernel,
        out_shape=struct((2 * PAD, TABLE), F32),
        compiler_params=params,
        cost_estimate=cost(2.0),
    )(hidden)
    other_table = lax.ppermute(table, "tensor", swap)
    raw, sums, const, residual = pl.pallas_call(
        score_kernel,
        out_shape=(
            struct((heads, TABLE), F32),
            struct((heads, STAT), F32),
            struct((heads, STAT), F32),
            struct((PAD, width), F32),
        ),
        in_specs=[whole()] * 2 + [whole(pltpu.SMEM)] + [whole()] * 4,
        out_specs=[whole()] * 4,
        compiler_params=params,
        cost_estimate=cost(4.0),
    )(hidden, other, token_lengths, ln_gains, ln_biases, w_three, layer_biases)
    partial = pl.pallas_call(
        attend_kernel,
        out_shape=struct((PAD, width), BF16),
        in_specs=[whole()] * 2 + [whole(pltpu.SMEM)] * 3 + [whole()] * 11,
        out_specs=whole(),
        scratch_shapes=[pltpu.VMEM((heads, width), BF16)],
        compiler_params=params,
        cost_estimate=cost(4.0),
    )(
        hidden,
        other,
        image_counts,
        cluster_ids,
        order_ranks,
        table,
        other_table,
        raw,
        sums,
        const,
        residual,
        ln_gains,
        ln_biases,
        layer_biases,
        w_three,
        w_out,
    )
    rows = lax.all_gather(partial, MEMBERS, axis=0, tiled=True)
    sent, first, meta, proj = pl.pallas_call(
        mlp_kernel,
        out_shape=(
            struct((members * SLOT, width), BF16),
            struct((SLOT, width), F32),
            struct((SLOT, INTS), F32),
            struct(proj.shape, BF16),
        ),
        in_specs=[whole()] * 7 + [hbm],
        out_specs=[whole()] * 3 + [hbm],
        input_output_aliases={7: 3},
        compiler_params=params,
        cost_estimate=cost(1.5),
    )(rows, ln_gains, ln_biases, layer_biases, w_fc1, fc1_bias.reshape(1, -1), w_fc2, proj)
    parts = lax.all_to_all(
        sent.reshape(members, SLOT, width), MEMBERS, split_axis=0, concat_axis=0, tiled=True
    )
    proj = pl.pallas_call(
        unpack_kernel,
        out_shape=struct((width, embed), BF16),
        compiler_params=params,
        cost_estimate=cost(0.7),
    )(proj, lax.ppermute(proj, "tensor", swap))
    send, features = pl.pallas_call(
        embed_kernel,
        out_shape=(struct((owners, SLOT, embed + INTS), BF16), struct((SLOT, embed), BF16)),
        compiler_params=params,
        cost_estimate=cost(0.6),
    )(parts, first, meta, ln_gains, ln_biases, layer_biases, proj)
    keys = lax.all_to_all(send, "dp", split_axis=0, concat_axis=0, tiled=True)
    back = pl.pallas_call(
        nearest_kernel,
        out_shape=struct((members * SLOT, embed + INTS), BF16),
        compiler_params=params,
        cost_estimate=cost(0.4),
    )(keys.reshape(owners * SLOT, embed + INTS), send, features, meta)
    home = lax.all_to_all(
        back.reshape(members, SLOT, embed + INTS), MEMBERS, split_axis=0, concat_axis=0, tiled=True
    )
    home = jnp.sum(home[:, :own_images].astype(F32), axis=0)
    nearest = home[:, embed] + home[:, embed + 1] + home[:, embed + 2]
    return (home[:, :embed].astype(BF16), nearest)


def solution(mesh):
    return jax.shard_map(
        local,
        mesh=mesh,
        in_specs=(
            P(("dp", "clus"), None, "tensor"),
            P(("dp", "clus")),
            P(("dp", "clus")),
            P(("dp", "clus", "tensor")),
            P(("dp", "clus", "tensor")),
            P(),
            P(),
            P(None, None, "tensor"),
            P(),
            P("tensor", None),
            P(None, ("clus", "tensor")),
            P(("clus", "tensor")),
            P(("clus", "tensor"), None),
            P(("clus", "tensor"), None),
        ),
        out_specs=(P(("dp", "clus", "tensor"), None), P(("dp", "clus", "tensor"))),
        check_vma=False,
    )
```

```python
import jax
import jax.numpy as jnp
from jax import lax
from jax.experimental import pallas as pl
from jax.experimental.pallas import tpu as pltpu
from jax.sharding import PartitionSpec as P

HEAD = 64
CLUS_DP = 4
SLOT = 8
PAD = 16
INTS = 128
STAT = 128
TABLE = 384
EPS = 1e-05
F32 = jnp.float32
BF16 = jnp.bfloat16
MEMBERS = ("clus", "tensor")


def iota(shape, axis):
    return lax.broadcasted_iota(jnp.int32, shape, axis)


def quarter_of(dp, flip):
    x_bit, y_bit = dp % 2, dp // 4 % 2
    x_bit = 1 - x_bit if flip % 2 else x_bit
    y_bit = 1 - y_bit if flip // 4 else y_bit
    return 2 * y_bit + x_bit


def layer_norm(values, gain_row, shift_row):
    average = jnp.mean(values, axis=-1, keepdims=True)
    centered = values - average
    spread = jnp.mean(centered * centered, axis=-1, keepdims=True)
    return centered * lax.rsqrt(spread + EPS) * gain_row + shift_row


def as_column(row):
    size = row.shape[1]
    eye = iota((size, size), 0) == iota((size, size), 1)
    return jnp.sum(jnp.where(eye, row, 0.0), axis=1, keepdims=True)


def nt_dot(left, right):
    return lax.dot_general(left, right, (((1,), (1,)), ((), ())), preferred_element_type=F32)


def tn_dot(left, right):
    return lax.dot_general(left, right, (((0,), (0,)), ((), ())), preferred_element_type=F32)


def stats_kernel(own_ref, table_ref):
    images, tokens, half = own_ref.shape
    rows, lane = table_ref.shape[1], iota((tokens, STAT), 1)
    table = jnp.zeros((tokens, STAT), F32)
    for i in range(images):
        states = own_ref[i].astype(F32)
        total = jnp.sum(states, axis=1, keepdims=True)
        centered = states - total * (1.0 / half)
        spread = jnp.sum(centered * centered, axis=1, keepdims=True)
        table = jnp.where(lane == i, total, table)
        table = jnp.where(lane == PAD + i, spread, table)
    table = jnp.concatenate([table, jnp.zeros((rows - tokens, STAT), F32)], axis=0)
    table_ref[...] = jnp.transpose(table)[: 2 * PAD]


def score_kernel(
    own_ref,
    other_ref,
    lengths_ref,
    gains_ref,
    shifts_ref,
    w_ref,
    biases_ref,
    raw_ref,
    sums_ref,
    const_ref,
    first_ref,
):
    images, tokens, half = own_ref.shape
    width = 2 * half
    tensor = lax.axis_index("tensor")
    own_first, other_first = own_ref[:, 0, :].astype(F32), other_ref[:, 0, :].astype(F32)
    first = jnp.concatenate(
        [
            jnp.where(tensor == 0, own_first, other_first),
            jnp.where(tensor == 0, other_first, own_first),
        ],
        axis=1,
    )
    first_ref[:images, :] = first
    first_ref[images:, :] = jnp.zeros((PAD - images, width), F32)
    normed = layer_norm(first, gains_ref[0:1, :], shifts_ref[0:1, :]).astype(BF16)
    start = pl.multiple_of(tensor * half, half)
    query = jnp.dot(normed, w_ref[0], preferred_element_type=F32)
    query = (query + biases_ref[0:1, pl.ds(start, half)]) * HEAD ** (-0.5)
    query = query.astype(BF16).astype(F32)
    mask = iota((PAD, half), 0) == iota((PAD, half), 1) // HEAD
    spread = jnp.where(mask[None], query[:, None, :], 0.0).reshape(images * PAD, half).astype(BF16)
    probe = nt_dot(spread, w_ref[1])
    const = jnp.sum(probe * shifts_ref[0:1, :], axis=1, keepdims=True)
    probe = (probe * gains_ref[0:1, :]).astype(BF16)
    sums = jnp.sum(probe.astype(F32), axis=1, keepdims=True)
    sums_ref[...] = jnp.broadcast_to(sums, sums_ref.shape)
    const_ref[...] = jnp.broadcast_to(const, const_ref.shape)
    own_probe = jnp.where(tensor == 0, probe[:, :half], probe[:, half:])
    other_probe = jnp.where(tensor == 0, probe[:, half:], probe[:, :half])
    lane = iota((PAD, tokens), 1)
    for i in range(images):
        heads = slice(i * PAD, (i + 1) * PAD)
        scores = nt_dot(own_probe[heads], own_ref[i]) + nt_dot(other_probe[heads], other_ref[i])
        raw_ref[heads, :tokens] = jnp.where(lane < lengths_ref[i], scores, -1e30)


def attend_kernel(
    own_ref,
    other_ref,
    counts_ref,
    clusters_ref,
    ranks_ref,
    own_table_ref,
    other_table_ref,
    raw_ref,
    sums_ref,
    const_ref,
    first_ref,
    gains_ref,
    shifts_ref,
    biases_ref,
    w_ref,
    w_out_ref,
    w_proj_ref,
    out_ref,
    mixed_ref,
):
    images, tokens, half = own_ref.shape
    width = 2 * half
    tensor = lax.axis_index("tensor")
    clus = lax.axis_index("clus")
    own_start = pl.multiple_of(tensor * half, half)
    other_start = pl.multiple_of((1 - tensor) * half, half)
    left, right = own_table_ref[...], other_table_ref[...]
    mean = (left[:images] + right[:images]) * (1.0 / width)
    apart = (left[:images] - right[:images]) * (1.0 / half)
    spread = left[PAD : PAD + images] + right[PAD : PAD + images] + apart * apart * (half / 2)
    scale = lax.rsqrt(spread * (1.0 / width) + EPS)
    mean, scale = (
        jnp.broadcast_to(row[:, None, :], (images, PAD, row.shape[1])).reshape(
            images * PAD, row.shape[1]
        )[:, :tokens]
        for row in (mean, scale)
    )
    scores = (raw_ref[:, :tokens] - sums_ref[:, 0:1] * mean) * scale + const_ref[:, 0:1]
    exponent = jnp.exp(scores - jnp.max(scores, axis=1, keepdims=True))
    weights = exponent * (1.0 / jnp.sum(exponent, axis=1, keepdims=True))
    part = (weights * scale).astype(BF16)
    offset = jnp.sum(part.astype(F32) * mean, axis=1, keepdims=True)
    for ref, start in ((own_ref, own_start), (other_ref, other_start)):
        gain, shift = gains_ref[0:1, pl.ds(start, half)], shifts_ref[0:1, pl.ds(start, half)]
        for i in range(images):
            heads = slice(i * PAD, (i + 1) * PAD)
            summed = jnp.dot(part[heads], ref[i], preferred_element_type=F32) - offset[heads]
            mixed_ref[heads, pl.ds(start, half)] = (summed * gain + shift).astype(BF16)
    context = jnp.dot(mixed_ref[...], w_ref[2], preferred_element_type=F32)
    mask = iota((PAD, half), 0) == iota((PAD, half), 1) // HEAD
    context = jnp.sum(jnp.where(mask[None], context.reshape(images, PAD, half), 0.0), axis=1)
    context = context + biases_ref[1:2, pl.ds(own_start, half)]
    fill = jnp.zeros((PAD - images, half), F32)
    context = jnp.concatenate([context, fill], axis=0).astype(BF16)
    out = jnp.dot(context, w_out_ref[...], preferred_element_type=F32)
    extra = jnp.where(tensor == 0, first_ref[...], 0.0)
    row, lane = iota((PAD, width), 0), iota((PAD, width), 1)
    own_images = images // 2
    for j in range(own_images):
        place = tensor * own_images + j
        hit = (lane // (2 * PAD) == clus) & (lane % PAD == place)
        cluster, rank = clusters_ref[j], ranks_ref[j]
        alive = (place < counts_ref[0]).astype(jnp.int32)
        for k, value in enumerate((cluster, rank // 64, rank % 64, alive)):
            extra = jnp.where(hit & (row == images + k), value.astype(F32), extra)
    out_ref[:, :width] = (out + extra).astype(BF16)
    piece = pl.multiple_of(quarter_of(lax.axis_index("dp"), 0) * PAD, PAD)
    out_ref[:, width:] = w_proj_ref[pl.ds(piece, PAD), :]


def cut_kernel(rows_ref, meta_ref, out_ref):
    clus, rows, embed = out_ref.shape
    tensor = lax.axis_index("tensor")
    width = rows_ref.shape[1] - embed
    for c in range(clus):
        start = pl.multiple_of((2 * c + tensor) * rows, rows)
        out_ref[c] = rows_ref[pl.ds(start, rows), width:]


def join_kernel(after_ref, own_ref, near_ref, far_ref, cross_ref, out_ref):
    dp = lax.axis_index("dp")
    for ref, flip in ((own_ref, 0), (near_ref, 1), (far_ref, 4), (cross_ref, 5)):
        out_ref[:, quarter_of(dp, flip)] = ref[...]


def unpack_kernel(own_ref, other_ref, out_ref):
    tensor = lax.axis_index("tensor")
    out_ref[:, tensor] = own_ref[...]
    out_ref[:, 1 - tensor] = other_ref[...]


def mlp_kernel(
    rows_ref,
    gains_ref,
    shifts_ref,
    biases_ref,
    w1_ref,
    b1_ref,
    w2_ref,
    out_ref,
    first_ref,
    meta_ref,
):
    total, width = rows_ref.shape[0], w1_ref.shape[0]
    images = PAD - 4
    members = total // PAD
    member = lax.axis_index("clus") * 2 + lax.axis_index("tensor")
    rows = rows_ref[:, :width]
    ints = jnp.sum(rows[:, :total].astype(F32).reshape(members, PAD, total), axis=0)
    cluster, rank_high, rank_low, alive = (ints[images + k : images + k + 1] for k in range(4))
    owner = jnp.floor(cluster * (1.0 / CLUS_DP))
    lane = iota((1, total), 1)
    valid = lane % PAD < images
    place = lane - (lane & PAD)
    before = iota((total, total), 0)
    earlier = (
        (as_column(owner) == owner) & (before % (2 * PAD) < images) & (before < place)
    )
    slot = jnp.sum(jnp.where(earlier, 1.0, 0.0), axis=0, keepdims=True)
    target = jnp.where(valid, owner * SLOT + slot, -1.0)
    slots = members * SLOT
    chosen = jnp.where(iota((slots, total), 0).astype(F32) == target, 1.0, 0.0).astype(BF16)
    first = jnp.dot(chosen, rows, preferred_element_type=F32) + biases_ref[2:3, :]
    mixed = layer_norm(first, gains_ref[1:2, :], shifts_ref[1:2, :]).astype(BF16)
    inner = jnp.dot(mixed, w1_ref[...], preferred_element_type=F32) + b1_ref[...]
    inner = (inner * jax.nn.sigmoid(1.702 * inner)).astype(BF16)
    out_ref[...] = jnp.dot(inner, w2_ref[...], preferred_element_type=F32).astype(BF16)
    mine = (iota((PAD, total), 0) + member * SLOT).astype(F32) == target
    mine = mine & (iota((PAD, total), 0) < SLOT)
    picked = jnp.dot(
        jnp.where(mine, 1.0, 0.0).astype(BF16), rows, preferred_element_type=F32
    )
    first_ref[...] = picked[:SLOT] + biases_ref[2:3, :]
    single = (mine & (lane % (2 * PAD) < PAD))[:SLOT]
    home = ((lane // (2 * PAD)) * images + lane % PAD + 1).astype(F32)
    meta = jnp.zeros((SLOT, INTS), F32)
    for k, value in enumerate((cluster, rank_high, rank_low, alive, home)):
        column = jnp.sum(jnp.where(single, value, 0.0), axis=1, keepdims=True)
        meta = jnp.where(iota((SLOT, INTS), 1) == k, column, meta)
    meta_ref[...] = meta


def pool_kernel(parts_ref, first_ref, meta_ref, gains_ref, shifts_ref, biases_ref, send_ref):
    second = jnp.sum(parts_ref[...].astype(F32), axis=0) + first_ref[...] + biases_ref[3:4, :]
    pooled = layer_norm(second, gains_ref[2:3, :], shifts_ref[2:3, :])
    row = jnp.concatenate([pooled, meta_ref[...]], axis=1).astype(BF16)
    send_ref[...] = jnp.broadcast_to(row[None], send_ref.shape)


def unit(features):
    norm = jnp.sum(features * features, axis=-1, keepdims=True)
    return (features * lax.rsqrt(norm + 1e-06)).astype(BF16)


def nearest_kernel(keys_ref, meta_ref, w_ref, out_ref, features_ref):
    width = w_ref.shape[0]
    keys = keys_ref[...]
    features = jnp.dot(keys[:, :width], w_ref[...], preferred_element_type=F32)
    features_ref[...] = features.astype(BF16).astype(F32)
    mine = pl.multiple_of(lax.axis_index("dp") * SLOT, SLOT)
    key_units = unit(features_ref[...])
    features = features_ref[pl.ds(mine, SLOT), :]
    similar = nt_dot(unit(features), key_units)
    select = (iota((SLOT, INTS), 0) == iota((SLOT, INTS), 1)).astype(F32).astype(BF16)
    key_ints = nt_dot(select, keys[:, width:])
    lane = iota((SLOT, INTS), 1)
    cluster, rank_high, rank_low, alive, home = (
        jnp.sum(jnp.where(lane == k, meta_ref[...], 0.0), axis=1, keepdims=True) for k in range(5)
    )
    key_rank = key_ints[1:2] * 64.0 + key_ints[2:3]
    allowed = (
        (key_ints[3:4] > 0.5)
        & (key_ints[0:1] == cluster)
        & (key_rank < rank_high * 64.0 + rank_low)
    )
    best = jnp.max(jnp.where(allowed, similar, -2.0), axis=1, keepdims=True)
    best = jnp.where(alive > 0.5, jnp.maximum(best, -1.0), -1.0)
    high = best.astype(BF16).astype(F32)
    middle = (best - high).astype(BF16).astype(F32)
    low = best - high - middle
    tail = jnp.where(lane == 0, high, jnp.where(lane == 1, middle, jnp.where(lane == 2, low, 0.0)))
    data = jnp.concatenate([features, tail], axis=1)
    data = jnp.concatenate([data, jnp.zeros_like(data)], axis=0).astype(BF16)
    slots = out_ref.shape[0]
    code = iota((SLOT, slots), 1)
    own_images = (PAD - 4) // 2
    wanted = jnp.where(code % SLOT < own_images, code // SLOT * own_images + code % SLOT + 1, -1)
    hit = jnp.where(wanted.astype(F32) == home, 1.0, 0.0)
    hit = jnp.concatenate([hit, jnp.zeros_like(hit)], axis=0).astype(BF16)
    out_ref[...] = tn_dot(hit, data).astype(BF16)


def home_kernel(parts_ref, feat_ref, near_ref):
    images, width = feat_ref.shape
    rows = jnp.sum(parts_ref[...].astype(F32), axis=0)
    feat_ref[...] = rows[:images, :width].astype(BF16)
    tail = rows[:, width:]
    near = tail[:, 0:1] + tail[:, 1:2] + tail[:, 2:3]
    eye = iota((SLOT, INTS), 0) == iota((SLOT, INTS), 1)
    near_ref[...] = jnp.sum(jnp.where(eye, near, 0.0), axis=0, keepdims=True)[:, :images]


def struct(shape, dtype):
    return jax.ShapeDtypeStruct(shape, dtype)


def cost(micros):
    return pl.CostEstimate(
        flops=int(micros * 1.15e9), bytes_accessed=int(micros * 3.69e6), transcendentals=0
    )


def whole(memory=pltpu.VMEM):
    return pl.BlockSpec(memory_space=memory)


def local(
    hidden,
    token_lengths,
    image_counts,
    cluster_ids,
    order_ranks,
    ln_gains,
    ln_biases,
    w_qkv,
    layer_biases,
    w_out,
    w_fc1,
    fc1_bias,
    w_fc2,
    w_proj,
):
    images, tokens, half = hidden.shape
    width = 2 * half
    embed = w_proj.shape[1]
    members = lax.axis_size("clus") * 2
    owners = lax.axis_size("dp")
    own_images = images // 2
    params = pltpu.CompilerParams(vmem_limit_bytes=24 * 1024 * 1024)
    swap = [(0, 1), (1, 0)]
    heads = images * PAD
    hbm = pl.BlockSpec(memory_space=pltpu.HBM)
    other = lax.ppermute(hidden, "tensor", swap)
    w_three = jnp.transpose(w_qkv, (1, 0, 2))
    table = pl.pallas_call(
        stats_kernel,
        out_shape=struct((2 * PAD, TABLE), F32),
        compiler_params=params,
        cost_estimate=cost(2.0),
    )(hidden)
    other_table = lax.ppermute(table, "tensor", swap)
    raw, sums, const, residual = pl.pallas_call(
        score_kernel,
        out_shape=(
            struct((heads, TABLE), F32),
            struct((heads, STAT), F32),
            struct((heads, STAT), F32),
            struct((PAD, width), F32),
        ),
        in_specs=[whole()] * 2 + [whole(pltpu.SMEM)] + [whole()] * 4,
        out_specs=[whole()] * 4,
        compiler_params=params,
        cost_estimate=cost(4.0),
    )(hidden, other, token_lengths, ln_gains, ln_biases, w_three, layer_biases)
    partial = pl.pallas_call(
        attend_kernel,
        out_shape=struct((PAD, width + embed), BF16),
        in_specs=[whole()] * 2 + [whole(pltpu.SMEM)] * 3 + [whole()] * 12,
        out_specs=whole(),
        scratch_shapes=[pltpu.VMEM((heads, width), BF16)],
        compiler_params=params,
        cost_estimate=cost(4.0),
    )(
        hidden,
        other,
        image_counts,
        cluster_ids,
        order_ranks,
        table,
        other_table,
        raw,
        sums,
        const,
        residual,
        ln_gains,
        ln_biases,
        layer_biases,
        w_three,
        w_out,
        w_proj,
    )
    rows = lax.all_gather(partial, MEMBERS, axis=0, tiled=True)
    sent, first, meta = pl.pallas_call(
        mlp_kernel,
        out_shape=(
            struct((members * SLOT, width), BF16),
            struct((SLOT, width), F32),
            struct((SLOT, INTS), F32),
        ),
        compiler_params=params,
        cost_estimate=cost(1.5),
    )(rows, ln_gains, ln_biases, layer_biases, w_fc1, fc1_bias.reshape(1, -1), w_fc2)
    parts = lax.all_to_all(
        sent.reshape(members, SLOT, width), MEMBERS, split_axis=0, concat_axis=0, tiled=True
    )
    clus = members // 2
    piece = pl.pallas_call(
        cut_kernel,
        out_shape=struct((clus, PAD, embed), BF16),
        compiler_params=params,
        cost_estimate=cost(0.5),
    )(rows, meta)
    flips = [[(i, i ^ flip) for i in range(owners)] for flip in (1, 4, 5)]
    send = pl.pallas_call(
        pool_kernel,
        out_shape=struct((owners, SLOT, width + INTS), BF16),
        compiler_params=params,
        cost_estimate=cost(0.5),
    )(parts, first, meta, ln_gains, ln_biases, layer_biases)
    proj = pl.pallas_call(
        join_kernel,
        out_shape=struct((clus, 4, PAD, embed), BF16),
        in_specs=[hbm] + [whole()] * 4,
        compiler_params=params,
        cost_estimate=cost(0.5),
    )(send, piece, *(lax.ppermute(piece, "dp", flip) for flip in flips))
    proj = pl.pallas_call(
        unpack_kernel,
        out_shape=struct((clus, 2, 4, PAD, embed), BF16),
        compiler_params=params,
        cost_estimate=cost(0.7),
    )(proj, lax.ppermute(proj, "tensor", swap))
    keys = lax.all_to_all(send, "dp", split_axis=0, concat_axis=0, tiled=True)
    back = pl.pallas_call(
        nearest_kernel,
        out_shape=struct((members * SLOT, embed + INTS), BF16),
        scratch_shapes=[pltpu.VMEM((owners * SLOT, embed), F32)],
        compiler_params=params,
        cost_estimate=cost(1.0),
    )(keys.reshape(owners * SLOT, width + INTS), meta, proj.reshape(width, embed))
    home = lax.all_to_all(
        back.reshape(members, SLOT, embed + INTS), MEMBERS, split_axis=0, concat_axis=0, tiled=True
    )
    features, nearest = pl.pallas_call(
        home_kernel,
        out_shape=(struct((own_images, embed), BF16), struct((1, own_images), F32)),
        compiler_params=params,
        cost_estimate=cost(0.5),
    )(home)
    return (features, nearest.reshape(own_images))


def solution(mesh):
    return jax.shard_map(
        local,
        mesh=mesh,
        in_specs=(
            P(("dp", "clus"), None, "tensor"),
            P(("dp", "clus")),
            P(("dp", "clus")),
            P(("dp", "clus", "tensor")),
            P(("dp", "clus", "tensor")),
            P(),
            P(),
            P(None, None, "tensor"),
            P(),
            P("tensor", None),
            P(None, ("clus", "tensor")),
            P(("clus", "tensor")),
            P(("clus", "tensor"), None),
            P(("clus", "tensor"), None),
        ),
        out_specs=(P(("dp", "clus", "tensor"), None), P(("dp", "clus", "tensor"))),
        check_vma=False,
    )
```

```python
import jax
import jax.numpy as jnp
from jax import lax
from jax.experimental import pallas as pl
from jax.experimental.pallas import tpu as pltpu
from jax.sharding import PartitionSpec as P

HEAD = 64
CLUS_DP = 4
SLOT = 8
PAD = 16
INTS = 128
STAT = 128
TABLE = 384
EPS = 1e-05
F32 = jnp.float32
BF16 = jnp.bfloat16
MEMBERS = ("clus", "tensor")


def iota(shape, axis):
    return lax.broadcasted_iota(jnp.int32, shape, axis)


def quarter_of(dp, flip):
    x_bit, y_bit = dp % 2, dp // 4 % 2
    x_bit = 1 - x_bit if flip % 2 else x_bit
    y_bit = 1 - y_bit if flip // 4 else y_bit
    return 2 * y_bit + x_bit


def layer_norm(values, gain_row, shift_row):
    average = jnp.mean(values, axis=-1, keepdims=True)
    centered = values - average
    spread = jnp.mean(centered * centered, axis=-1, keepdims=True)
    return centered * lax.rsqrt(spread + EPS) * gain_row + shift_row


def as_column(row):
    size = row.shape[1]
    eye = iota((size, size), 0) == iota((size, size), 1)
    return jnp.sum(jnp.where(eye, row, 0.0), axis=1, keepdims=True)


def nt_dot(left, right):
    return lax.dot_general(left, right, (((1,), (1,)), ((), ())), preferred_element_type=F32)


def tn_dot(left, right):
    return lax.dot_general(left, right, (((0,), (0,)), ((), ())), preferred_element_type=F32)


def stats_kernel(hidden_ref, own_ref, table_ref, sem):
    images, tokens, half = own_ref.shape
    block = images // sem.shape[0]
    copies = [
        pltpu.make_async_copy(
            hidden_ref.at[pl.ds(c * block, block)], own_ref.at[pl.ds(c * block, block)], sem.at[c]
        )
        for c in range(sem.shape[0])
    ]
    for copy in copies:
        copy.start()
    rows, lane = TABLE, iota((tokens, STAT), 1)
    table = jnp.zeros((tokens, STAT), F32)
    for i in range(images):
        if i % block == 0:
            copies[i // block].wait()
        states = own_ref[i].astype(F32)
        total = jnp.sum(states, axis=1, keepdims=True)
        centered = states - total * (1.0 / half)
        spread = jnp.sum(centered * centered, axis=1, keepdims=True)
        table = jnp.where(lane == i, total, table)
        table = jnp.where(lane == PAD + i, spread, table)
    table = jnp.concatenate([table, jnp.zeros((rows - tokens, STAT), F32)], axis=0)
    table_ref[: 2 * PAD, :rows] = jnp.transpose(table)[: 2 * PAD]
    table_ref[2 * PAD : 2 * PAD + images, :] = own_ref[:, 0, :].astype(F32)


def moments(own_table_ref, other_table_ref, images, width):
    left, right = own_table_ref[: 2 * PAD, :TABLE], other_table_ref[: 2 * PAD, :TABLE]
    half = width // 2
    mean = (left[:images] + right[:images]) * (1.0 / width)
    apart = (left[:images] - right[:images]) * (1.0 / half)
    spread = left[PAD : PAD + images] + right[PAD : PAD + images] + apart * apart * (half / 2)
    return mean, lax.rsqrt(spread * (1.0 / width) + EPS)


def over_heads(rows, tokens):
    images, lanes = rows.shape
    wide = jnp.broadcast_to(rows[:, None, :], (images, PAD, lanes))
    return wide.reshape(images * PAD, lanes)[:, :tokens]


def score_kernel(
    own_ref,
    lengths_ref,
    own_table_ref,
    other_table_ref,
    gains_ref,
    shifts_ref,
    w_ref,
    biases_ref,
    probe_ref,
    scores_ref,
    first_ref,
):
    images, tokens, half = own_ref.shape
    width = 2 * half
    tensor = lax.axis_index("tensor")
    own_first = own_table_ref[2 * PAD : 2 * PAD + images, :]
    other_first = other_table_ref[2 * PAD : 2 * PAD + images, :]
    first = jnp.concatenate(
        [
            jnp.where(tensor == 0, own_first, other_first),
            jnp.where(tensor == 0, other_first, own_first),
        ],
        axis=1,
    )
    first_ref[:images, :] = first
    first_ref[images:, :] = jnp.zeros((PAD - images, width), F32)
    normed = layer_norm(first, gains_ref[0:1, :], shifts_ref[0:1, :]).astype(BF16)
    start = pl.multiple_of(tensor * half, half)
    query = jnp.dot(normed, w_ref[0], preferred_element_type=F32)
    query = (query + biases_ref[0:1, pl.ds(start, half)]) * HEAD ** (-0.5)
    query = query.astype(BF16).astype(F32)
    mask = iota((PAD, half), 0) == iota((PAD, half), 1) // HEAD
    spread = jnp.where(mask[None], query[:, None, :], 0.0).reshape(images * PAD, half).astype(BF16)
    probe = nt_dot(spread, w_ref[1])
    const = jnp.sum(probe * shifts_ref[0:1, :], axis=1, keepdims=True)
    probe = (probe * gains_ref[0:1, :]).astype(BF16)
    sums = jnp.sum(probe.astype(F32), axis=1, keepdims=True)
    own_probe = jnp.where(tensor == 0, probe[:, :half], probe[:, half:])
    probe_ref[...] = jnp.where(tensor == 0, probe[:, half:], probe[:, :half])
    mean, scale = moments(own_table_ref, other_table_ref, images, width)
    lane = iota((PAD, tokens), 1)
    for i in range(images):
        heads = slice(i * PAD, (i + 1) * PAD)
        scores = nt_dot(own_probe[heads], own_ref[i]) - sums[heads] * mean[i : i + 1, :tokens]
        scores = scores * scale[i : i + 1, :tokens] + const[heads]
        scores_ref[heads, :tokens] = jnp.where(lane < lengths_ref[i], scores, -1e30)


def attend_kernel(
    own_ref,
    other_ref,
    counts_ref,
    clusters_ref,
    ranks_ref,
    own_table_ref,
    other_table_ref,
    probe_ref,
    scores_ref,
    first_ref,
    gains_ref,
    shifts_ref,
    biases_ref,
    w_ref,
    w_out_ref,
    w_proj_ref,
    out_ref,
    raw_ref,
    mixed_ref,
):
    images, tokens, half = own_ref.shape
    width = 2 * half
    tensor = lax.axis_index("tensor")
    clus = lax.axis_index("clus")
    own_start = pl.multiple_of(tensor * half, half)
    other_start = pl.multiple_of((1 - tensor) * half, half)
    for i in range(images):
        heads = slice(i * PAD, (i + 1) * PAD)
        raw_ref[heads, :tokens] = nt_dot(probe_ref[heads], other_ref[i])
    mean, scale = (
        over_heads(rows, tokens)
        for rows in moments(own_table_ref, other_table_ref, images, width)
    )
    scores = scores_ref[:, :tokens] + raw_ref[:, :tokens] * scale
    exponent = jnp.exp(scores - jnp.max(scores, axis=1, keepdims=True))
    weights = exponent * (1.0 / jnp.sum(exponent, axis=1, keepdims=True))
    part = (weights * scale).astype(BF16)
    offset = jnp.sum(part.astype(F32) * mean, axis=1, keepdims=True)
    for ref, start in ((own_ref, own_start), (other_ref, other_start)):
        gain, shift = gains_ref[0:1, pl.ds(start, half)], shifts_ref[0:1, pl.ds(start, half)]
        for i in range(images):
            heads = slice(i * PAD, (i + 1) * PAD)
            summed = jnp.dot(part[heads], ref[i], preferred_element_type=F32) - offset[heads]
            mixed_ref[heads, pl.ds(start, half)] = (summed * gain + shift).astype(BF16)
    context = jnp.dot(mixed_ref[...], w_ref[2], preferred_element_type=F32)
    mask = iota((PAD, half), 0) == iota((PAD, half), 1) // HEAD
    context = jnp.sum(jnp.where(mask[None], context.reshape(images, PAD, half), 0.0), axis=1)
    context = context + biases_ref[1:2, pl.ds(own_start, half)]
    fill = jnp.zeros((PAD - images, half), F32)
    context = jnp.concatenate([context, fill], axis=0).astype(BF16)
    out = jnp.dot(context, w_out_ref[...], preferred_element_type=F32)
    extra = jnp.where(tensor == 0, first_ref[...], 0.0)
    row, lane = iota((PAD, width), 0), iota((PAD, width), 1)
    own_images = images // 2
    for j in range(own_images):
        place = tensor * own_images + j
        hit = (lane // (2 * PAD) == clus) & (lane % PAD == place)
        cluster, rank = clusters_ref[j], ranks_ref[j]
        alive = (place < counts_ref[0]).astype(jnp.int32)
        for k, value in enumerate((cluster, rank // 64, rank % 64, alive)):
            extra = jnp.where(hit & (row == images + k), value.astype(F32), extra)
    out_ref[:, :width] = (out + extra).astype(BF16)
    piece = pl.multiple_of(quarter_of(lax.axis_index("dp"), 0) * PAD, PAD)
    out_ref[:, width:] = w_proj_ref[pl.ds(piece, PAD), :]


def cut_kernel(rows_ref, meta_ref, out_ref):
    clus, rows, embed = out_ref.shape
    tensor = lax.axis_index("tensor")
    width = rows_ref.shape[1] - embed
    for c in range(clus):
        start = pl.multiple_of((2 * c + tensor) * rows, rows)
        out_ref[c] = rows_ref[pl.ds(start, rows), width:]


def join_kernel(after_ref, own_ref, near_ref, far_ref, cross_ref, out_ref):
    dp = lax.axis_index("dp")
    for ref, flip in ((own_ref, 0), (near_ref, 1), (far_ref, 4), (cross_ref, 5)):
        out_ref[:, quarter_of(dp, flip)] = ref[...]


def unpack_kernel(own_ref, other_ref, out_ref):
    tensor = lax.axis_index("tensor")
    out_ref[:, tensor] = own_ref[...]
    out_ref[:, 1 - tensor] = other_ref[...]


def mlp_kernel(
    rows_ref,
    gains_ref,
    shifts_ref,
    biases_ref,
    w1_ref,
    b1_ref,
    w2_ref,
    out_ref,
    first_ref,
    meta_ref,
):
    total, width = rows_ref.shape[0], w1_ref.shape[0]
    images = PAD - 4
    members = total // PAD
    member = lax.axis_index("clus") * 2 + lax.axis_index("tensor")
    rows = rows_ref[:, :width]
    ints = jnp.sum(rows[:, :total].astype(F32).reshape(members, PAD, total), axis=0)
    cluster, rank_high, rank_low, alive = (ints[images + k : images + k + 1] for k in range(4))
    owner = jnp.floor(cluster * (1.0 / CLUS_DP))
    lane = iota((1, total), 1)
    valid = lane % PAD < images
    place = lane - (lane & PAD)
    before = iota((total, total), 0)
    earlier = (
        (as_column(owner) == owner) & (before % (2 * PAD) < images) & (before < place)
    )
    slot = jnp.sum(jnp.where(earlier, 1.0, 0.0), axis=0, keepdims=True)
    target = jnp.where(valid, owner * SLOT + slot, -1.0)
    slots = members * SLOT
    chosen = jnp.where(iota((slots, total), 0).astype(F32) == target, 1.0, 0.0).astype(BF16)
    first = jnp.dot(chosen, rows, preferred_element_type=F32) + biases_ref[2:3, :]
    mixed = layer_norm(first, gains_ref[1:2, :], shifts_ref[1:2, :]).astype(BF16)
    inner = jnp.dot(mixed, w1_ref[...], preferred_element_type=F32) + b1_ref[...]
    inner = (inner * jax.nn.sigmoid(1.702 * inner)).astype(BF16)
    out_ref[...] = jnp.dot(inner, w2_ref[...], preferred_element_type=F32).astype(BF16)
    mine = (iota((PAD, total), 0) + member * SLOT).astype(F32) == target
    mine = mine & (iota((PAD, total), 0) < SLOT)
    picked = jnp.dot(
        jnp.where(mine, 1.0, 0.0).astype(BF16), rows, preferred_element_type=F32
    )
    first_ref[...] = picked[:SLOT] + biases_ref[2:3, :]
    single = (mine & (lane % (2 * PAD) < PAD))[:SLOT]
    home = ((lane // (2 * PAD)) * images + lane % PAD + 1).astype(F32)
    meta = jnp.zeros((SLOT, INTS), F32)
    for k, value in enumerate((cluster, rank_high, rank_low, alive, home)):
        column = jnp.sum(jnp.where(single, value, 0.0), axis=1, keepdims=True)
        meta = jnp.where(iota((SLOT, INTS), 1) == k, column, meta)
    meta_ref[...] = meta


def pool_kernel(parts_ref, first_ref, meta_ref, gains_ref, shifts_ref, biases_ref, send_ref):
    second = jnp.sum(parts_ref[...].astype(F32), axis=0) + first_ref[...] + biases_ref[3:4, :]
    pooled = layer_norm(second, gains_ref[2:3, :], shifts_ref[2:3, :])
    sub, lane = iota((SLOT, INTS), 0), iota((SLOT, INTS), 1)
    ints = jnp.zeros((SLOT, INTS), F32)
    for k in range(4):
        ints = jnp.where(lane == k * SLOT + sub, meta_ref[:, k : k + 1], ints)
    ints = jnp.sum(ints, axis=0, keepdims=True)
    fill = jnp.zeros((1, pooled.shape[1] - INTS), F32)
    last = iota(pooled.shape, 0) == SLOT - 1
    row = jnp.where(last, jnp.concatenate([ints, fill], axis=1), pooled).astype(BF16)
    send_ref[...] = jnp.broadcast_to(row[None], send_ref.shape)


def unit(features):
    norm = jnp.sum(features * features, axis=-1, keepdims=True)
    return (features * lax.rsqrt(norm + 1e-06)).astype(BF16)


def nearest_kernel(keys_ref, meta_ref, w_ref, out_ref, features_ref):
    total = keys_ref.shape[0]
    keys = keys_ref[...]
    features = jnp.dot(keys, w_ref[...], preferred_element_type=F32)
    features_ref[...] = features.astype(BF16).astype(F32)
    mine = pl.multiple_of(lax.axis_index("dp") * SLOT, SLOT)
    key_units = unit(features_ref[...])
    features = features_ref[pl.ds(mine, SLOT), :]
    similar = nt_dot(unit(features), key_units)
    owners = total // SLOT
    last = iota((owners, total), 1) == iota((owners, total), 0) * SLOT + SLOT - 1
    ints = jnp.dot(
        jnp.where(last, 1.0, 0.0).astype(BF16), keys[:, :INTS], preferred_element_type=F32
    ).astype(BF16)
    place = iota((INTS, total), 1) % SLOT
    block = iota((owners, total), 1) // SLOT == iota((owners, total), 0)
    key_ints = []
    for k in range(4):
        spread = jnp.where(iota((INTS, total), 0) == place + k * SLOT, 1.0, 0.0).astype(BF16)
        rows = jnp.dot(ints, spread, preferred_element_type=F32)
        key_ints.append(jnp.sum(jnp.where(block, rows, 0.0), axis=0, keepdims=True))
    lane = iota((SLOT, INTS), 1)
    cluster, rank_high, rank_low, alive, home = (
        jnp.sum(jnp.where(lane == k, meta_ref[...], 0.0), axis=1, keepdims=True) for k in range(5)
    )
    key_rank = key_ints[1] * 64.0 + key_ints[2]
    allowed = (
        (key_ints[3] > 0.5)
        & (key_ints[0] == cluster)
        & (key_rank < rank_high * 64.0 + rank_low)
    )
    best = jnp.max(jnp.where(allowed, similar, -2.0), axis=1, keepdims=True)
    best = jnp.where(alive > 0.5, jnp.maximum(best, -1.0), -1.0)
    high = best.astype(BF16).astype(F32)
    middle = (best - high).astype(BF16).astype(F32)
    low = best - high - middle
    own_images = (PAD - 4) // 2
    block = jnp.floor((home - 0.5) * (1.0 / own_images))
    place = home - 1.0 - block * own_images
    tail = jnp.zeros((SLOT, INTS), F32)
    for k, value in enumerate((high, middle, low)):
        tail = jnp.where(lane.astype(F32) == place + k * SLOT, value, tail)
    fill = jnp.zeros((SLOT, features.shape[1] - INTS), F32)
    tail = jnp.concatenate([tail, fill], axis=1)
    data = jnp.concatenate([features, tail], axis=0).astype(BF16)
    slots = out_ref.shape[0]
    code = iota((SLOT, slots), 1)
    target, line = (code // SLOT).astype(F32), (code % SLOT).astype(F32)
    here = target == block
    hit = jnp.concatenate(
        [
            jnp.where(here & (line == place), 1.0, 0.0),
            jnp.where(here & (line == SLOT - 1), 1.0, 0.0),
        ],
        axis=0,
    ).astype(BF16)
    out_ref[...] = tn_dot(hit, data).astype(BF16)


def home_kernel(parts_ref, feat_ref, near_ref):
    images = feat_ref.shape[0]
    rows = jnp.sum(parts_ref[...].astype(F32), axis=0)
    feat_ref[...] = rows[:images].astype(BF16)
    tail = rows[SLOT - 1 :, :INTS]
    high, middle, low = (tail[:, k * SLOT : k * SLOT + images] for k in range(3))
    near_ref[...] = high + middle + low


def struct(shape, dtype):
    return jax.ShapeDtypeStruct(shape, dtype)


def cost(micros):
    return pl.CostEstimate(
        flops=int(micros * 1.15e9), bytes_accessed=int(micros * 3.69e6), transcendentals=0
    )


def whole(memory=pltpu.VMEM):
    return pl.BlockSpec(memory_space=memory)


def local(
    hidden,
    token_lengths,
    image_counts,
    cluster_ids,
    order_ranks,
    ln_gains,
    ln_biases,
    w_qkv,
    layer_biases,
    w_out,
    w_fc1,
    fc1_bias,
    w_fc2,
    w_proj,
):
    images, tokens, half = hidden.shape
    width = 2 * half
    embed = w_proj.shape[1]
    members = lax.axis_size("clus") * 2
    owners = lax.axis_size("dp")
    own_images = images // 2
    params = pltpu.CompilerParams(vmem_limit_bytes=24 * 1024 * 1024)
    greedy = pltpu.CompilerParams(vmem_limit_bytes=50 * 1024 * 1024)
    swap = [(0, 1), (1, 0)]
    heads = images * PAD
    hbm = pl.BlockSpec(memory_space=pltpu.HBM)
    other = lax.ppermute(hidden, "tensor", swap)
    w_three = jnp.transpose(w_qkv, (1, 0, 2))
    own, table = pl.pallas_call(
        stats_kernel,
        out_shape=(struct(hidden.shape, BF16), struct((3 * PAD, half), F32)),
        in_specs=[hbm],
        out_specs=[whole()] * 2,
        scratch_shapes=[pltpu.SemaphoreType.DMA((4,))],
        compiler_params=greedy,
        cost_estimate=cost(2.0),
    )(hidden)
    other_table = lax.ppermute(table, "tensor", swap)
    w_three = jnp.transpose(w_qkv, (1, 0, 2))
    probe, scores, residual = pl.pallas_call(
        score_kernel,
        out_shape=(
            struct((heads, half), BF16),
            struct((heads, TABLE), F32),
            struct((PAD, width), F32),
        ),
        in_specs=[whole(), whole(pltpu.SMEM)] + [whole()] * 6,
        out_specs=[whole()] * 3,
        compiler_params=params,
        cost_estimate=cost(2.4),
    )(own, token_lengths, table, other_table, ln_gains, ln_biases, w_three, layer_biases)
    partial = pl.pallas_call(
        attend_kernel,
        out_shape=struct((PAD, width + embed), BF16),
        in_specs=[whole()] * 2 + [whole(pltpu.SMEM)] * 3 + [whole()] * 11,
        out_specs=whole(),
        scratch_shapes=[pltpu.VMEM((heads, TABLE), F32), pltpu.VMEM((heads, width), BF16)],
        compiler_params=params,
        cost_estimate=cost(4.0),
    )(
        own,
        other,
        image_counts,
        cluster_ids,
        order_ranks,
        table,
        other_table,
        probe,
        scores,
        residual,
        ln_gains,
        ln_biases,
        layer_biases,
        w_three,
        w_out,
        w_proj,
    )
    rows = lax.all_gather(partial, MEMBERS, axis=0, tiled=True)
    sent, first, meta = pl.pallas_call(
        mlp_kernel,
        out_shape=(
            struct((members * SLOT, width), BF16),
            struct((SLOT, width), F32),
            struct((SLOT, INTS), F32),
        ),
        compiler_params=params,
        cost_estimate=cost(1.5),
    )(rows, ln_gains, ln_biases, layer_biases, w_fc1, fc1_bias.reshape(1, -1), w_fc2)
    parts = lax.all_to_all(
        sent.reshape(members, SLOT, width), MEMBERS, split_axis=0, concat_axis=0, tiled=True
    )
    clus = members // 2
    piece = pl.pallas_call(
        cut_kernel,
        out_shape=struct((clus, PAD, embed), BF16),
        compiler_params=params,
        cost_estimate=cost(0.5),
    )(rows, meta)
    flips = [[(i, i ^ flip) for i in range(owners)] for flip in (1, 4, 5)]
    send = pl.pallas_call(
        pool_kernel,
        out_shape=struct((owners, SLOT, width), BF16),
        compiler_params=params,
        cost_estimate=cost(0.5),
    )(parts, first, meta, ln_gains, ln_biases, layer_biases)
    proj = pl.pallas_call(
        join_kernel,
        out_shape=struct((clus, 4, PAD, embed), BF16),
        in_specs=[hbm] + [whole()] * 4,
        compiler_params=params,
        cost_estimate=cost(0.5),
    )(send, piece, *(lax.ppermute(piece, "dp", flip) for flip in flips))
    proj = pl.pallas_call(
        unpack_kernel,
        out_shape=struct((clus, 2, 4, PAD, embed), BF16),
        compiler_params=params,
        cost_estimate=cost(0.7),
    )(proj, lax.ppermute(proj, "tensor", swap))
    keys = lax.all_to_all(send, "dp", split_axis=0, concat_axis=0, tiled=True)
    back = pl.pallas_call(
        nearest_kernel,
        out_shape=struct((members * SLOT, embed), BF16),
        scratch_shapes=[pltpu.VMEM((owners * SLOT, embed), F32)],
        compiler_params=params,
        cost_estimate=cost(1.0),
    )(keys.reshape(owners * SLOT, width), meta, proj.reshape(width, embed))
    home = lax.all_to_all(
        back.reshape(members, SLOT, embed), MEMBERS, split_axis=0, concat_axis=0, tiled=True
    )
    features, nearest = pl.pallas_call(
        home_kernel,
        out_shape=(struct((own_images, embed), BF16), struct((1, own_images), F32)),
        compiler_params=params,
        cost_estimate=cost(0.5),
    )(home)
    return (features, nearest.reshape(own_images))


def solution(mesh):
    return jax.shard_map(
        local,
        mesh=mesh,
        in_specs=(
            P(("dp", "clus"), None, "tensor"),
            P(("dp", "clus")),
            P(("dp", "clus")),
            P(("dp", "clus", "tensor")),
            P(("dp", "clus", "tensor")),
            P(),
            P(),
            P(None, None, "tensor"),
            P(),
            P("tensor", None),
            P(None, ("clus", "tensor")),
            P(("clus", "tensor")),
            P(("clus", "tensor"), None),
            P(("clus", "tensor"), None),
        ),
        out_specs=(P(("dp", "clus", "tensor"), None), P(("dp", "clus", "tensor"))),
        check_vma=False,
    )
```

```python
import jax
import jax.numpy as jnp
from jax import lax
from jax.experimental import pallas as pl
from jax.experimental.pallas import tpu as pltpu
from jax.sharding import PartitionSpec as P

HEAD = 64
CLUS_DP = 4
SLOT = 8
PAD = 16
INTS = 128
STAT = 128
TABLE = 384
FLIPS = (1, 4, 5)
EPS = 1e-05
F32 = jnp.float32
BF16 = jnp.bfloat16
MEMBERS = ("clus", "tensor")


def iota(shape, axis):
    return lax.broadcasted_iota(jnp.int32, shape, axis)


def quarter_of(dp, flip):
    x_bit, y_bit = dp % 2, dp // 4 % 2
    x_bit = 1 - x_bit if flip % 2 else x_bit
    y_bit = 1 - y_bit if flip // 4 else y_bit
    return 2 * y_bit + x_bit


def layer_norm(values, gain_row, shift_row):
    average = jnp.mean(values, axis=-1, keepdims=True)
    centered = values - average
    spread = jnp.mean(centered * centered, axis=-1, keepdims=True)
    return centered * lax.rsqrt(spread + EPS) * gain_row + shift_row


def as_column(row):
    size = row.shape[1]
    eye = iota((size, size), 0) == iota((size, size), 1)
    return jnp.sum(jnp.where(eye, row, 0.0), axis=1, keepdims=True)


def nt_dot(left, right):
    return lax.dot_general(left, right, (((1,), (1,)), ((), ())), preferred_element_type=F32)


def tn_dot(left, right):
    return lax.dot_general(left, right, (((0,), (0,)), ((), ())), preferred_element_type=F32)


def stats_kernel(hidden_ref, own_ref, table_ref, sem):
    images, tokens, half = own_ref.shape
    block = images // sem.shape[0]
    copies = [
        pltpu.make_async_copy(
            hidden_ref.at[pl.ds(c * block, block)], own_ref.at[pl.ds(c * block, block)], sem.at[c]
        )
        for c in range(sem.shape[0])
    ]
    for copy in copies:
        copy.start()
    rows, lane = TABLE, iota((tokens, STAT), 1)
    table = jnp.zeros((tokens, STAT), F32)
    for i in range(images):
        if i % block == 0:
            copies[i // block].wait()
        states = own_ref[i].astype(F32)
        total = jnp.sum(states, axis=1, keepdims=True)
        centered = states - total * (1.0 / half)
        spread = jnp.sum(centered * centered, axis=1, keepdims=True)
        table = jnp.where(lane == i, total, table)
        table = jnp.where(lane == PAD + i, spread, table)
    table = jnp.concatenate([table, jnp.zeros((rows - tokens, STAT), F32)], axis=0)
    table_ref[: 2 * PAD, :rows] = jnp.transpose(table)[: 2 * PAD]
    table_ref[2 * PAD : 2 * PAD + images, :] = own_ref[:, 0, :].astype(F32)


def moments(own_table_ref, other_table_ref, images, width):
    left, right = own_table_ref[: 2 * PAD, :TABLE], other_table_ref[: 2 * PAD, :TABLE]
    half = width // 2
    mean = (left[:images] + right[:images]) * (1.0 / width)
    apart = (left[:images] - right[:images]) * (1.0 / half)
    spread = left[PAD : PAD + images] + right[PAD : PAD + images] + apart * apart * (half / 2)
    return mean, lax.rsqrt(spread * (1.0 / width) + EPS)


def over_heads(rows, tokens):
    images, lanes = rows.shape
    wide = jnp.broadcast_to(rows[:, None, :], (images, PAD, lanes))
    return wide.reshape(images * PAD, lanes)[:, :tokens]


def score_kernel(
    own_ref,
    lengths_ref,
    own_table_ref,
    other_table_ref,
    gains_ref,
    shifts_ref,
    w_ref,
    biases_ref,
    probe_ref,
    scores_ref,
    first_ref,
):
    images, tokens, half = own_ref.shape
    width = 2 * half
    tensor = lax.axis_index("tensor")
    own_first = own_table_ref[2 * PAD : 2 * PAD + images, :]
    other_first = other_table_ref[2 * PAD : 2 * PAD + images, :]
    first = jnp.concatenate(
        [
            jnp.where(tensor == 0, own_first, other_first),
            jnp.where(tensor == 0, other_first, own_first),
        ],
        axis=1,
    )
    first_ref[:images, :] = first
    first_ref[images:, :] = jnp.zeros((PAD - images, width), F32)
    normed = layer_norm(first, gains_ref[0:1, :], shifts_ref[0:1, :]).astype(BF16)
    start = pl.multiple_of(tensor * half, half)
    query = jnp.dot(normed, w_ref[0], preferred_element_type=F32)
    query = (query + biases_ref[0:1, pl.ds(start, half)]) * HEAD ** (-0.5)
    query = query.astype(BF16).astype(F32)
    mask = iota((PAD, half), 0) == iota((PAD, half), 1) // HEAD
    spread = jnp.where(mask[None], query[:, None, :], 0.0).reshape(images * PAD, half).astype(BF16)
    probe = nt_dot(spread, w_ref[1])
    const = jnp.sum(probe * shifts_ref[0:1, :], axis=1, keepdims=True)
    probe = (probe * gains_ref[0:1, :]).astype(BF16)
    sums = jnp.sum(probe.astype(F32), axis=1, keepdims=True)
    own_probe = jnp.where(tensor == 0, probe[:, :half], probe[:, half:])
    probe_ref[...] = jnp.where(tensor == 0, probe[:, half:], probe[:, :half])
    mean, scale = moments(own_table_ref, other_table_ref, images, width)
    lane = iota((PAD, tokens), 1)
    for i in range(images):
        heads = slice(i * PAD, (i + 1) * PAD)
        scores = nt_dot(own_probe[heads], own_ref[i]) - sums[heads] * mean[i : i + 1, :tokens]
        scores = scores * scale[i : i + 1, :tokens] + const[heads]
        scores_ref[heads, :tokens] = jnp.where(lane < lengths_ref[i], scores, -1e30)


def attend_kernel(
    own_ref,
    other_ref,
    counts_ref,
    clusters_ref,
    ranks_ref,
    own_table_ref,
    other_table_ref,
    probe_ref,
    scores_ref,
    first_ref,
    gains_ref,
    shifts_ref,
    biases_ref,
    w_ref,
    w_out_ref,
    w_proj_ref,
    out_ref,
    raw_ref,
    mixed_ref,
):
    images, tokens, half = own_ref.shape
    width = 2 * half
    tensor = lax.axis_index("tensor")
    clus = lax.axis_index("clus")
    own_start = pl.multiple_of(tensor * half, half)
    other_start = pl.multiple_of((1 - tensor) * half, half)
    for i in range(images):
        heads = slice(i * PAD, (i + 1) * PAD)
        raw_ref[heads, :tokens] = nt_dot(probe_ref[heads], other_ref[i])
    mean, scale = (
        over_heads(rows, tokens)
        for rows in moments(own_table_ref, other_table_ref, images, width)
    )
    scores = scores_ref[:, :tokens] + raw_ref[:, :tokens] * scale
    exponent = jnp.exp(scores - jnp.max(scores, axis=1, keepdims=True))
    weights = exponent * (1.0 / jnp.sum(exponent, axis=1, keepdims=True))
    part = (weights * scale).astype(BF16)
    offset = jnp.sum(part.astype(F32) * mean, axis=1, keepdims=True)
    for ref, start in ((own_ref, own_start), (other_ref, other_start)):
        gain, shift = gains_ref[0:1, pl.ds(start, half)], shifts_ref[0:1, pl.ds(start, half)]
        for i in range(images):
            heads = slice(i * PAD, (i + 1) * PAD)
            summed = jnp.dot(part[heads], ref[i], preferred_element_type=F32) - offset[heads]
            mixed_ref[heads, pl.ds(start, half)] = (summed * gain + shift).astype(BF16)
    context = jnp.dot(mixed_ref[...], w_ref[2], preferred_element_type=F32)
    mask = iota((PAD, half), 0) == iota((PAD, half), 1) // HEAD
    context = jnp.sum(jnp.where(mask[None], context.reshape(images, PAD, half), 0.0), axis=1)
    context = context + biases_ref[1:2, pl.ds(own_start, half)]
    fill = jnp.zeros((PAD - images, half), F32)
    context = jnp.concatenate([context, fill], axis=0).astype(BF16)
    out = jnp.dot(context, w_out_ref[...], preferred_element_type=F32)
    extra = jnp.where(tensor == 0, first_ref[...], 0.0)
    row, lane = iota((PAD, width), 0), iota((PAD, width), 1)
    own_images = images // 2
    for j in range(own_images):
        place = tensor * own_images + j
        hit = (lane // PAD == clus) & (lane % PAD == place)
        cluster, rank = clusters_ref[j], ranks_ref[j]
        alive = (place < counts_ref[0]).astype(jnp.int32)
        for k, value in enumerate((cluster, rank // 64, rank % 64, alive)):
            extra = jnp.where(hit & (row == images + k), value.astype(F32), extra)
    out_ref[:, :width] = (out + extra).astype(BF16)
    piece = pl.multiple_of(quarter_of(lax.axis_index("dp"), 0) * PAD, PAD)
    out_ref[:, width:] = w_proj_ref[pl.ds(piece, PAD), :]


def cut_kernel(rows_ref, meta_ref, out_ref):
    clus, rows, embed = out_ref.shape
    tensor = lax.axis_index("tensor")
    width = rows_ref.shape[1] - embed
    for c in range(clus):
        start = pl.multiple_of((2 * c + tensor) * rows, rows)
        out_ref[c] = rows_ref[pl.ds(start, rows), width:]


def unpack_kernel(rows_ref, *refs):
    *piece_refs, out_ref = refs
    _, clus, rows, embed = piece_refs[0].shape
    width = rows_ref.shape[1] - embed
    dp = lax.axis_index("dp")
    own = rows_ref[:, width:].reshape(clus, 2, rows, embed)
    out_ref[:, :, quarter_of(dp, 0)] = own
    for piece_ref, flip in zip(piece_refs, FLIPS):
        for side in range(2):
            out_ref[:, side, quarter_of(dp, flip)] = piece_ref[side]


def mlp_kernel(
    rows_ref,
    gains_ref,
    shifts_ref,
    biases_ref,
    w1_ref,
    b1_ref,
    w2_ref,
    out_ref,
    first_ref,
    meta_ref,
):
    width, images = w1_ref.shape[0], PAD - 4
    members = rows_ref.shape[0] // PAD
    total = members // 2 * PAD
    member = lax.axis_index("clus") * 2 + lax.axis_index("tensor")
    halves = rows_ref[:, :width].reshape(members // 2, 2, PAD, width)
    halves = [halves[:, side].reshape(total, width) for side in range(2)]
    ints = jnp.sum(
        rows_ref[:, :total].astype(F32).reshape(members, PAD, total)[:, PAD // 2 :], axis=0
    )[images - PAD // 2 :]
    cluster, rank_high, rank_low, alive = (ints[k : k + 1] for k in range(4))
    owner = jnp.floor(cluster * (1.0 / CLUS_DP))
    lane = iota((1, total), 1)
    valid = lane % PAD < images
    before = iota((total, total), 0)
    earlier = (as_column(owner) == owner) & (before % PAD < images) & (before < lane)
    slot = jnp.sum(jnp.where(earlier, 1.0, 0.0), axis=0, keepdims=True)
    target = jnp.where(valid, owner * SLOT + slot, -1.0)
    slots = members * SLOT
    chosen = jnp.where(iota((slots, total), 0).astype(F32) == target, 1.0, 0.0).astype(BF16)
    first = sum(jnp.dot(chosen, half, preferred_element_type=F32) for half in halves)
    first = first + biases_ref[2:3, :]
    mixed = layer_norm(first, gains_ref[1:2, :], shifts_ref[1:2, :]).astype(BF16)
    inner = jnp.dot(mixed, w1_ref[...], preferred_element_type=F32) + b1_ref[...]
    inner = (inner * jax.nn.sigmoid(1.702 * inner)).astype(BF16)
    out_ref[...] = jnp.dot(inner, w2_ref[...], preferred_element_type=F32).astype(BF16)
    mine = (iota((PAD, total), 0) + member * SLOT).astype(F32) == target
    mine = mine & (iota((PAD, total), 0) < SLOT)
    mine_rows = jnp.where(mine, 1.0, 0.0).astype(BF16)
    picked = sum(jnp.dot(mine_rows, half, preferred_element_type=F32) for half in halves)
    first_ref[...] = picked[:SLOT] + biases_ref[2:3, :]
    single = mine[:SLOT]
    home = ((lane // PAD) * images + lane % PAD + 1).astype(F32)
    meta = jnp.zeros((SLOT, INTS), F32)
    for k, value in enumerate((cluster, rank_high, rank_low, alive, home)):
        column = jnp.sum(jnp.where(single, value, 0.0), axis=1, keepdims=True)
        meta = jnp.where(iota((SLOT, INTS), 1) == k, column, meta)
    meta_ref[...] = meta


def pool_kernel(parts_ref, first_ref, meta_ref, gains_ref, shifts_ref, biases_ref, send_ref):
    second = jnp.sum(parts_ref[...].astype(F32), axis=0) + first_ref[...] + biases_ref[3:4, :]
    pooled = layer_norm(second, gains_ref[2:3, :], shifts_ref[2:3, :])
    sub, lane = iota((SLOT, INTS), 0), iota((SLOT, INTS), 1)
    ints = jnp.zeros((SLOT, INTS), F32)
    for k in range(4):
        ints = jnp.where(lane == k * SLOT + sub, meta_ref[:, k : k + 1], ints)
    ints = jnp.sum(ints, axis=0, keepdims=True)
    fill = jnp.zeros((1, pooled.shape[1] - INTS), F32)
    last = iota(pooled.shape, 0) == SLOT - 1
    row = jnp.where(last, jnp.concatenate([ints, fill], axis=1), pooled).astype(BF16)
    send_ref[...] = jnp.broadcast_to(row[None], send_ref.shape)


def unit(features):
    norm = jnp.sum(features * features, axis=-1, keepdims=True)
    return (features * lax.rsqrt(norm + 1e-06)).astype(BF16)


def nearest_kernel(keys_ref, meta_ref, w_ref, out_ref, features_ref):
    total = keys_ref.shape[0]
    keys = keys_ref[...]
    features = jnp.dot(keys, w_ref[...], preferred_element_type=F32)
    features_ref[...] = features.astype(BF16).astype(F32)
    mine = pl.multiple_of(lax.axis_index("dp") * SLOT, SLOT)
    key_units = unit(features_ref[...])
    features = features_ref[pl.ds(mine, SLOT), :]
    similar = nt_dot(unit(features), key_units)
    owners = total // SLOT
    last = iota((owners, total), 1) == iota((owners, total), 0) * SLOT + SLOT - 1
    ints = jnp.dot(
        jnp.where(last, 1.0, 0.0).astype(BF16), keys[:, :INTS], preferred_element_type=F32
    ).astype(BF16)
    place = iota((INTS, total), 1) % SLOT
    block = iota((owners, total), 1) // SLOT == iota((owners, total), 0)
    key_ints = []
    for k in range(4):
        spread = jnp.where(iota((INTS, total), 0) == place + k * SLOT, 1.0, 0.0).astype(BF16)
        rows = jnp.dot(ints, spread, preferred_element_type=F32)
        key_ints.append(jnp.sum(jnp.where(block, rows, 0.0), axis=0, keepdims=True))
    lane = iota((SLOT, INTS), 1)
    cluster, rank_high, rank_low, alive, home = (
        jnp.sum(jnp.where(lane == k, meta_ref[...], 0.0), axis=1, keepdims=True) for k in range(5)
    )
    key_rank = key_ints[1] * 64.0 + key_ints[2]
    allowed = (
        (key_ints[3] > 0.5)
        & (key_ints[0] == cluster)
        & (key_rank < rank_high * 64.0 + rank_low)
    )
    best = jnp.max(jnp.where(allowed, similar, -2.0), axis=1, keepdims=True)
    best = jnp.where(alive > 0.5, jnp.maximum(best, -1.0), -1.0)
    high = best.astype(BF16).astype(F32)
    middle = (best - high).astype(BF16).astype(F32)
    low = best - high - middle
    own_images = (PAD - 4) // 2
    block = jnp.floor((home - 0.5) * (1.0 / own_images))
    place = home - 1.0 - block * own_images
    tail = jnp.zeros((SLOT, INTS), F32)
    for k, value in enumerate((high, middle, low)):
        tail = jnp.where(lane.astype(F32) == place + k * SLOT, value, tail)
    fill = jnp.zeros((SLOT, features.shape[1] - INTS), F32)
    tail = jnp.concatenate([tail, fill], axis=1)
    data = jnp.concatenate([features, tail], axis=0).astype(BF16)
    slots = out_ref.shape[0]
    code = iota((SLOT, slots), 1)
    target, line = (code // SLOT).astype(F32), (code % SLOT).astype(F32)
    here = target == block
    hit = jnp.concatenate(
        [
            jnp.where(here & (line == place), 1.0, 0.0),
            jnp.where(here & (line == SLOT - 1), 1.0, 0.0),
        ],
        axis=0,
    ).astype(BF16)
    out_ref[...] = tn_dot(hit, data).astype(BF16)


def home_kernel(parts_ref, feat_ref, near_ref):
    images = feat_ref.shape[0]
    rows = jnp.sum(parts_ref[...].astype(F32), axis=0)
    feat_ref[...] = rows[:images].astype(BF16)
    tail = rows[SLOT - 1 :, :INTS]
    high, middle, low = (tail[:, k * SLOT : k * SLOT + images] for k in range(3))
    near_ref[...] = high + middle + low


def struct(shape, dtype):
    return jax.ShapeDtypeStruct(shape, dtype)


def cost(micros):
    return pl.CostEstimate(
        flops=int(micros * 1.15e9), bytes_accessed=int(micros * 3.69e6), transcendentals=0
    )


def whole(memory=pltpu.VMEM):
    return pl.BlockSpec(memory_space=memory)


def local(
    hidden,
    token_lengths,
    image_counts,
    cluster_ids,
    order_ranks,
    ln_gains,
    ln_biases,
    w_qkv,
    layer_biases,
    w_out,
    w_fc1,
    fc1_bias,
    w_fc2,
    w_proj,
):
    images, tokens, half = hidden.shape
    width = 2 * half
    embed = w_proj.shape[1]
    members = lax.axis_size("clus") * 2
    owners = lax.axis_size("dp")
    own_images = images // 2
    params = pltpu.CompilerParams(vmem_limit_bytes=24 * 1024 * 1024)
    greedy = pltpu.CompilerParams(vmem_limit_bytes=50 * 1024 * 1024)
    swap = [(0, 1), (1, 0)]
    heads = images * PAD
    hbm = pl.BlockSpec(memory_space=pltpu.HBM)
    other = lax.ppermute(hidden, "tensor", swap)
    w_three = jnp.transpose(w_qkv, (1, 0, 2))
    own, table = pl.pallas_call(
        stats_kernel,
        out_shape=(struct(hidden.shape, BF16), struct((3 * PAD, half), F32)),
        in_specs=[hbm],
        out_specs=[whole()] * 2,
        scratch_shapes=[pltpu.SemaphoreType.DMA((4,))],
        compiler_params=greedy,
        cost_estimate=cost(2.0),
    )(hidden)
    other_table = lax.ppermute(table, "tensor", swap)
    w_three = jnp.transpose(w_qkv, (1, 0, 2))
    probe, scores, residual = pl.pallas_call(
        score_kernel,
        out_shape=(
            struct((heads, half), BF16),
            struct((heads, TABLE), F32),
            struct((PAD, width), F32),
        ),
        in_specs=[whole(), whole(pltpu.SMEM)] + [whole()] * 6,
        out_specs=[whole()] * 3,
        compiler_params=params,
        cost_estimate=cost(2.4),
    )(own, token_lengths, table, other_table, ln_gains, ln_biases, w_three, layer_biases)
    partial = pl.pallas_call(
        attend_kernel,
        out_shape=struct((PAD, width + embed), BF16),
        in_specs=[whole()] * 2 + [whole(pltpu.SMEM)] * 3 + [whole()] * 11,
        out_specs=whole(),
        scratch_shapes=[pltpu.VMEM((heads, TABLE), F32), pltpu.VMEM((heads, width), BF16)],
        compiler_params=params,
        cost_estimate=cost(4.0),
    )(
        own,
        other,
        image_counts,
        cluster_ids,
        order_ranks,
        table,
        other_table,
        probe,
        scores,
        residual,
        ln_gains,
        ln_biases,
        layer_biases,
        w_three,
        w_out,
        w_proj,
    )
    rows = lax.all_gather(partial, MEMBERS, axis=0, tiled=True)
    sent, first, meta = pl.pallas_call(
        mlp_kernel,
        out_shape=(
            struct((members * SLOT, width), BF16),
            struct((SLOT, width), F32),
            struct((SLOT, INTS), F32),
        ),
        compiler_params=params,
        cost_estimate=cost(1.5),
    )(rows, ln_gains, ln_biases, layer_biases, w_fc1, fc1_bias.reshape(1, -1), w_fc2)
    parts = lax.all_to_all(
        sent.reshape(members, SLOT, width), MEMBERS, split_axis=0, concat_axis=0, tiled=True
    )
    clus = members // 2
    piece = pl.pallas_call(
        cut_kernel,
        out_shape=struct((clus, PAD, embed), BF16),
        compiler_params=params,
        cost_estimate=cost(0.5),
    )(rows, meta)
    swaps = [[(i, i ^ flip) for i in range(owners)] for flip in FLIPS]
    pieces = [lax.ppermute(piece, "dp", pairs) for pairs in swaps]
    send = pl.pallas_call(
        pool_kernel,
        out_shape=struct((owners, SLOT, width), BF16),
        compiler_params=params,
        cost_estimate=cost(0.5),
    )(parts, first, meta, ln_gains, ln_biases, layer_biases)
    pieces = [lax.all_gather(piece, "tensor", axis=0, tiled=False) for piece in pieces]
    proj = pl.pallas_call(
        unpack_kernel,
        out_shape=struct((clus, 2, 4, PAD, embed), BF16),
        compiler_params=params,
        cost_estimate=cost(0.7),
    )(rows, *pieces)
    keys = lax.all_to_all(send, "dp", split_axis=0, concat_axis=0, tiled=True)
    back = pl.pallas_call(
        nearest_kernel,
        out_shape=struct((members * SLOT, embed), BF16),
        scratch_shapes=[pltpu.VMEM((owners * SLOT, embed), F32)],
        compiler_params=params,
        cost_estimate=cost(1.0),
    )(keys.reshape(owners * SLOT, width), meta, proj.reshape(width, embed))
    home = lax.all_to_all(
        back.reshape(members, SLOT, embed), MEMBERS, split_axis=0, concat_axis=0, tiled=True
    )
    features, nearest = pl.pallas_call(
        home_kernel,
        out_shape=(struct((own_images, embed), BF16), struct((1, own_images), F32)),
        compiler_params=params,
        cost_estimate=cost(0.5),
    )(home)
    return (features, nearest.reshape(own_images))


def solution(mesh):
    return jax.shard_map(
        local,
        mesh=mesh,
        in_specs=(
            P(("dp", "clus"), None, "tensor"),
            P(("dp", "clus")),
            P(("dp", "clus")),
            P(("dp", "clus", "tensor")),
            P(("dp", "clus", "tensor")),
            P(),
            P(),
            P(None, None, "tensor"),
            P(),
            P("tensor", None),
            P(None, ("clus", "tensor")),
            P(("clus", "tensor")),
            P(("clus", "tensor"), None),
            P(("clus", "tensor"), None),
        ),
        out_specs=(P(("dp", "clus", "tensor"), None), P(("dp", "clus", "tensor"))),
        check_vma=False,
    )
```

```python
import jax
import jax.numpy as jnp
from jax import lax
from jax.experimental import pallas as pl
from jax.experimental.pallas import tpu as pltpu
from jax.sharding import PartitionSpec as P

HEAD = 64
CLUS_DP = 4
SLOT = 8
PAD = 16
INTS = 128
STAT = 128
TABLE = 384
SIDE = 4
STEPS = (1, 2, 3)
EPS = 1e-05
F32 = jnp.float32
BF16 = jnp.bfloat16
MEMBERS = ("clus", "tensor")


def iota(shape, axis):
    return lax.broadcasted_iota(jnp.int32, shape, axis)


def quarter_of(dp, step):
    return (dp % SIDE + 2 * (dp // SIDE) + step) % 4


def neighbours(owners):
    pairs = {1: [], 2: [], 3: []}
    for dp in range(owners):
        x, y = dp % SIDE, dp // SIDE
        pairs[1].append((y * SIDE + (x + 1) % SIDE, dp))
        pairs[2].append(((y + 1) % SIDE * SIDE + x, dp))
        pairs[3].append((y * SIDE + (x + SIDE - 1) % SIDE, dp))
    return pairs


def layer_norm(values, gain_row, shift_row):
    average = jnp.mean(values, axis=-1, keepdims=True)
    centered = values - average
    spread = jnp.mean(centered * centered, axis=-1, keepdims=True)
    return centered * lax.rsqrt(spread + EPS) * gain_row + shift_row


def as_column(row):
    size = row.shape[1]
    eye = iota((size, size), 0) == iota((size, size), 1)
    return jnp.sum(jnp.where(eye, row, 0.0), axis=1, keepdims=True)


def nt_dot(left, right):
    return lax.dot_general(left, right, (((1,), (1,)), ((), ())), preferred_element_type=F32)


def tn_dot(left, right):
    return lax.dot_general(left, right, (((0,), (0,)), ((), ())), preferred_element_type=F32)


def stats_kernel(hidden_ref, own_ref, table_ref, sem):
    images, tokens, half = own_ref.shape
    block = images // sem.shape[0]
    copies = [
        pltpu.make_async_copy(
            hidden_ref.at[pl.ds(c * block, block)], own_ref.at[pl.ds(c * block, block)], sem.at[c]
        )
        for c in range(sem.shape[0])
    ]
    for copy in copies:
        copy.start()
    rows, lane = TABLE, iota((tokens, STAT), 1)
    table = jnp.zeros((tokens, STAT), F32)
    for i in range(images):
        if i % block == 0:
            copies[i // block].wait()
        states = own_ref[i].astype(F32)
        total = jnp.sum(states, axis=1, keepdims=True)
        centered = states - total * (1.0 / half)
        spread = jnp.sum(centered * centered, axis=1, keepdims=True)
        table = jnp.where(lane == i, total, table)
        table = jnp.where(lane == PAD + i, spread, table)
    table = jnp.concatenate([table, jnp.zeros((rows - tokens, STAT), F32)], axis=0)
    table_ref[: 2 * PAD, :rows] = jnp.transpose(table)[: 2 * PAD]
    table_ref[2 * PAD : 2 * PAD + images, :] = own_ref[:, 0, :].astype(F32)


def moments(own_table_ref, other_table_ref, images, width):
    left, right = own_table_ref[: 2 * PAD, :TABLE], other_table_ref[: 2 * PAD, :TABLE]
    half = width // 2
    mean = (left[:images] + right[:images]) * (1.0 / width)
    apart = (left[:images] - right[:images]) * (1.0 / half)
    spread = left[PAD : PAD + images] + right[PAD : PAD + images] + apart * apart * (half / 2)
    return mean, lax.rsqrt(spread * (1.0 / width) + EPS)


def over_heads(rows, tokens):
    images, lanes = rows.shape
    wide = jnp.broadcast_to(rows[:, None, :], (images, PAD, lanes))
    return wide.reshape(images * PAD, lanes)[:, :tokens]


def score_kernel(
    own_ref,
    lengths_ref,
    own_table_ref,
    other_table_ref,
    gains_ref,
    shifts_ref,
    w_ref,
    biases_ref,
    probe_ref,
    scores_ref,
    first_ref,
):
    images, tokens, half = own_ref.shape
    width = 2 * half
    tensor = lax.axis_index("tensor")
    own_first = own_table_ref[2 * PAD : 2 * PAD + images, :]
    other_first = other_table_ref[2 * PAD : 2 * PAD + images, :]
    first = jnp.concatenate(
        [
            jnp.where(tensor == 0, own_first, other_first),
            jnp.where(tensor == 0, other_first, own_first),
        ],
        axis=1,
    )
    first_ref[:images, :] = first
    first_ref[images:, :] = jnp.zeros((PAD - images, width), F32)
    normed = layer_norm(first, gains_ref[0:1, :], shifts_ref[0:1, :]).astype(BF16)
    start = pl.multiple_of(tensor * half, half)
    query = jnp.dot(normed, w_ref[0], preferred_element_type=F32)
    query = (query + biases_ref[0:1, pl.ds(start, half)]) * HEAD ** (-0.5)
    query = query.astype(BF16).astype(F32)
    mask = iota((PAD, half), 0) == iota((PAD, half), 1) // HEAD
    spread = jnp.where(mask[None], query[:, None, :], 0.0).reshape(images * PAD, half).astype(BF16)
    probe = nt_dot(spread, w_ref[1])
    const = jnp.sum(probe * shifts_ref[0:1, :], axis=1, keepdims=True)
    probe = (probe * gains_ref[0:1, :]).astype(BF16)
    sums = jnp.sum(probe.astype(F32), axis=1, keepdims=True)
    own_probe = jnp.where(tensor == 0, probe[:, :half], probe[:, half:])
    probe_ref[...] = jnp.where(tensor == 0, probe[:, half:], probe[:, :half])
    mean, scale = moments(own_table_ref, other_table_ref, images, width)
    lane = iota((PAD, tokens), 1)
    for i in range(images):
        heads = slice(i * PAD, (i + 1) * PAD)
        scores = nt_dot(own_probe[heads], own_ref[i]) - sums[heads] * mean[i : i + 1, :tokens]
        scores = scores * scale[i : i + 1, :tokens] + const[heads]
        scores_ref[heads, :tokens] = jnp.where(lane < lengths_ref[i], scores, -1e30)


def attend_kernel(
    own_ref,
    other_ref,
    counts_ref,
    clusters_ref,
    ranks_ref,
    own_table_ref,
    other_table_ref,
    probe_ref,
    scores_ref,
    first_ref,
    gains_ref,
    shifts_ref,
    biases_ref,
    w_ref,
    w_out_ref,
    w_proj_ref,
    out_ref,
    raw_ref,
    mixed_ref,
):
    images, tokens, half = own_ref.shape
    width = 2 * half
    tensor = lax.axis_index("tensor")
    clus = lax.axis_index("clus")
    own_start = pl.multiple_of(tensor * half, half)
    other_start = pl.multiple_of((1 - tensor) * half, half)
    for i in range(images):
        heads = slice(i * PAD, (i + 1) * PAD)
        raw_ref[heads, :tokens] = nt_dot(probe_ref[heads], other_ref[i])
    mean, scale = (
        over_heads(rows, tokens)
        for rows in moments(own_table_ref, other_table_ref, images, width)
    )
    scores = scores_ref[:, :tokens] + raw_ref[:, :tokens] * scale
    exponent = jnp.exp(scores - jnp.max(scores, axis=1, keepdims=True))
    weights = exponent * (1.0 / jnp.sum(exponent, axis=1, keepdims=True))
    part = (weights * scale).astype(BF16)
    offset = jnp.sum(part.astype(F32) * mean, axis=1, keepdims=True)
    for ref, start in ((own_ref, own_start), (other_ref, other_start)):
        gain, shift = gains_ref[0:1, pl.ds(start, half)], shifts_ref[0:1, pl.ds(start, half)]
        for i in range(images):
            heads = slice(i * PAD, (i + 1) * PAD)
            summed = jnp.dot(part[heads], ref[i], preferred_element_type=F32) - offset[heads]
            mixed_ref[heads, pl.ds(start, half)] = (summed * gain + shift).astype(BF16)
    context = jnp.dot(mixed_ref[...], w_ref[2], preferred_element_type=F32)
    mask = iota((PAD, half), 0) == iota((PAD, half), 1) // HEAD
    context = jnp.sum(jnp.where(mask[None], context.reshape(images, PAD, half), 0.0), axis=1)
    context = context + biases_ref[1:2, pl.ds(own_start, half)]
    fill = jnp.zeros((PAD - images, half), F32)
    context = jnp.concatenate([context, fill], axis=0).astype(BF16)
    out = jnp.dot(context, w_out_ref[...], preferred_element_type=F32)
    extra = jnp.where(tensor == 0, first_ref[...], 0.0)
    row, lane = iota((PAD, width), 0), iota((PAD, width), 1)
    own_images = images // 2
    for j in range(own_images):
        place = tensor * own_images + j
        hit = (lane // PAD == clus) & (lane % PAD == place)
        cluster, rank = clusters_ref[j], ranks_ref[j]
        alive = (place < counts_ref[0]).astype(jnp.int32)
        for k, value in enumerate((cluster, rank // 64, rank % 64, alive)):
            extra = jnp.where(hit & (row == images + k), value.astype(F32), extra)
    out_ref[:, :width] = (out + extra).astype(BF16)
    piece = pl.multiple_of(quarter_of(lax.axis_index("dp"), 0) * PAD, PAD)
    out_ref[:, width:] = w_proj_ref[pl.ds(piece, PAD), :]


def cut_kernel(rows_ref, meta_ref, out_ref):
    width = rows_ref.shape[1] - out_ref.shape[2]
    out_ref[...] = rows_ref[:, width:].reshape(out_ref.shape)


def unpack_kernel(own_ref, next_ref, along_ref, before_ref, out_ref):
    dp = lax.axis_index("dp")
    for ref, step in zip((own_ref, next_ref, along_ref, before_ref), (0, *STEPS)):
        out_ref[:, quarter_of(dp, step)] = ref[...]


def mlp_kernel(
    rows_ref,
    gains_ref,
    shifts_ref,
    biases_ref,
    w1_ref,
    b1_ref,
    w2_ref,
    out_ref,
    first_ref,
    meta_ref,
):
    width, images = w1_ref.shape[0], PAD - 4
    members = rows_ref.shape[0] // PAD
    total = members // 2 * PAD
    member = lax.axis_index("clus") * 2 + lax.axis_index("tensor")
    halves = rows_ref[:, :width].reshape(members // 2, 2, PAD, width)
    halves = [halves[:, side].reshape(total, width) for side in range(2)]
    ints = jnp.sum(
        rows_ref[:, :total].astype(F32).reshape(members, PAD, total)[:, PAD // 2 :], axis=0
    )[images - PAD // 2 :]
    cluster, rank_high, rank_low, alive = (ints[k : k + 1] for k in range(4))
    owner = jnp.floor(cluster * (1.0 / CLUS_DP))
    lane = iota((1, total), 1)
    valid = lane % PAD < images
    before = iota((total, total), 0)
    earlier = (as_column(owner) == owner) & (before % PAD < images) & (before < lane)
    slot = jnp.sum(jnp.where(earlier, 1.0, 0.0), axis=0, keepdims=True)
    target = jnp.where(valid, owner * SLOT + slot, -1.0)
    slots = members * SLOT
    chosen = jnp.where(iota((slots, total), 0).astype(F32) == target, 1.0, 0.0).astype(BF16)
    first = sum(jnp.dot(chosen, half, preferred_element_type=F32) for half in halves)
    first = first + biases_ref[2:3, :]
    mixed = layer_norm(first, gains_ref[1:2, :], shifts_ref[1:2, :]).astype(BF16)
    inner = jnp.dot(mixed, w1_ref[...], preferred_element_type=F32) + b1_ref[...]
    inner = (inner * jax.nn.sigmoid(1.702 * inner)).astype(BF16)
    out_ref[...] = jnp.dot(inner, w2_ref[...], preferred_element_type=F32).astype(BF16)
    mine = (iota((PAD, total), 0) + member * SLOT).astype(F32) == target
    mine = mine & (iota((PAD, total), 0) < SLOT)
    mine_rows = jnp.where(mine, 1.0, 0.0).astype(BF16)
    picked = sum(jnp.dot(mine_rows, half, preferred_element_type=F32) for half in halves)
    first_ref[...] = picked[:SLOT] + biases_ref[2:3, :]
    single = mine[:SLOT]
    home = ((lane // PAD) * images + lane % PAD + 1).astype(F32)
    meta = jnp.zeros((SLOT, INTS), F32)
    for k, value in enumerate((cluster, rank_high, rank_low, alive, home)):
        column = jnp.sum(jnp.where(single, value, 0.0), axis=1, keepdims=True)
        meta = jnp.where(iota((SLOT, INTS), 1) == k, column, meta)
    meta_ref[...] = meta


def pool_kernel(parts_ref, first_ref, meta_ref, gains_ref, shifts_ref, biases_ref, send_ref):
    second = jnp.sum(parts_ref[...].astype(F32), axis=0) + first_ref[...] + biases_ref[3:4, :]
    pooled = layer_norm(second, gains_ref[2:3, :], shifts_ref[2:3, :])
    sub, lane = iota((SLOT, INTS), 0), iota((SLOT, INTS), 1)
    ints = jnp.zeros((SLOT, INTS), F32)
    for k in range(4):
        ints = jnp.where(lane == k * SLOT + sub, meta_ref[:, k : k + 1], ints)
    ints = jnp.sum(ints, axis=0, keepdims=True)
    fill = jnp.zeros((1, pooled.shape[1] - INTS), F32)
    last = iota(pooled.shape, 0) == SLOT - 1
    row = jnp.where(last, jnp.concatenate([ints, fill], axis=1), pooled).astype(BF16)
    send_ref[...] = jnp.broadcast_to(row[None], send_ref.shape)


def unit(features):
    norm = jnp.sum(features * features, axis=-1, keepdims=True)
    return (features * lax.rsqrt(norm + 1e-06)).astype(BF16)


def nearest_kernel(keys_ref, meta_ref, w_ref, out_ref, features_ref):
    total = keys_ref.shape[0]
    keys = keys_ref[...]
    features = jnp.dot(keys, w_ref[...], preferred_element_type=F32)
    features_ref[...] = features.astype(BF16).astype(F32)
    mine = pl.multiple_of(lax.axis_index("dp") * SLOT, SLOT)
    key_units = unit(features_ref[...])
    features = features_ref[pl.ds(mine, SLOT), :]
    similar = nt_dot(unit(features), key_units)
    owners = total // SLOT
    last = iota((owners, total), 1) == iota((owners, total), 0) * SLOT + SLOT - 1
    ints = jnp.dot(
        jnp.where(last, 1.0, 0.0).astype(BF16), keys[:, :INTS], preferred_element_type=F32
    ).astype(BF16)
    place = iota((INTS, total), 1) % SLOT
    block = iota((owners, total), 1) // SLOT == iota((owners, total), 0)
    key_ints = []
    for k in range(4):
        spread = jnp.where(iota((INTS, total), 0) == place + k * SLOT, 1.0, 0.0).astype(BF16)
        rows = jnp.dot(ints, spread, preferred_element_type=F32)
        key_ints.append(jnp.sum(jnp.where(block, rows, 0.0), axis=0, keepdims=True))
    lane = iota((SLOT, INTS), 1)
    cluster, rank_high, rank_low, alive, home = (
        jnp.sum(jnp.where(lane == k, meta_ref[...], 0.0), axis=1, keepdims=True) for k in range(5)
    )
    key_rank = key_ints[1] * 64.0 + key_ints[2]
    allowed = (
        (key_ints[3] > 0.5)
        & (key_ints[0] == cluster)
        & (key_rank < rank_high * 64.0 + rank_low)
    )
    best = jnp.max(jnp.where(allowed, similar, -2.0), axis=1, keepdims=True)
    best = jnp.where(alive > 0.5, jnp.maximum(best, -1.0), -1.0)
    high = best.astype(BF16).astype(F32)
    middle = (best - high).astype(BF16).astype(F32)
    low = best - high - middle
    own_images = (PAD - 4) // 2
    block = jnp.floor((home - 0.5) * (1.0 / own_images))
    place = home - 1.0 - block * own_images
    tail = jnp.zeros((SLOT, INTS), F32)
    for k, value in enumerate((high, middle, low)):
        tail = jnp.where(lane.astype(F32) == place + k * SLOT, value, tail)
    fill = jnp.zeros((SLOT, features.shape[1] - INTS), F32)
    tail = jnp.concatenate([tail, fill], axis=1)
    data = jnp.concatenate([features, tail], axis=0).astype(BF16)
    slots = out_ref.shape[0]
    code = iota((SLOT, slots), 1)
    target, line = (code // SLOT).astype(F32), (code % SLOT).astype(F32)
    here = target == block
    hit = jnp.concatenate(
        [
            jnp.where(here & (line == place), 1.0, 0.0),
            jnp.where(here & (line == SLOT - 1), 1.0, 0.0),
        ],
        axis=0,
    ).astype(BF16)
    out_ref[...] = tn_dot(hit, data).astype(BF16)


def home_kernel(parts_ref, feat_ref, near_ref):
    images = feat_ref.shape[0]
    rows = jnp.sum(parts_ref[...].astype(F32), axis=0)
    feat_ref[...] = rows[:images].astype(BF16)
    tail = rows[SLOT - 1 :, :INTS]
    high, middle, low = (tail[:, k * SLOT : k * SLOT + images] for k in range(3))
    near_ref[...] = high + middle + low


def struct(shape, dtype):
    return jax.ShapeDtypeStruct(shape, dtype)


def cost(micros):
    return pl.CostEstimate(
        flops=int(micros * 1.15e9), bytes_accessed=int(micros * 3.69e6), transcendentals=0
    )


def whole(memory=pltpu.VMEM):
    return pl.BlockSpec(memory_space=memory)


def local(
    hidden,
    token_lengths,
    image_counts,
    cluster_ids,
    order_ranks,
    ln_gains,
    ln_biases,
    w_qkv,
    layer_biases,
    w_out,
    w_fc1,
    fc1_bias,
    w_fc2,
    w_proj,
):
    images, tokens, half = hidden.shape
    width = 2 * half
    embed = w_proj.shape[1]
    members = lax.axis_size("clus") * 2
    owners = lax.axis_size("dp")
    own_images = images // 2
    params = pltpu.CompilerParams(vmem_limit_bytes=24 * 1024 * 1024)
    greedy = pltpu.CompilerParams(vmem_limit_bytes=50 * 1024 * 1024)
    swap = [(0, 1), (1, 0)]
    heads = images * PAD
    hbm = pl.BlockSpec(memory_space=pltpu.HBM)
    other = lax.ppermute(hidden, "tensor", swap)
    w_three = jnp.transpose(w_qkv, (1, 0, 2))
    own, table = pl.pallas_call(
        stats_kernel,
        out_shape=(struct(hidden.shape, BF16), struct((3 * PAD, half), F32)),
        in_specs=[hbm],
        out_specs=[whole()] * 2,
        scratch_shapes=[pltpu.SemaphoreType.DMA((4,))],
        compiler_params=greedy,
        cost_estimate=cost(2.0),
    )(hidden)
    other_table = lax.ppermute(table, "tensor", swap)
    w_three = jnp.transpose(w_qkv, (1, 0, 2))
    probe, scores, residual = pl.pallas_call(
        score_kernel,
        out_shape=(
            struct((heads, half), BF16),
            struct((heads, TABLE), F32),
            struct((PAD, width), F32),
        ),
        in_specs=[whole(), whole(pltpu.SMEM)] + [whole()] * 6,
        out_specs=[whole()] * 3,
        compiler_params=params,
        cost_estimate=cost(2.4),
    )(own, token_lengths, table, other_table, ln_gains, ln_biases, w_three, layer_biases)
    partial = pl.pallas_call(
        attend_kernel,
        out_shape=struct((PAD, width + embed), BF16),
        in_specs=[whole()] * 2 + [whole(pltpu.SMEM)] * 3 + [whole()] * 11,
        out_specs=whole(),
        scratch_shapes=[pltpu.VMEM((heads, TABLE), F32), pltpu.VMEM((heads, width), BF16)],
        compiler_params=params,
        cost_estimate=cost(4.0),
    )(
        own,
        other,
        image_counts,
        cluster_ids,
        order_ranks,
        table,
        other_table,
        probe,
        scores,
        residual,
        ln_gains,
        ln_biases,
        layer_biases,
        w_three,
        w_out,
        w_proj,
    )
    rows = lax.all_gather(partial, MEMBERS, axis=0, tiled=True)
    sent, first, meta = pl.pallas_call(
        mlp_kernel,
        out_shape=(
            struct((members * SLOT, width), BF16),
            struct((SLOT, width), F32),
            struct((SLOT, INTS), F32),
        ),
        compiler_params=params,
        cost_estimate=cost(1.5),
    )(rows, ln_gains, ln_biases, layer_biases, w_fc1, fc1_bias.reshape(1, -1), w_fc2)
    parts = lax.all_to_all(
        sent.reshape(members, SLOT, width), MEMBERS, split_axis=0, concat_axis=0, tiled=True
    )
    piece = pl.pallas_call(
        cut_kernel,
        out_shape=struct((members, PAD, embed), BF16),
        compiler_params=params,
        cost_estimate=cost(0.5),
    )(rows, meta)
    pairs = neighbours(owners)
    pieces = [lax.ppermute(piece, "dp", pairs[step]) for step in STEPS]
    send = pl.pallas_call(
        pool_kernel,
        out_shape=struct((owners, SLOT, width), BF16),
        compiler_params=params,
        cost_estimate=cost(0.5),
    )(parts, first, meta, ln_gains, ln_biases, layer_biases)
    proj = pl.pallas_call(
        unpack_kernel,
        out_shape=struct((members, 4, PAD, embed), BF16),
        compiler_params=params,
        cost_estimate=cost(0.7),
    )(piece, *pieces)
    keys = lax.all_to_all(send, "dp", split_axis=0, concat_axis=0, tiled=True)
    back = pl.pallas_call(
        nearest_kernel,
        out_shape=struct((members * SLOT, embed), BF16),
        scratch_shapes=[pltpu.VMEM((owners * SLOT, embed), F32)],
        compiler_params=params,
        cost_estimate=cost(1.0),
    )(keys.reshape(owners * SLOT, width), meta, proj.reshape(width, embed))
    home = lax.all_to_all(
        back.reshape(members, SLOT, embed), MEMBERS, split_axis=0, concat_axis=0, tiled=True
    )
    features, nearest = pl.pallas_call(
        home_kernel,
        out_shape=(struct((own_images, embed), BF16), struct((1, own_images), F32)),
        compiler_params=params,
        cost_estimate=cost(0.5),
    )(home)
    return (features, nearest.reshape(own_images))


def solution(mesh):
    return jax.shard_map(
        local,
        mesh=mesh,
        in_specs=(
            P(("dp", "clus"), None, "tensor"),
            P(("dp", "clus")),
            P(("dp", "clus")),
            P(("dp", "clus", "tensor")),
            P(("dp", "clus", "tensor")),
            P(),
            P(),
            P(None, None, "tensor"),
            P(),
            P("tensor", None),
            P(None, ("clus", "tensor")),
            P(("clus", "tensor")),
            P(("clus", "tensor"), None),
            P(("clus", "tensor"), None),
        ),
        out_specs=(P(("dp", "clus", "tensor"), None), P(("dp", "clus", "tensor"))),
        check_vma=False,
    )
```

```python
import jax
import jax.numpy as jnp
from jax import lax
from jax.experimental import pallas as pl
from jax.experimental.pallas import tpu as pltpu
from jax.sharding import PartitionSpec as P

HEAD = 64
CLUS_DP = 4
SLOT = 8
PAD = 16
INTS = 128
STAT = 128
TABLE = 384
SIDE = 4
STEPS = (1, 2, 3)
EPS = 1e-05
F32 = jnp.float32
BF16 = jnp.bfloat16
MEMBERS = ("clus", "tensor")


def iota(shape, axis):
    return lax.broadcasted_iota(jnp.int32, shape, axis)


def quarter_of(dp, step):
    return (dp % SIDE + 2 * (dp // SIDE) + step) % 4


def neighbours(owners):
    pairs = {1: [], 2: [], 3: []}
    for dp in range(owners):
        x, y = dp % SIDE, dp // SIDE
        pairs[1].append((y * SIDE + (x + 1) % SIDE, dp))
        pairs[2].append(((y + 1) % SIDE * SIDE + x, dp))
        pairs[3].append((y * SIDE + (x + SIDE - 1) % SIDE, dp))
    return pairs


def layer_norm(values, gain_row, shift_row):
    average = jnp.mean(values, axis=-1, keepdims=True)
    centered = values - average
    spread = jnp.mean(centered * centered, axis=-1, keepdims=True)
    return centered * lax.rsqrt(spread + EPS) * gain_row + shift_row


def as_column(row):
    size = row.shape[1]
    eye = iota((size, size), 0) == iota((size, size), 1)
    return jnp.sum(jnp.where(eye, row, 0.0), axis=1, keepdims=True)


def nt_dot(left, right):
    return lax.dot_general(left, right, (((1,), (1,)), ((), ())), preferred_element_type=F32)


def tn_dot(left, right):
    return lax.dot_general(left, right, (((0,), (0,)), ((), ())), preferred_element_type=F32)


def stats_kernel(hidden_ref, own_ref, table_ref, sem):
    images, tokens, half = own_ref.shape
    block = images // sem.shape[0]
    copies = [
        pltpu.make_async_copy(
            hidden_ref.at[pl.ds(c * block, block)], own_ref.at[pl.ds(c * block, block)], sem.at[c]
        )
        for c in range(sem.shape[0])
    ]
    for copy in copies:
        copy.start()
    rows, lane = TABLE, iota((tokens, STAT), 1)
    table = jnp.zeros((tokens, STAT), F32)
    for i in range(images):
        if i % block == 0:
            copies[i // block].wait()
        states = own_ref[i].astype(F32)
        total = jnp.sum(states, axis=1, keepdims=True)
        centered = states - total * (1.0 / half)
        spread = jnp.sum(centered * centered, axis=1, keepdims=True)
        table = jnp.where(lane == i, total, table)
        table = jnp.where(lane == PAD + i, spread, table)
    table = jnp.concatenate([table, jnp.zeros((rows - tokens, STAT), F32)], axis=0)
    table_ref[: 2 * PAD, :rows] = jnp.transpose(table)[: 2 * PAD]
    table_ref[2 * PAD : 2 * PAD + images, :] = own_ref[:, 0, :].astype(F32)


def moments(own_table_ref, other_table_ref, images, width):
    left, right = own_table_ref[: 2 * PAD, :TABLE], other_table_ref[: 2 * PAD, :TABLE]
    half = width // 2
    mean = (left[:images] + right[:images]) * (1.0 / width)
    apart = (left[:images] - right[:images]) * (1.0 / half)
    spread = left[PAD : PAD + images] + right[PAD : PAD + images] + apart * apart * (half / 2)
    return mean, lax.rsqrt(spread * (1.0 / width) + EPS)


def over_heads(rows, tokens):
    images, lanes = rows.shape
    wide = jnp.broadcast_to(rows[:, None, :], (images, PAD, lanes))
    return wide.reshape(images * PAD, lanes)[:, :tokens]


def attend_kernel(
    own_ref,
    other_ref,
    lengths_ref,
    counts_ref,
    clusters_ref,
    ranks_ref,
    own_table_ref,
    other_table_ref,
    gains_ref,
    shifts_ref,
    biases_ref,
    w_ref,
    w_out_ref,
    w_proj_ref,
    out_ref,
    raw_ref,
    mixed_ref,
):
    images, tokens, half = own_ref.shape
    width = 2 * half
    tensor = lax.axis_index("tensor")
    clus = lax.axis_index("clus")
    own_start = pl.multiple_of(tensor * half, half)
    other_start = pl.multiple_of((1 - tensor) * half, half)
    own_first = own_table_ref[2 * PAD : 2 * PAD + images, :]
    other_first = other_table_ref[2 * PAD : 2 * PAD + images, :]
    first = jnp.concatenate(
        [
            jnp.where(tensor == 0, own_first, other_first),
            jnp.where(tensor == 0, other_first, own_first),
        ],
        axis=1,
    )
    normed = layer_norm(first, gains_ref[0:1, :], shifts_ref[0:1, :]).astype(BF16)
    query = jnp.dot(normed, w_ref[0], preferred_element_type=F32)
    query = (query + biases_ref[0:1, pl.ds(own_start, half)]) * HEAD ** (-0.5)
    query = query.astype(BF16).astype(F32)
    mask = iota((PAD, half), 0) == iota((PAD, half), 1) // HEAD
    wide = jnp.where(mask[None], query[:, None, :], 0.0).reshape(images * PAD, half).astype(BF16)
    probe = nt_dot(wide, w_ref[1])
    const = jnp.sum(probe * shifts_ref[0:1, :], axis=1, keepdims=True)
    probe = (probe * gains_ref[0:1, :]).astype(BF16)
    sums = jnp.sum(probe.astype(F32), axis=1, keepdims=True)
    own_probe = jnp.where(tensor == 0, probe[:, :half], probe[:, half:])
    other_probe = jnp.where(tensor == 0, probe[:, half:], probe[:, :half])
    lane = iota((PAD, tokens), 1)
    for i in range(images):
        heads = slice(i * PAD, (i + 1) * PAD)
        scores = nt_dot(own_probe[heads], own_ref[i]) + nt_dot(other_probe[heads], other_ref[i])
        raw_ref[heads, :tokens] = jnp.where(lane < lengths_ref[i], scores, -1e30)
    mean, scale = (
        over_heads(rows, tokens)
        for rows in moments(own_table_ref, other_table_ref, images, width)
    )
    scores = (raw_ref[:, :tokens] - sums * mean) * scale + const
    exponent = jnp.exp(scores - jnp.max(scores, axis=1, keepdims=True))
    weights = exponent * (1.0 / jnp.sum(exponent, axis=1, keepdims=True))
    part = (weights * scale).astype(BF16)
    offset = jnp.sum(part.astype(F32) * mean, axis=1, keepdims=True)
    for ref, start in ((own_ref, own_start), (other_ref, other_start)):
        gain, shift = gains_ref[0:1, pl.ds(start, half)], shifts_ref[0:1, pl.ds(start, half)]
        for i in range(images):
            heads = slice(i * PAD, (i + 1) * PAD)
            summed = jnp.dot(part[heads], ref[i], preferred_element_type=F32) - offset[heads]
            mixed_ref[heads, pl.ds(start, half)] = (summed * gain + shift).astype(BF16)
    context = jnp.dot(mixed_ref[...], w_ref[2], preferred_element_type=F32)
    mask = iota((PAD, half), 0) == iota((PAD, half), 1) // HEAD
    context = jnp.sum(jnp.where(mask[None], context.reshape(images, PAD, half), 0.0), axis=1)
    context = context + biases_ref[1:2, pl.ds(own_start, half)]
    fill = jnp.zeros((PAD - images, half), F32)
    context = jnp.concatenate([context, fill], axis=0).astype(BF16)
    out = jnp.dot(context, w_out_ref[...], preferred_element_type=F32)
    extra = jnp.where(tensor == 0, first, 0.0)
    extra = jnp.concatenate([extra, jnp.zeros((PAD - images, width), F32)], axis=0)
    row, lane = iota((PAD, width), 0), iota((PAD, width), 1)
    own_images = images // 2
    for j in range(own_images):
        place = tensor * own_images + j
        hit = (lane // PAD == clus) & (lane % PAD == place)
        cluster, rank = clusters_ref[j], ranks_ref[j]
        alive = (place < counts_ref[0]).astype(jnp.int32)
        for k, value in enumerate((cluster, rank // 64, rank % 64, alive)):
            extra = jnp.where(hit & (row == images + k), value.astype(F32), extra)
    out_ref[:, :width] = (out + extra).astype(BF16)
    piece = pl.multiple_of(quarter_of(lax.axis_index("dp"), 0) * PAD, PAD)
    out_ref[:, width:] = w_proj_ref[pl.ds(piece, PAD), :]


def cut_kernel(rows_ref, meta_ref, out_ref):
    width = rows_ref.shape[1] - out_ref.shape[2]
    out_ref[...] = rows_ref[:, width:].reshape(out_ref.shape)


def unpack_kernel(own_ref, next_ref, along_ref, before_ref, out_ref):
    dp = lax.axis_index("dp")
    for ref, step in zip((own_ref, next_ref, along_ref, before_ref), (0, *STEPS)):
        out_ref[:, quarter_of(dp, step)] = ref[...]


def mlp_kernel(
    rows_ref,
    gains_ref,
    shifts_ref,
    biases_ref,
    w1_ref,
    b1_ref,
    w2_ref,
    out_ref,
    first_ref,
    meta_ref,
):
    width, images = w1_ref.shape[0], PAD - 4
    members = rows_ref.shape[0] // PAD
    total = members // 2 * PAD
    member = lax.axis_index("clus") * 2 + lax.axis_index("tensor")
    halves = rows_ref[:, :width].reshape(members // 2, 2, PAD, width)
    halves = [halves[:, side].reshape(total, width) for side in range(2)]
    ints = jnp.sum(
        rows_ref[:, :total].astype(F32).reshape(members, PAD, total)[:, PAD // 2 :], axis=0
    )[images - PAD // 2 :]
    cluster, rank_high, rank_low, alive = (ints[k : k + 1] for k in range(4))
    owner = jnp.floor(cluster * (1.0 / CLUS_DP))
    lane = iota((1, total), 1)
    valid = lane % PAD < images
    before = iota((total, total), 0)
    earlier = (as_column(owner) == owner) & (before % PAD < images) & (before < lane)
    slot = jnp.sum(jnp.where(earlier, 1.0, 0.0), axis=0, keepdims=True)
    target = jnp.where(valid, owner * SLOT + slot, -1.0)
    slots = members * SLOT
    chosen = jnp.where(iota((slots, total), 0).astype(F32) == target, 1.0, 0.0).astype(BF16)
    first = sum(jnp.dot(chosen, half, preferred_element_type=F32) for half in halves)
    first = first + biases_ref[2:3, :]
    mixed = layer_norm(first, gains_ref[1:2, :], shifts_ref[1:2, :]).astype(BF16)
    inner = jnp.dot(mixed, w1_ref[...], preferred_element_type=F32) + b1_ref[...]
    inner = (inner * jax.nn.sigmoid(1.702 * inner)).astype(BF16)
    out_ref[...] = jnp.dot(inner, w2_ref[...], preferred_element_type=F32).astype(BF16)
    mine = (iota((PAD, total), 0) + member * SLOT).astype(F32) == target
    mine = mine & (iota((PAD, total), 0) < SLOT)
    mine_rows = jnp.where(mine, 1.0, 0.0).astype(BF16)
    picked = sum(jnp.dot(mine_rows, half, preferred_element_type=F32) for half in halves)
    first_ref[...] = picked[:SLOT] + biases_ref[2:3, :]
    single = mine[:SLOT]
    home = ((lane // PAD) * images + lane % PAD + 1).astype(F32)
    meta = jnp.zeros((SLOT, INTS), F32)
    for k, value in enumerate((cluster, rank_high, rank_low, alive, home)):
        column = jnp.sum(jnp.where(single, value, 0.0), axis=1, keepdims=True)
        meta = jnp.where(iota((SLOT, INTS), 1) == k, column, meta)
    meta_ref[...] = meta


def pool_kernel(parts_ref, first_ref, meta_ref, gains_ref, shifts_ref, biases_ref, send_ref):
    second = jnp.sum(parts_ref[...].astype(F32), axis=0) + first_ref[...] + biases_ref[3:4, :]
    pooled = layer_norm(second, gains_ref[2:3, :], shifts_ref[2:3, :])
    sub, lane = iota((SLOT, INTS), 0), iota((SLOT, INTS), 1)
    ints = jnp.zeros((SLOT, INTS), F32)
    for k in range(4):
        ints = jnp.where(lane == k * SLOT + sub, meta_ref[:, k : k + 1], ints)
    ints = jnp.sum(ints, axis=0, keepdims=True)
    fill = jnp.zeros((1, pooled.shape[1] - INTS), F32)
    last = iota(pooled.shape, 0) == SLOT - 1
    row = jnp.where(last, jnp.concatenate([ints, fill], axis=1), pooled).astype(BF16)
    send_ref[...] = jnp.broadcast_to(row[None], send_ref.shape)


def unit(features):
    norm = jnp.sum(features * features, axis=-1, keepdims=True)
    return (features * lax.rsqrt(norm + 1e-06)).astype(BF16)


def nearest_kernel(keys_ref, meta_ref, w_ref, out_ref, features_ref):
    total = keys_ref.shape[0]
    keys = keys_ref[...]
    features = jnp.dot(keys, w_ref[...], preferred_element_type=F32)
    features_ref[...] = features.astype(BF16).astype(F32)
    mine = pl.multiple_of(lax.axis_index("dp") * SLOT, SLOT)
    key_units = unit(features_ref[...])
    features = features_ref[pl.ds(mine, SLOT), :]
    similar = nt_dot(unit(features), key_units)
    owners = total // SLOT
    last = iota((owners, total), 1) == iota((owners, total), 0) * SLOT + SLOT - 1
    ints = jnp.dot(
        jnp.where(last, 1.0, 0.0).astype(BF16), keys[:, :INTS], preferred_element_type=F32
    ).astype(BF16)
    place = iota((INTS, total), 1) % SLOT
    block = iota((owners, total), 1) // SLOT == iota((owners, total), 0)
    key_ints = []
    for k in range(4):
        spread = jnp.where(iota((INTS, total), 0) == place + k * SLOT, 1.0, 0.0).astype(BF16)
        rows = jnp.dot(ints, spread, preferred_element_type=F32)
        key_ints.append(jnp.sum(jnp.where(block, rows, 0.0), axis=0, keepdims=True))
    lane = iota((SLOT, INTS), 1)
    cluster, rank_high, rank_low, alive, home = (
        jnp.sum(jnp.where(lane == k, meta_ref[...], 0.0), axis=1, keepdims=True) for k in range(5)
    )
    key_rank = key_ints[1] * 64.0 + key_ints[2]
    allowed = (
        (key_ints[3] > 0.5)
        & (key_ints[0] == cluster)
        & (key_rank < rank_high * 64.0 + rank_low)
    )
    best = jnp.max(jnp.where(allowed, similar, -2.0), axis=1, keepdims=True)
    best = jnp.where(alive > 0.5, jnp.maximum(best, -1.0), -1.0)
    high = best.astype(BF16).astype(F32)
    middle = (best - high).astype(BF16).astype(F32)
    low = best - high - middle
    own_images = (PAD - 4) // 2
    block = jnp.floor((home - 0.5) * (1.0 / own_images))
    place = home - 1.0 - block * own_images
    tail = jnp.zeros((SLOT, INTS), F32)
    for k, value in enumerate((high, middle, low)):
        tail = jnp.where(lane.astype(F32) == place + k * SLOT, value, tail)
    fill = jnp.zeros((SLOT, features.shape[1] - INTS), F32)
    tail = jnp.concatenate([tail, fill], axis=1)
    data = jnp.concatenate([features, tail], axis=0).astype(BF16)
    slots = out_ref.shape[0]
    code = iota((SLOT, slots), 1)
    target, line = (code // SLOT).astype(F32), (code % SLOT).astype(F32)
    here = target == block
    hit = jnp.concatenate(
        [
            jnp.where(here & (line == place), 1.0, 0.0),
            jnp.where(here & (line == SLOT - 1), 1.0, 0.0),
        ],
        axis=0,
    ).astype(BF16)
    out_ref[...] = tn_dot(hit, data).astype(BF16)


def home_kernel(parts_ref, feat_ref, near_ref):
    images = feat_ref.shape[0]
    rows = jnp.sum(parts_ref[...].astype(F32), axis=0)
    feat_ref[...] = rows[:images].astype(BF16)
    tail = rows[SLOT - 1 :, :INTS]
    high, middle, low = (tail[:, k * SLOT : k * SLOT + images] for k in range(3))
    near_ref[...] = high + middle + low


def struct(shape, dtype):
    return jax.ShapeDtypeStruct(shape, dtype)


def cost(micros):
    return pl.CostEstimate(
        flops=int(micros * 1.15e9), bytes_accessed=int(micros * 3.69e6), transcendentals=0
    )


def whole(memory=pltpu.VMEM):
    return pl.BlockSpec(memory_space=memory)


def local(
    hidden,
    token_lengths,
    image_counts,
    cluster_ids,
    order_ranks,
    ln_gains,
    ln_biases,
    w_qkv,
    layer_biases,
    w_out,
    w_fc1,
    fc1_bias,
    w_fc2,
    w_proj,
):
    images, tokens, half = hidden.shape
    width = 2 * half
    embed = w_proj.shape[1]
    members = lax.axis_size("clus") * 2
    owners = lax.axis_size("dp")
    own_images = images // 2
    params = pltpu.CompilerParams(vmem_limit_bytes=24 * 1024 * 1024)
    greedy = pltpu.CompilerParams(vmem_limit_bytes=50 * 1024 * 1024)
    swap = [(0, 1), (1, 0)]
    heads = images * PAD
    hbm = pl.BlockSpec(memory_space=pltpu.HBM)
    other = lax.ppermute(hidden, "tensor", swap)
    w_three = jnp.transpose(w_qkv, (1, 0, 2))
    own, table = pl.pallas_call(
        stats_kernel,
        out_shape=(struct(hidden.shape, BF16), struct((3 * PAD, half), F32)),
        in_specs=[hbm],
        out_specs=[whole()] * 2,
        scratch_shapes=[pltpu.SemaphoreType.DMA((4,))],
        compiler_params=greedy,
        cost_estimate=cost(2.0),
    )(hidden)
    other_table = lax.ppermute(table, "tensor", swap)
    w_three = jnp.transpose(w_qkv, (1, 0, 2))
    partial = pl.pallas_call(
        attend_kernel,
        out_shape=struct((PAD, width + embed), BF16),
        in_specs=[whole()] * 2 + [whole(pltpu.SMEM)] * 4 + [whole()] * 8,
        out_specs=whole(),
        scratch_shapes=[pltpu.VMEM((heads, TABLE), F32), pltpu.VMEM((heads, width), BF16)],
        compiler_params=params,
        cost_estimate=cost(6.0),
    )(
        own,
        other,
        token_lengths,
        image_counts,
        cluster_ids,
        order_ranks,
        table,
        other_table,
        ln_gains,
        ln_biases,
        layer_biases,
        w_three,
        w_out,
        w_proj,
    )
    rows = lax.all_gather(partial, MEMBERS, axis=0, tiled=True)
    sent, first, meta = pl.pallas_call(
        mlp_kernel,
        out_shape=(
            struct((members * SLOT, width), BF16),
            struct((SLOT, width), F32),
            struct((SLOT, INTS), F32),
        ),
        compiler_params=params,
        cost_estimate=cost(1.5),
    )(rows, ln_gains, ln_biases, layer_biases, w_fc1, fc1_bias.reshape(1, -1), w_fc2)
    parts = lax.all_to_all(
        sent.reshape(members, SLOT, width), MEMBERS, split_axis=0, concat_axis=0, tiled=True
    )
    piece = pl.pallas_call(
        cut_kernel,
        out_shape=struct((members, PAD, embed), BF16),
        compiler_params=params,
        cost_estimate=cost(0.5),
    )(rows, meta)
    pairs = neighbours(owners)
    pieces = [lax.ppermute(piece, "dp", pairs[step]) for step in STEPS]
    send = pl.pallas_call(
        pool_kernel,
        out_shape=struct((owners, SLOT, width), BF16),
        compiler_params=params,
        cost_estimate=cost(0.5),
    )(parts, first, meta, ln_gains, ln_biases, layer_biases)
    proj = pl.pallas_call(
        unpack_kernel,
        out_shape=struct((members, 4, PAD, embed), BF16),
        compiler_params=params,
        cost_estimate=cost(0.7),
    )(piece, *pieces)
    keys = lax.all_to_all(send, "dp", split_axis=0, concat_axis=0, tiled=True)
    back = pl.pallas_call(
        nearest_kernel,
        out_shape=struct((members * SLOT, embed), BF16),
        scratch_shapes=[pltpu.VMEM((owners * SLOT, embed), F32)],
        compiler_params=params,
        cost_estimate=cost(1.0),
    )(keys.reshape(owners * SLOT, width), meta, proj.reshape(width, embed))
    home = lax.all_to_all(
        back.reshape(members, SLOT, embed), MEMBERS, split_axis=0, concat_axis=0, tiled=True
    )
    features, nearest = pl.pallas_call(
        home_kernel,
        out_shape=(struct((own_images, embed), BF16), struct((1, own_images), F32)),
        compiler_params=params,
        cost_estimate=cost(0.5),
    )(home)
    return (features, nearest.reshape(own_images))


def solution(mesh):
    return jax.shard_map(
        local,
        mesh=mesh,
        in_specs=(
            P(("dp", "clus"), None, "tensor"),
            P(("dp", "clus")),
            P(("dp", "clus")),
            P(("dp", "clus", "tensor")),
            P(("dp", "clus", "tensor")),
            P(),
            P(),
            P(None, None, "tensor"),
            P(),
            P("tensor", None),
            P(None, ("clus", "tensor")),
            P(("clus", "tensor")),
            P(("clus", "tensor"), None),
            P(("clus", "tensor"), None),
        ),
        out_specs=(P(("dp", "clus", "tensor"), None), P(("dp", "clus", "tensor"))),
        check_vma=False,
    )
```

```python
import jax
import jax.numpy as jnp
from jax import lax
from jax.experimental import pallas as pl
from jax.experimental.pallas import tpu as pltpu
from jax.sharding import PartitionSpec as P

HEAD = 64
CLUS_DP = 4
SLOT = 8
PAD = 16
INTS = 128
STAT = 128
TABLE = 384
SIDE = 4
STEPS = (1, 2, 3)
EPS = 1e-05
F32 = jnp.float32
BF16 = jnp.bfloat16
MEMBERS = ("clus", "tensor")
SPREAD = ("tensor", "clus")


def iota(shape, axis):
    return lax.broadcasted_iota(jnp.int32, shape, axis)


def quarter_of(dp, step):
    return (dp % SIDE + 2 * (dp // SIDE) + step) % 4


def neighbours(owners):
    pairs = {1: [], 2: [], 3: []}
    for dp in range(owners):
        x, y = dp % SIDE, dp // SIDE
        pairs[1].append((y * SIDE + (x + 1) % SIDE, dp))
        pairs[2].append(((y + 1) % SIDE * SIDE + x, dp))
        pairs[3].append((y * SIDE + (x + SIDE - 1) % SIDE, dp))
    return pairs


def layer_norm(values, gain_row, shift_row):
    average = jnp.mean(values, axis=-1, keepdims=True)
    centered = values - average
    spread = jnp.mean(centered * centered, axis=-1, keepdims=True)
    return centered * lax.rsqrt(spread + EPS) * gain_row + shift_row


def as_column(row):
    size = row.shape[1]
    eye = iota((size, size), 0) == iota((size, size), 1)
    return jnp.sum(jnp.where(eye, row, 0.0), axis=1, keepdims=True)


def nt_dot(left, right):
    return lax.dot_general(left, right, (((1,), (1,)), ((), ())), preferred_element_type=F32)


def tn_dot(left, right):
    return lax.dot_general(left, right, (((0,), (0,)), ((), ())), preferred_element_type=F32)


def stats_kernel(hidden_ref, own_ref, table_ref, sem):
    images, tokens, half = own_ref.shape
    block = images // sem.shape[0]
    copies = [
        pltpu.make_async_copy(
            hidden_ref.at[pl.ds(c * block, block)], own_ref.at[pl.ds(c * block, block)], sem.at[c]
        )
        for c in range(sem.shape[0])
    ]
    for copy in copies:
        copy.start()
    rows, lane = TABLE, iota((tokens, STAT), 1)
    table = jnp.zeros((tokens, STAT), F32)
    for i in range(images):
        if i % block == 0:
            copies[i // block].wait()
        states = own_ref[i].astype(F32)
        total = jnp.sum(states, axis=1, keepdims=True)
        centered = states - total * (1.0 / half)
        spread = jnp.sum(centered * centered, axis=1, keepdims=True)
        table = jnp.where(lane == i, total, table)
        table = jnp.where(lane == PAD + i, spread, table)
    table = jnp.concatenate([table, jnp.zeros((rows - tokens, STAT), F32)], axis=0)
    table_ref[: 2 * PAD, :rows] = jnp.transpose(table)[: 2 * PAD]
    table_ref[2 * PAD : 2 * PAD + images, :] = own_ref[:, 0, :].astype(F32)


def moments(own_table_ref, other_table_ref, images, width):
    left, right = own_table_ref[: 2 * PAD, :TABLE], other_table_ref[: 2 * PAD, :TABLE]
    half = width // 2
    mean = (left[:images] + right[:images]) * (1.0 / width)
    apart = (left[:images] - right[:images]) * (1.0 / half)
    spread = left[PAD : PAD + images] + right[PAD : PAD + images] + apart * apart * (half / 2)
    return mean, lax.rsqrt(spread * (1.0 / width) + EPS)


def over_heads(rows, tokens):
    images, lanes = rows.shape
    wide = jnp.broadcast_to(rows[:, None, :], (images, PAD, lanes))
    return wide.reshape(images * PAD, lanes)[:, :tokens]


def attend_kernel(
    own_ref,
    other_ref,
    lengths_ref,
    counts_ref,
    clusters_ref,
    ranks_ref,
    own_table_ref,
    other_table_ref,
    gains_ref,
    shifts_ref,
    biases_ref,
    w_ref,
    w_out_ref,
    w_proj_ref,
    out_ref,
    raw_ref,
    mixed_ref,
):
    images, tokens, half = own_ref.shape
    width = 2 * half
    tensor = lax.axis_index("tensor")
    clus = lax.axis_index("clus")
    own_start = pl.multiple_of(tensor * half, half)
    other_start = pl.multiple_of((1 - tensor) * half, half)
    own_first = own_table_ref[2 * PAD : 2 * PAD + images, :]
    other_first = other_table_ref[2 * PAD : 2 * PAD + images, :]
    first = jnp.concatenate(
        [
            jnp.where(tensor == 0, own_first, other_first),
            jnp.where(tensor == 0, other_first, own_first),
        ],
        axis=1,
    )
    normed = layer_norm(first, gains_ref[0:1, :], shifts_ref[0:1, :]).astype(BF16)
    query = jnp.dot(normed, w_ref[0], preferred_element_type=F32)
    query = (query + biases_ref[0:1, pl.ds(own_start, half)]) * HEAD ** (-0.5)
    query = query.astype(BF16).astype(F32)
    mask = iota((PAD, half), 0) == iota((PAD, half), 1) // HEAD
    wide = jnp.where(mask[None], query[:, None, :], 0.0).reshape(images * PAD, half).astype(BF16)
    probe = nt_dot(wide, w_ref[1])
    const = jnp.sum(probe * shifts_ref[0:1, :], axis=1, keepdims=True)
    probe = (probe * gains_ref[0:1, :]).astype(BF16)
    sums = jnp.sum(probe.astype(F32), axis=1, keepdims=True)
    own_probe = jnp.where(tensor == 0, probe[:, :half], probe[:, half:])
    other_probe = jnp.where(tensor == 0, probe[:, half:], probe[:, :half])
    lane = iota((PAD, tokens), 1)
    for i in range(images):
        heads = slice(i * PAD, (i + 1) * PAD)
        scores = nt_dot(own_probe[heads], own_ref[i]) + nt_dot(other_probe[heads], other_ref[i])
        raw_ref[heads, :tokens] = jnp.where(lane < lengths_ref[i], scores, -1e30)
    mean, scale = (
        over_heads(rows, tokens)
        for rows in moments(own_table_ref, other_table_ref, images, width)
    )
    scores = (raw_ref[:, :tokens] - sums * mean) * scale + const
    exponent = jnp.exp(scores - jnp.max(scores, axis=1, keepdims=True))
    weights = exponent * (1.0 / jnp.sum(exponent, axis=1, keepdims=True))
    part = (weights * scale).astype(BF16)
    offset = jnp.sum(part.astype(F32) * mean, axis=1, keepdims=True)
    for ref, start in ((own_ref, own_start), (other_ref, other_start)):
        gain, shift = gains_ref[0:1, pl.ds(start, half)], shifts_ref[0:1, pl.ds(start, half)]
        for i in range(images):
            heads = slice(i * PAD, (i + 1) * PAD)
            summed = jnp.dot(part[heads], ref[i], preferred_element_type=F32) - offset[heads]
            mixed_ref[heads, pl.ds(start, half)] = (summed * gain + shift).astype(BF16)
    context = jnp.dot(mixed_ref[...], w_ref[2], preferred_element_type=F32)
    mask = iota((PAD, half), 0) == iota((PAD, half), 1) // HEAD
    context = jnp.sum(jnp.where(mask[None], context.reshape(images, PAD, half), 0.0), axis=1)
    context = context + biases_ref[1:2, pl.ds(own_start, half)]
    fill = jnp.zeros((PAD - images, half), F32)
    context = jnp.concatenate([context, fill], axis=0).astype(BF16)
    out = jnp.dot(context, w_out_ref[...], preferred_element_type=F32)
    extra = jnp.where(tensor == 0, first, 0.0)
    extra = jnp.concatenate([extra, jnp.zeros((PAD - images, width), F32)], axis=0)
    row, lane = iota((PAD, width), 0), iota((PAD, width), 1)
    own_images = images // 2
    for j in range(own_images):
        place = tensor * own_images + j
        hit = (lane // PAD == clus) & (lane % PAD == place)
        cluster, rank = clusters_ref[j], ranks_ref[j]
        alive = (place < counts_ref[0]).astype(jnp.int32)
        for k, value in enumerate((cluster, rank // 64, rank % 64, alive)):
            extra = jnp.where(hit & (row == images + k), value.astype(F32), extra)
    out_ref[:, :width] = (out + extra).astype(BF16)
    piece = pl.multiple_of(quarter_of(lax.axis_index("dp"), 0) * PAD, PAD)
    out_ref[:, width:] = w_proj_ref[pl.ds(piece, PAD), :]


def cut_kernel(rows_ref, meta_ref, out_ref):
    width = rows_ref.shape[1] - out_ref.shape[2]
    out_ref[...] = rows_ref[:, width:].reshape(out_ref.shape)


def unpack_kernel(own_ref, next_ref, along_ref, before_ref, out_ref):
    dp = lax.axis_index("dp")
    for ref, step in zip((own_ref, next_ref, along_ref, before_ref), (0, *STEPS)):
        out_ref[:, quarter_of(dp, step)] = ref[...]


def mlp_kernel(
    rows_ref,
    gains_ref,
    shifts_ref,
    biases_ref,
    w1_ref,
    b1_ref,
    w2_ref,
    out_ref,
    first_ref,
    meta_ref,
):
    width, images = w1_ref.shape[0], PAD - 4
    members = rows_ref.shape[0] // PAD
    total = members // 2 * PAD
    member = lax.axis_index("tensor") * (members // 2) + lax.axis_index("clus")
    halves = rows_ref[:, :width].reshape(members // 2, 2, PAD, width)
    halves = [halves[:, side].reshape(total, width) for side in range(2)]
    ints = jnp.sum(
        rows_ref[:, :total].astype(F32).reshape(members, PAD, total)[:, PAD // 2 :], axis=0
    )[images - PAD // 2 :]
    cluster, rank_high, rank_low, alive = (ints[k : k + 1] for k in range(4))
    owner = jnp.floor(cluster * (1.0 / CLUS_DP))
    lane = iota((1, total), 1)
    valid = lane % PAD < images
    before = iota((total, total), 0)
    earlier = (as_column(owner) == owner) & (before % PAD < images) & (before < lane)
    slot = jnp.sum(jnp.where(earlier, 1.0, 0.0), axis=0, keepdims=True)
    target = jnp.where(valid, owner * SLOT + slot, -1.0)
    slots = members * SLOT
    chosen = jnp.where(iota((slots, total), 0).astype(F32) == target, 1.0, 0.0).astype(BF16)
    first = sum(jnp.dot(chosen, half, preferred_element_type=F32) for half in halves)
    first = first + biases_ref[2:3, :]
    mixed = layer_norm(first, gains_ref[1:2, :], shifts_ref[1:2, :]).astype(BF16)
    inner = jnp.dot(mixed, w1_ref[...], preferred_element_type=F32) + b1_ref[...]
    inner = (inner * jax.nn.sigmoid(1.702 * inner)).astype(BF16)
    out_ref[...] = jnp.dot(inner, w2_ref[...], preferred_element_type=F32).astype(BF16)
    mine = (iota((PAD, total), 0) + member * SLOT).astype(F32) == target
    mine = mine & (iota((PAD, total), 0) < SLOT)
    mine_rows = jnp.where(mine, 1.0, 0.0).astype(BF16)
    picked = sum(jnp.dot(mine_rows, half, preferred_element_type=F32) for half in halves)
    first_ref[...] = picked[:SLOT] + biases_ref[2:3, :]
    single = mine[:SLOT]
    home = ((lane // PAD) * images + lane % PAD + 1).astype(F32)
    meta = jnp.zeros((SLOT, INTS), F32)
    for k, value in enumerate((cluster, rank_high, rank_low, alive, home)):
        column = jnp.sum(jnp.where(single, value, 0.0), axis=1, keepdims=True)
        meta = jnp.where(iota((SLOT, INTS), 1) == k, column, meta)
    meta_ref[...] = meta


def pool_kernel(parts_ref, first_ref, meta_ref, gains_ref, shifts_ref, biases_ref, send_ref):
    second = jnp.sum(parts_ref[...].astype(F32), axis=0) + first_ref[...] + biases_ref[3:4, :]
    pooled = layer_norm(second, gains_ref[2:3, :], shifts_ref[2:3, :])
    sub, lane = iota((SLOT, INTS), 0), iota((SLOT, INTS), 1)
    ints = jnp.zeros((SLOT, INTS), F32)
    for k in range(4):
        ints = jnp.where(lane == k * SLOT + sub, meta_ref[:, k : k + 1], ints)
    ints = jnp.sum(ints, axis=0, keepdims=True)
    fill = jnp.zeros((1, pooled.shape[1] - INTS), F32)
    last = iota(pooled.shape, 0) == SLOT - 1
    row = jnp.where(last, jnp.concatenate([ints, fill], axis=1), pooled).astype(BF16)
    send_ref[...] = jnp.broadcast_to(row[None], send_ref.shape)


def unit(features):
    norm = jnp.sum(features * features, axis=-1, keepdims=True)
    return (features * lax.rsqrt(norm + 1e-06)).astype(BF16)


def nearest_kernel(keys_ref, meta_ref, w_ref, out_ref, features_ref):
    total = keys_ref.shape[0]
    keys = keys_ref[...]
    features = jnp.dot(keys, w_ref[...], preferred_element_type=F32)
    features_ref[...] = features.astype(BF16).astype(F32)
    mine = pl.multiple_of(lax.axis_index("dp") * SLOT, SLOT)
    key_units = unit(features_ref[...])
    features = features_ref[pl.ds(mine, SLOT), :]
    similar = nt_dot(unit(features), key_units)
    owners = total // SLOT
    last = iota((owners, total), 1) == iota((owners, total), 0) * SLOT + SLOT - 1
    ints = jnp.dot(
        jnp.where(last, 1.0, 0.0).astype(BF16), keys[:, :INTS], preferred_element_type=F32
    ).astype(BF16)
    place = iota((INTS, total), 1) % SLOT
    block = iota((owners, total), 1) // SLOT == iota((owners, total), 0)
    key_ints = []
    for k in range(4):
        spread = jnp.where(iota((INTS, total), 0) == place + k * SLOT, 1.0, 0.0).astype(BF16)
        rows = jnp.dot(ints, spread, preferred_element_type=F32)
        key_ints.append(jnp.sum(jnp.where(block, rows, 0.0), axis=0, keepdims=True))
    lane = iota((SLOT, INTS), 1)
    cluster, rank_high, rank_low, alive, home = (
        jnp.sum(jnp.where(lane == k, meta_ref[...], 0.0), axis=1, keepdims=True) for k in range(5)
    )
    key_rank = key_ints[1] * 64.0 + key_ints[2]
    allowed = (
        (key_ints[3] > 0.5)
        & (key_ints[0] == cluster)
        & (key_rank < rank_high * 64.0 + rank_low)
    )
    best = jnp.max(jnp.where(allowed, similar, -2.0), axis=1, keepdims=True)
    best = jnp.where(alive > 0.5, jnp.maximum(best, -1.0), -1.0)
    high = best.astype(BF16).astype(F32)
    middle = (best - high).astype(BF16).astype(F32)
    low = best - high - middle
    own_images = (PAD - 4) // 2
    block = jnp.floor((home - 0.5) * (1.0 / own_images))
    place = home - 1.0 - block * own_images
    tail = jnp.zeros((SLOT, INTS), F32)
    for k, value in enumerate((high, middle, low)):
        tail = jnp.where(lane.astype(F32) == place + k * SLOT, value, tail)
    fill = jnp.zeros((SLOT, features.shape[1] - INTS), F32)
    tail = jnp.concatenate([tail, fill], axis=1)
    data = jnp.concatenate([features, tail], axis=0).astype(BF16)
    slots = out_ref.shape[0]
    chip = jnp.floor(block * 0.5)
    member = (block - 2.0 * chip) * (slots // SLOT // 2) + chip
    code = iota((SLOT, slots), 1)
    target, line = (code // SLOT).astype(F32), (code % SLOT).astype(F32)
    here = (target == member) & (home > 0.5)
    hit = jnp.concatenate(
        [
            jnp.where(here & (line == place), 1.0, 0.0),
            jnp.where(here & (line == SLOT - 1), 1.0, 0.0),
        ],
        axis=0,
    ).astype(BF16)
    out_ref[...] = tn_dot(hit, data).astype(BF16)


def home_kernel(parts_ref, feat_ref, near_ref):
    images = feat_ref.shape[0]
    rows = jnp.sum(parts_ref[...].astype(F32), axis=0)
    feat_ref[...] = rows[:images].astype(BF16)
    tail = rows[SLOT - 1 :, :INTS]
    high, middle, low = (tail[:, k * SLOT : k * SLOT + images] for k in range(3))
    near_ref[...] = high + middle + low


def struct(shape, dtype):
    return jax.ShapeDtypeStruct(shape, dtype)


def cost(micros):
    return pl.CostEstimate(
        flops=int(micros * 1.15e9), bytes_accessed=int(micros * 3.69e6), transcendentals=0
    )


def whole(memory=pltpu.VMEM):
    return pl.BlockSpec(memory_space=memory)


def local(
    hidden,
    token_lengths,
    image_counts,
    cluster_ids,
    order_ranks,
    ln_gains,
    ln_biases,
    w_qkv,
    layer_biases,
    w_out,
    w_fc1,
    fc1_bias,
    w_fc2,
    w_proj,
):
    images, tokens, half = hidden.shape
    width = 2 * half
    embed = w_proj.shape[1]
    members = lax.axis_size("clus") * 2
    owners = lax.axis_size("dp")
    own_images = images // 2
    params = pltpu.CompilerParams(vmem_limit_bytes=24 * 1024 * 1024)
    greedy = pltpu.CompilerParams(vmem_limit_bytes=50 * 1024 * 1024)
    swap = [(0, 1), (1, 0)]
    heads = images * PAD
    hbm = pl.BlockSpec(memory_space=pltpu.HBM)
    other = lax.ppermute(hidden, "tensor", swap)
    w_three = jnp.transpose(w_qkv, (1, 0, 2))
    own, table = pl.pallas_call(
        stats_kernel,
        out_shape=(struct(hidden.shape, BF16), struct((3 * PAD, half), F32)),
        in_specs=[hbm],
        out_specs=[whole()] * 2,
        scratch_shapes=[pltpu.SemaphoreType.DMA((4,))],
        compiler_params=greedy,
        cost_estimate=cost(2.0),
    )(hidden)
    other_table = lax.ppermute(table, "tensor", swap)
    w_three = jnp.transpose(w_qkv, (1, 0, 2))
    partial = pl.pallas_call(
        attend_kernel,
        out_shape=struct((PAD, width + embed), BF16),
        in_specs=[whole()] * 2 + [whole(pltpu.SMEM)] * 4 + [whole()] * 8,
        out_specs=whole(),
        scratch_shapes=[pltpu.VMEM((heads, TABLE), F32), pltpu.VMEM((heads, width), BF16)],
        compiler_params=params,
        cost_estimate=cost(6.0),
    )(
        own,
        other,
        token_lengths,
        image_counts,
        cluster_ids,
        order_ranks,
        table,
        other_table,
        ln_gains,
        ln_biases,
        layer_biases,
        w_three,
        w_out,
        w_proj,
    )
    rows = lax.all_gather(partial, MEMBERS, axis=0, tiled=True)
    sent, first, meta = pl.pallas_call(
        mlp_kernel,
        out_shape=(
            struct((members * SLOT, width), BF16),
            struct((SLOT, width), F32),
            struct((SLOT, INTS), F32),
        ),
        compiler_params=params,
        cost_estimate=cost(1.5),
    )(rows, ln_gains, ln_biases, layer_biases, w_fc1, fc1_bias.reshape(1, -1), w_fc2)
    parts = lax.all_to_all(
        sent.reshape(members, SLOT, width), SPREAD, split_axis=0, concat_axis=0, tiled=True
    )
    piece = pl.pallas_call(
        cut_kernel,
        out_shape=struct((members, PAD, embed), BF16),
        compiler_params=params,
        cost_estimate=cost(0.5),
    )(rows, meta)
    pairs = neighbours(owners)
    pieces = [lax.ppermute(piece, "dp", pairs[step]) for step in STEPS]
    send = pl.pallas_call(
        pool_kernel,
        out_shape=struct((owners, SLOT, width), BF16),
        compiler_params=params,
        cost_estimate=cost(0.5),
    )(parts, first, meta, ln_gains, ln_biases, layer_biases)
    proj = pl.pallas_call(
        unpack_kernel,
        out_shape=struct((members, 4, PAD, embed), BF16),
        compiler_params=params,
        cost_estimate=cost(0.7),
    )(piece, *pieces)
    keys = lax.all_to_all(send, "dp", split_axis=0, concat_axis=0, tiled=True)
    back = pl.pallas_call(
        nearest_kernel,
        out_shape=struct((members * SLOT, embed), BF16),
        scratch_shapes=[pltpu.VMEM((owners * SLOT, embed), F32)],
        compiler_params=params,
        cost_estimate=cost(1.0),
    )(keys.reshape(owners * SLOT, width), meta, proj.reshape(width, embed))
    home = lax.all_to_all(
        back.reshape(members, SLOT, embed), SPREAD, split_axis=0, concat_axis=0, tiled=True
    )
    features, nearest = pl.pallas_call(
        home_kernel,
        out_shape=(struct((own_images, embed), BF16), struct((1, own_images), F32)),
        compiler_params=params,
        cost_estimate=cost(0.5),
    )(home)
    return (features, nearest.reshape(own_images))


def solution(mesh):
    return jax.shard_map(
        local,
        mesh=mesh,
        in_specs=(
            P(("dp", "clus"), None, "tensor"),
            P(("dp", "clus")),
            P(("dp", "clus")),
            P(("dp", "clus", "tensor")),
            P(("dp", "clus", "tensor")),
            P(),
            P(),
            P(None, None, "tensor"),
            P(),
            P("tensor", None),
            P(None, ("clus", "tensor")),
            P(("clus", "tensor")),
            P(("clus", "tensor"), None),
            P(("clus", "tensor"), None),
        ),
        out_specs=(P(("dp", "clus", "tensor"), None), P(("dp", "clus", "tensor"))),
        check_vma=False,
    )
```
